32 devices in a mesh: dp: 8 (over y, x, core), tensor: 4 (over z).
Axes of the slice: x: 2, y: 2, z: 4, core: 2. Of those that a mesh axis runs over, the one named last changes fastest.
Arguments:
- activations: bfloat16 [8, 256, 1536], P('dp', 'tensor'), may hold values from -6 to 6
- encoder: bfloat16 [8, 512, 1536], P('dp', 'tensor'), may hold values from -6 to 6
- species: int32 [8], P('dp'), may hold values from 0 to 1
- cotangent: bfloat16 [8, 512, 1536], P('dp', 'tensor'), may hold values from -6 to 6
- norm_gain: bfloat16 [2, 1536], P(None, ('dp', 'tensor')), may hold values from 0.25 to 1.75
- norm_shift: bfloat16 [2, 1536], P(None, ('dp', 'tensor')), may hold values from -1.5 to 1.5
- species_table: bfloat16 [2, 1536], P(None, ('dp', 'tensor')), may hold values from -3 to 3
- query_weight: bfloat16 [1536, 512], P('dp', 'tensor'), may hold values from -0.15625 to 0.15625
- key_weight: bfloat16 [1536, 512], P('dp', 'tensor'), may hold values from -0.15625 to 0.15625
- value_weight: bfloat16 [1536, 1536], P('dp', 'tensor'), may hold values from -0.15625 to 0.15625
- output_weight: bfloat16 [1536, 1536], P('tensor', 'dp'), may hold values from -1.25 to 1.25
- expand_weight: bfloat16 [1536, 3072], P('dp', 'tensor'), may hold values from -0.15625 to 0.15625
- contract_weight: bfloat16 [3072, 1536], P('tensor', 'dp'), may hold values from -0.109375 to 0.109375
- position_weight: bfloat16 [64, 32, 8], P('dp', None, 'tensor'), may hold values from -1 to 1
- content_bias: bfloat16 [64, 8], P('dp', 'tensor'), may hold values from -3 to 3
- position_bias: bfloat16 [64, 8], P('dp', 'tensor'), may hold values from -3 to 3
- upsample_weight: bfloat16 [1536, 1536], P(None, ('dp', 'tensor')), may hold values from -0.15625 to 0.15625
- lateral_weight: bfloat16 [1536, 1536], P(None, ('dp', 'tensor')), may hold values from -0.15625 to 0.15625
- depthwise_weight: bfloat16 [3, 1536], P(None, ('dp', 'tensor')), may hold values from -3.5 to 3.5
- section_bias: bfloat16 [1536], P(('dp', 'tensor')), may hold values from -3 to 3
- pointwise_weight: bfloat16 [1536, 1536], P(('dp', 'tensor')), may hold values from -0.15625 to 0.15625
Outputs:
- section_output: bfloat16 [8, 512, 1536], P('dp', 'tensor')
- activations_grad: float32 [8, 256, 1536], P('dp', 'tensor')
- encoder_grad: float32 [8, 512, 1536], P('dp', 'tensor')
- norm_gain_grad: float32 [2, 1536], P(None, ('dp', 'tensor'))
- norm_shift_grad: float32 [2, 1536], P(None, ('dp', 'tensor'))
- species_table_grad: float32 [2, 1536], P(None, ('dp', 'tensor'))
- query_weight_grad: float32 [1536, 512], P('dp', 'tensor')
- key_weight_grad: float32 [1536, 512], P('dp', 'tensor')
- value_weight_grad: float32 [1536, 1536], P('dp', 'tensor')
- output_weight_grad: float32 [1536, 1536], P('tensor', 'dp')
- expand_weight_grad: float32 [1536, 3072], P('dp', 'tensor')
- contract_weight_grad: float32 [3072, 1536], P('tensor', 'dp')
- position_weight_grad: float32 [64, 32, 8], P('dp', None, 'tensor')
- content_bias_grad: float32 [64, 8], P('dp', 'tensor')
- position_bias_grad: float32 [64, 8], P('dp', 'tensor')
- upsample_weight_grad: float32 [1536, 1536], P(None, ('dp', 'tensor'))
- lateral_weight_grad: float32 [1536, 1536], P(None, ('dp', 'tensor'))
- depthwise_weight_grad: float32 [3, 1536], P(None, ('dp', 'tensor'))
- section_bias_grad: float32 [1536], P(('dp', 'tensor'))
- pointwise_weight_grad: float32 [1536, 1536], P(('dp', 'tensor'))
The draws below stay inside these ranges and needn't reach their ends.
Inputs may be any that keep to these rules, and one draw needn't show every extreme that they name: Both species occur among the windows.
All inputs are finite; a program needn't handle non-finite values.
Results may differ from the reference program's by a relative error of at most 0.019.
Values may be sent and summed in bfloat16 or wider, within the bound.
No kernel may reach another device: no remote copies, remote signals or barrier semaphores. Data moves between devices by JAX's collectives and lax.ppermute only.
A program may use at most 192 MiB of HBM per device.

```python
import math
import jax
import jax.numpy as jnp
from jax import lax

D = 1536
HEADS = 8
KEYD = 64
VALD = 192
FF = 3072
BASIS = 32
SPECIES = 2
LEN = 256
QBLOCK = 256
WINDOWS = 8


def place_ends(values, stream_key, smallest, high):
    shape = values.shape
    spot = [jax.random.randint(jax.random.fold_in(stream_key, axis), (), 0, shape[axis]) for axis in range(len(shape))]
    values = values.at[tuple(spot)].set(smallest)
    longest = shape.index(max(shape))
    spot[longest] = (spot[longest] + 1) % shape[longest]
    return values.at[tuple(spot)].set(high)


def spiked(drawn, own_key, source, target, blocks, factor):
    owner, partner = [(jnp.arange(drawn.shape[axis_at]) // (drawn.shape[axis_at] // blocks)).reshape([-1 if axis == axis_at else 1 for axis in range(drawn.ndim)]) for axis_at in (source, target)]
    chosen = jax.random.permutation(own_key, blocks)[partner]
    strong = (owner == chosen) | (owner == (partner + blocks // 2) % blocks)
    return jnp.where(strong, factor * drawn, drawn)


def shard_levels(key, dims, pieces, smallest, largest):
    gain, own = 1.0, jax.random.fold_in(key, 6)
    for position, parts in pieces:
        heights = jnp.exp(jax.random.uniform(jax.random.fold_in(own, position), (parts,), jnp.float32, smallest / len(pieces), largest / len(pieces)))
        gain = gain * jnp.repeat(heights, dims[position] // parts).reshape([-1 if axis == position else 1 for axis in range(len(dims))])
    return gain


def noise(rng, extent, scale, most, cuts=(), held_as=jnp.bfloat16):
    result = scale * jax.random.normal(rng, extent, jnp.float32)
    if cuts:
        result = result * shard_levels(rng, extent, cuts, -0.22, 0.18)
    return jnp.clip(result, -most, most).astype(held_as)


def gaussian_with(key, shape, spread, reach, split, heavy, held_as=jnp.bfloat16):
    drawn = spread * jax.random.normal(key, shape, jnp.float32)
    if split:
        drawn = drawn * shard_levels(key, shape, split, -0.22, 0.18)
    return jnp.clip(spiked(drawn, jax.random.fold_in(key, 3), *heavy), -reach, reach).astype(held_as)


def setup_inputs(seed: int = 0) -> dict:
    keys = jax.random.split(jax.random.key(seed), 22)
    return {
        "activations": noise(keys[0], (WINDOWS, LEN, D), 1.0, 6.0, ((0, 8), (1, 4))),
        "encoder": noise(keys[1], (WINDOWS, 2 * LEN, D), 1.0, 6.0, ((0, 8), (1, 4))),
        "species": place_ends(jax.random.randint(keys[2], (WINDOWS,), 0, SPECIES), jax.random.fold_in(keys[2], 1), 0, SPECIES - 1).astype(jnp.int32),
        "cotangent": gaussian_with(keys[3], (WINDOWS, 2 * LEN, D), 1.0, 6.0, ((0, 8), (1, 4)), (0, 2, 8, 2.0)),
        "norm_gain": jnp.clip(1.0 + 0.15 * jax.random.normal(keys[4], (2, D), jnp.float32), 0.25, 1.75).astype(jnp.bfloat16),
        "norm_shift": noise(keys[5], (2, D), 0.3, 1.5, ((1, 32),)),
        "species_table": noise(keys[6], (SPECIES, D), 0.5, 3.0, ((1, 32),)),
        "query_weight": noise(keys[7], (D, HEADS * KEYD), D ** -0.5, 0.15625, ((0, 8), (1, 4))),
        "key_weight": noise(keys[8], (D, HEADS * KEYD), D ** -0.5, 0.15625, ((0, 8), (1, 4))),
        "value_weight": noise(keys[9], (D, HEADS * VALD), D ** -0.5, 0.15625, ((0, 8), (1, 4))),
        "output_weight": noise(keys[10], (HEADS * VALD, D), (max(HEADS * VALD * 4 // LEN, 1)) ** -0.5, 1.25, ((0, 4), (1, 8))),
        "expand_weight": noise(keys[11], (D, FF), D ** -0.5, 0.15625, ((0, 8), (1, 4))),
        "contract_weight": noise(keys[12], (FF, D), FF ** -0.5, 0.109375, ((0, 4), (1, 8))),
        "position_weight": noise(keys[13], (KEYD, BASIS, HEADS), BASIS ** -0.5, 1.0, ((0, 8), (2, 4))),
        "content_bias": noise(keys[14], (KEYD, HEADS), 0.5, 3.0, ((0, 8), (1, 4))),
        "position_bias": noise(keys[15], (KEYD, HEADS), 0.5, 3.0, ((0, 8), (1, 4))),
        "upsample_weight": noise(keys[16], (D, D), D ** -0.5, 0.15625, ((1, 32),)),
        "lateral_weight": noise(keys[17], (D, D), D ** -0.5, 0.15625, ((1, 32),)),
        "depthwise_weight": noise(keys[18], (3, D), 3 ** -0.5, 3.5, ((1, 32),)),
        "section_bias": noise(keys[19], (D,), 0.5, 3.0, ((0, 32),)),
        "pointwise_weight": noise(keys[20], (D, D), D ** -0.5, 0.15625, ((0, 32),)),
    }


highest = lax.Precision.HIGHEST

@jax.custom_vjp
def low(v):
    return lax.optimization_barrier(v.astype(jnp.bfloat16)).astype(jnp.float32)

@jax.custom_vjp
def low_back(v):
    return v

def low_keep(v):
    return (low(v), None)

def low_pass(kept, grad):
    return (grad,)

def back_keep(v):
    return (v, None)

def back_low(kept, grad):
    return (low(grad),)
low.defvjp(low_keep, low_pass)
low_back.defvjp(back_keep, back_low)

def dot_high(left_side, right_side):
    return jnp.dot(left_side, right_side, precision=highest)

def layer_norm(values, gain_vec, shift_vec):
    centred = values - lax.optimization_barrier(jnp.mean(values, axis=-1, keepdims=True))
    variance = lax.optimization_barrier(jnp.mean(centred * centred, axis=-1, keepdims=True))
    return centred * lax.rsqrt(variance + 1e-05) * gain_vec + shift_vec

def basis_table(length, features):
    distance = jnp.arange(2 * length - 1).astype(jnp.float32) - (length - 1)
    halves = features // 2
    fraction = jnp.arange(halves).astype(jnp.float32) / (halves - 1)
    lifetimes = 3.0 * jnp.power(length / 3.0, fraction)
    decays = jnp.exp(-0.6931471805599453 * jnp.abs(distance)[:, None] / lifetimes[None, :])
    return jnp.concatenate([decays, jnp.sign(distance)[:, None] * decays], axis=1)

def skew_band(banded, length):
    head_count, row_count, band_width = banded.shape
    flipped = banded[:, :, ::-1]
    flat = flipped.reshape(head_count, row_count * band_width)
    flat = flat[:, row_count - 1:row_count - 1 + row_count * (band_width - 1)]
    return flat.reshape(head_count, row_count, band_width - 1)[:, :, :length]

def attention(query_content, query_position, key_rows, value_rows, rel_keys):
    score_scale = 1.0 / math.sqrt(KEYD)
    content_heads = query_content.reshape(LEN, HEADS, KEYD)
    position_heads = query_position.reshape(LEN, HEADS, KEYD)
    key_heads = key_rows.reshape(LEN, HEADS, KEYD)
    value_heads = value_rows.reshape(LEN, HEADS, VALD)
    rel_heads = rel_keys.reshape(2 * LEN - 1, HEADS, KEYD)

    def attend_block(offset):
        content_block = lax.dynamic_slice_in_dim(content_heads, offset, QBLOCK, 0)
        position_block = lax.dynamic_slice_in_dim(position_heads, offset, QBLOCK, 0)
        band_keys = lax.dynamic_slice_in_dim(rel_heads, offset, QBLOCK + LEN - 1, 0)
        content = jnp.einsum('bhk,jhk->hbj', content_block, key_heads, precision=highest)
        banded = jnp.einsum('bhk,whk->hbw', position_block, band_keys, precision=highest)
        scores = low_back((content + skew_band(banded, LEN)) * score_scale)
        attn_probs = low(jax.nn.softmax(scores, axis=-1))
        mixed_block = jnp.einsum('hbj,jhv->bhv', attn_probs, value_heads, precision=highest)
        return mixed_block.reshape(QBLOCK, HEADS * VALD)
    offsets = jnp.arange(LEN // QBLOCK, dtype=jnp.int32) * QBLOCK
    return lax.map(jax.checkpoint(attend_block), offsets).reshape(LEN, HEADS * VALD)

def window_forward(params, row_values, encoder_rows, species_mask, basis):
    gain_rows, shift_rows, table_rows, w_query, w_key, w_value, w_output, w_expand, w_contract, w_position, bias_content, bias_position, w_upsample, w_lateral, w_depth, bias_section, w_point = params
    resid_in = row_values + dot_high(species_mask, table_rows)[None, :]
    normed_one = low(layer_norm(resid_in, gain_rows[0], shift_rows[0]))
    query = low_back(dot_high(normed_one, w_query))
    key_rows = low(low_back(dot_high(normed_one, w_key)))
    value_rows = low(low_back(dot_high(normed_one, w_value)))
    query_content = low(query + bias_content.T.reshape(-1))
    query_position = low(query + bias_position.T.reshape(-1))
    rel_weight = jnp.transpose(w_position, (1, 2, 0)).reshape(BASIS, HEADS * KEYD)
    rel_keys = low(low_back(dot_high(basis, rel_weight)))
    mixed_rows = low(low_back(attention(query_content, query_position, key_rows, value_rows, rel_keys)))
    resid_one = resid_in + low_back(dot_high(mixed_rows, w_output))
    normed_two = low(layer_norm(resid_one, gain_rows[1], shift_rows[1]))
    hidden = low(jax.nn.gelu(low_back(dot_high(normed_two, w_expand)), approximate=False))
    resid_two = resid_one + low_back(dot_high(hidden, w_contract))
    coarse_rows = low_back(dot_high(low(resid_two), w_upsample))
    section_mix = low(low_back(jnp.repeat(coarse_rows, 2, axis=0) + dot_high(encoder_rows, w_lateral) + bias_section))
    padded = jnp.pad(section_mix, ((1, 1), (0, 0)))
    deep_rows = low(low_back(w_depth[0] * padded[:-2] + w_depth[1] * padded[1:-1] + w_depth[2] * padded[2:]))
    return dot_high(deep_rows, w_point)

def reference(activations, encoder, species, cotangent, norm_gain, norm_shift, species_table, query_weight, key_weight, value_weight, output_weight, expand_weight, contract_weight, position_weight, content_bias, position_bias, upsample_weight, lateral_weight, depthwise_weight, section_bias, pointwise_weight):
    params = tuple((item.astype(jnp.float32) for item in (norm_gain, norm_shift, species_table, query_weight, key_weight, value_weight, output_weight, expand_weight, contract_weight, position_weight, content_bias, position_bias, upsample_weight, lateral_weight, depthwise_weight, section_bias, pointwise_weight)))
    basis = low(basis_table(LEN, BASIS))

    def window_step(grad_sums, inputs):
        window_rows, window_encoder, window_species, window_cotangent = inputs
        species_mask = (jnp.arange(SPECIES, dtype=jnp.int32) == window_species).astype(jnp.float32)

        def forward(param_set, row_values, encoder_rows):
            return window_forward(param_set, row_values, encoder_rows, species_mask, basis)
        section_out, pullback = jax.vjp(forward, params, window_rows.astype(jnp.float32), window_encoder.astype(jnp.float32))
        grad_params, grad_rows, grad_encoder = pullback(window_cotangent.astype(jnp.float32))
        grad_sums = jax.tree.map(jnp.add, grad_sums, grad_params)
        return (grad_sums, (section_out.astype(jnp.bfloat16), grad_rows, grad_encoder))
    zero_grads = jax.tree.map(jnp.zeros_like, params)
    grad_sums, (section_outs, rows_grads, encoder_grads) = lax.scan(window_step, zero_grads, (activations, encoder, species, cotangent))
    gain_grad, shift_grad, table_grad, query_grad, key_grad, value_grad, output_grad, expand_grad, contract_grad, position_grad, content_grad, position_bias_grad, upsample_grad, lateral_grad, depthwise_grad, section_bias_grad, pointwise_grad = grad_sums
    return (section_outs, rows_grads, encoder_grads, gain_grad, shift_grad, table_grad, query_grad, key_grad, value_grad, output_grad, expand_grad, contract_grad, position_grad, content_grad, position_bias_grad, upsample_grad, lateral_grad, depthwise_grad, section_bias_grad, pointwise_grad)
```

```python
import math

import jax
import jax.numpy as jnp
from jax import lax
from jax.sharding import PartitionSpec as P

KEYD = 64
VALD = 192
BASIS = 32
SPECIES = 2
SCALE = 1.0 / math.sqrt(KEYD)
LOW = jnp.bfloat16


def dot_plain(left_side, right_side):
    return jnp.dot(left_side, right_side, preferred_element_type=jnp.float32)


def dot_transposed(left_side, right_side):
    return lax.dot_general(
        left_side, right_side, (((1,), (1,)), ((), ())), preferred_element_type=jnp.float32
    )


def dot_leading(left_side, right_side):
    return lax.dot_general(
        left_side, right_side, (((0,), (0,)), ((), ())), preferred_element_type=jnp.float32
    )


def exact_gelu(values):
    return jax.nn.gelu(values, approximate=False)


def normalize(values):
    centred = values - jnp.mean(values, axis=-1, keepdims=True)
    variance = jnp.mean(centred * centred, axis=-1, keepdims=True)
    scale = lax.rsqrt(variance + 1e-05)
    return centred * scale, scale


def normalize_back(unit, scale, grad_unit):
    return scale * (
        grad_unit
        - jnp.mean(grad_unit, axis=-1, keepdims=True)
        - unit * jnp.mean(grad_unit * unit, axis=-1, keepdims=True)
    )


def basis_table(length, features):
    distance = jnp.arange(2 * length - 1).astype(jnp.float32) - (length - 1)
    halves = features // 2
    fraction = jnp.arange(halves).astype(jnp.float32) / (halves - 1)
    lifetimes = 3.0 * jnp.power(length / 3.0, fraction)
    decays = jnp.exp(-0.6931471805599453 * jnp.abs(distance)[:, None] / lifetimes[None, :])
    return jnp.concatenate([decays, jnp.sign(distance)[:, None] * decays], axis=1)


def skew_band(banded, length):
    head_count, row_count, band_width = banded.shape
    flipped = banded[:, :, ::-1]
    flat = flipped.reshape(head_count, row_count * band_width)
    flat = flat[:, row_count - 1 : row_count - 1 + row_count * (band_width - 1)]
    return flat.reshape(head_count, row_count, band_width - 1)[:, :, :length]


def unskew_band(grid, band_width):
    head_count, row_count, length = grid.shape
    padded = jnp.pad(grid, ((0, 0), (0, 0), (0, band_width - 1 - length)))
    flat = jnp.pad(
        padded.reshape(head_count, row_count * (band_width - 1)), ((0, 0), (row_count - 1, 1))
    )
    return flat.reshape(head_count, row_count, band_width)[:, :, ::-1]


def from_ahead(rows, step):
    count = lax.axis_size("tensor")
    return lax.ppermute(rows, "tensor", [((i + step) % count, i) for i in range(count)])


def spread_rows(rows):
    count = lax.axis_size("tensor")
    return jnp.concatenate([rows] + [from_ahead(rows, k) for k in range(1, count)], axis=0)


def collect_rows(partial_rows):
    count = lax.axis_size("tensor")
    low = partial_rows.astype(LOW).reshape(count, -1, partial_rows.shape[1])
    total = partial_rows.reshape(low.shape)[0]
    for k in range(1, count):
        total = total + from_ahead(low[k], count - k).astype(jnp.float32)
    return total


def to_true(rows):
    return jnp.roll(rows, lax.axis_index("tensor") * (rows.shape[0] // lax.axis_size("tensor")), 0)


def to_own(rows):
    return jnp.roll(rows, -lax.axis_index("tensor") * (rows.shape[0] // lax.axis_size("tensor")), 0)


def gather_dp(shard, axis=0):
    return lax.all_gather(shard, "dp", axis=axis, tiled=True)


def scatter_dp(whole):
    return lax.psum_scatter(whole, "dp", scatter_dimension=0, tiled=True)


def scatter_tensor(whole):
    return lax.psum_scatter(whole, "tensor", scatter_dimension=0, tiled=True)


def halo(cells):
    count = lax.axis_size("tensor")
    ends = count - 1
    before = lax.ppermute(cells[:, -1:], "tensor", [(i, i + 1) for i in range(ends)])
    after = lax.ppermute(cells[:, :1], "tensor", [(i + 1, i) for i in range(ends)])
    return jnp.concatenate([before, cells, after], axis=1)


def body(
    activations,
    encoder,
    species,
    cotangent,
    norm_gain,
    norm_shift,
    species_table,
    query_weight,
    key_weight,
    value_weight,
    output_weight,
    expand_weight,
    contract_weight,
    position_weight,
    content_bias,
    position_bias,
    upsample_weight,
    lateral_weight,
    depthwise_weight,
    section_bias,
    pointwise_weight,
):
    windows = lax.axis_size("dp")
    count = lax.axis_size("tensor")
    own = activations.shape[1]
    length = own * count
    width = activations.shape[2]
    local_heads = query_weight.shape[1] // KEYD
    keys = local_heads * KEYD
    values = local_heads * VALD

    raw_all = spread_rows(activations[0])
    attn_shard = jnp.concatenate([query_weight, key_weight, value_weight, output_weight.T], axis=1)
    w_attn = gather_dp(attn_shard)
    w_query = w_attn[:, :keys]
    w_key = w_attn[:, keys : 2 * keys]
    w_value = w_attn[:, 2 * keys : 2 * keys + values]
    w_output_t = w_attn[:, 2 * keys + values :]

    small = jnp.concatenate(
        [norm_gain, norm_shift, species_table, depthwise_weight, section_bias[None]], axis=0
    )
    small_group = jnp.swapaxes(lax.all_gather(small, "tensor", axis=0), 0, 1).reshape(10, -1)
    norm_group = small_group[:6]
    heads_group = jnp.concatenate(
        [position_weight.reshape(-1), content_bias.reshape(-1), position_bias.reshape(-1)]
    )
    packed = gather_dp(jnp.concatenate([norm_group.reshape(-1), heads_group])[None])
    channels = norm_group.shape[1]
    norm_all = jnp.swapaxes(packed[:, : 6 * channels].reshape(windows, 6, channels), 0, 1)
    norm_all = norm_all.reshape(6, width).astype(jnp.float32)
    heads_all = packed[:, 6 * channels :]
    n_position = position_weight.size
    n_bias = content_bias.size
    w_position = heads_all[:, :n_position].reshape(KEYD, BASIS, local_heads)
    bias_content = heads_all[:, n_position : n_position + n_bias].reshape(KEYD, local_heads)
    bias_position = heads_all[:, n_position + n_bias :].reshape(KEYD, local_heads)
    gain_vals, shift_vals, table_rows = norm_all[:2], norm_all[2:4], norm_all[4:]
    depth_taps = small_group[6:9].astype(jnp.float32)
    bias_section = small_group[9].astype(jnp.float32)

    w_point = lax.all_gather(pointwise_weight, "tensor", axis=0, tiled=True)
    w_up = lax.all_gather(upsample_weight.T, "tensor", axis=0, tiled=True)
    w_lat = lax.all_gather(lateral_weight.T, "tensor", axis=0, tiled=True)
    cot_all = gather_dp(cotangent[0])
    ffn_shard = jnp.concatenate([expand_weight, contract_weight.T], axis=1)
    w_ffn = gather_dp(ffn_shard)
    hidden_count = expand_weight.shape[1]
    w_expand = w_ffn[:, :hidden_count]
    w_contract_t = w_ffn[:, hidden_count:]
    enc_all = gather_dp(encoder[0])

    fine = 2 * own
    grad_deep = dot_transposed(cot_all, w_point).astype(LOW)
    grad_wide = halo(grad_deep.reshape(windows, fine, channels)).astype(jnp.float32)
    grad_mix = (
        depth_taps[0] * grad_wide[:, 2:]
        + depth_taps[1] * grad_wide[:, 1:-1]
        + depth_taps[2] * grad_wide[:, :-2]
    ).astype(LOW)
    grad_coarse = jnp.sum(
        grad_mix.astype(jnp.float32).reshape(windows * own, 2, channels), axis=1
    ).astype(LOW)
    grad_resid_two = scatter_dp(dot_plain(grad_coarse, w_up).astype(LOW))
    grad_ffn_all = spread_rows(grad_resid_two)
    grad_resid_two = grad_resid_two.astype(jnp.float32)

    species_mask = (jnp.arange(SPECIES, dtype=jnp.int32) == species[0]).astype(jnp.float32)
    species_row = jnp.sum(species_mask[:, None] * table_rows, axis=0)
    resid_in_all = raw_all.astype(jnp.float32) + species_row[None, :]
    unit_one_all, scale_one_all = normalize(resid_in_all)
    normed_all = (unit_one_all * gain_vals[0] + shift_vals[0]).astype(LOW)
    resid_in = resid_in_all[:own]
    content_flat = bias_content.astype(jnp.float32).T.reshape(-1)
    position_flat = bias_position.astype(jnp.float32).T.reshape(-1)
    query_full = dot_plain(normed_all, w_query)
    query_content = to_true((query_full + content_flat).astype(LOW))
    query_position = to_true((query_full + position_flat).astype(LOW))
    key_low = to_true(dot_plain(normed_all, w_key).astype(LOW))
    value_low = to_true(dot_plain(normed_all, w_value).astype(LOW))
    basis_low = basis_table(length, BASIS).astype(LOW)
    rel_weight = jnp.transpose(w_position, (1, 2, 0)).reshape(BASIS, -1)
    rel_low = dot_plain(basis_low, rel_weight).astype(LOW)
    content_heads = query_content.reshape(length, local_heads, KEYD)
    position_heads = query_position.reshape(length, local_heads, KEYD)
    key_heads = key_low.reshape(length, local_heads, KEYD)
    value_heads = value_low.reshape(length, local_heads, VALD)
    rel_heads = rel_low.reshape(2 * length - 1, local_heads, KEYD)
    content = jnp.einsum(
        "bhk,jhk->hbj", content_heads, key_heads, preferred_element_type=jnp.float32
    )
    banded = jnp.einsum(
        "bhk,whk->hbw", position_heads, rel_heads, preferred_element_type=jnp.float32
    )
    scores = (content + skew_band(banded, length)) * SCALE
    attn_soft = jax.nn.softmax(scores, axis=-1)
    attn_low = attn_soft.astype(LOW)
    mixed = jnp.einsum("hbj,jhv->bhv", attn_low, value_heads, preferred_element_type=jnp.float32)
    mixed_rows = to_own(mixed.reshape(length, -1).astype(LOW))
    resid_one = resid_in + collect_rows(dot_transposed(mixed_rows, w_output_t))

    unit_two, scale_two = normalize(resid_one)
    normed_two = (unit_two * gain_vals[1] + shift_vals[1]).astype(LOW)
    normed_two_all = spread_rows(normed_two)
    hidden_pre = dot_plain(normed_two_all, w_expand)
    hidden_low = exact_gelu(hidden_pre).astype(LOW)
    grad_hidden = dot_plain(grad_ffn_all, w_contract_t)
    grad_hidden_pre = jax.vjp(exact_gelu, hidden_pre)[1](grad_hidden)[0].astype(LOW)
    grad_normed_two = collect_rows(dot_transposed(grad_hidden_pre, w_expand))
    grad_from_second = normalize_back(unit_two, scale_two, grad_normed_two * gain_vals[1])
    grad_resid_one = grad_resid_two + grad_from_second
    grad_gain_two = jnp.sum(grad_normed_two * unit_two, axis=0)
    grad_shift_two = jnp.sum(grad_normed_two, axis=0)
    grad_attn_own = spread_rows(grad_resid_one.astype(LOW))

    resid_two = resid_one + collect_rows(dot_transposed(hidden_low, w_contract_t))
    section_all = gather_dp(resid_two.astype(LOW))
    coarse = dot_transposed(section_all, w_up).reshape(windows, own, channels)
    section_mix = (
        jnp.repeat(coarse, 2, axis=1)
        + dot_transposed(enc_all, w_lat).reshape(windows, fine, channels)
        + bias_section
    ).astype(LOW)
    mix_wide = halo(section_mix).astype(jnp.float32)
    deep_rows = (
        depth_taps[0] * mix_wide[:, :-2]
        + depth_taps[1] * mix_wide[:, 1:-1]
        + depth_taps[2] * mix_wide[:, 2:]
    ).astype(LOW)
    deep_rows = deep_rows.reshape(windows * fine, channels)
    section_out = scatter_dp(dot_plain(deep_rows, w_point).astype(LOW))
    grad_mix_rows = grad_mix.reshape(windows * fine, channels)
    encoder_grad = scatter_dp(dot_plain(grad_mix_rows, w_lat).astype(LOW)).astype(jnp.float32)
    grad_centre = grad_wide[:, 1:-1]
    grad_section_small = jnp.stack(
        [jnp.sum(mix_wide[:, s : s + fine] * grad_centre, axis=(0, 1)) for s in range(3)]
        + [jnp.sum(grad_mix.astype(jnp.float32), axis=(0, 1))],
        axis=1,
    )
    upsample_cols = scatter_tensor(dot_leading(grad_coarse, section_all).astype(LOW))
    lateral_cols = scatter_tensor(dot_leading(grad_mix_rows, enc_all).astype(LOW))
    point_out = scatter_tensor(dot_leading(deep_rows, cot_all).astype(LOW))

    grad_contract_cols = dot_leading(grad_ffn_all, hidden_low)
    grad_expand = dot_leading(normed_two_all, grad_hidden_pre)
    ffn_out = scatter_dp(
        jnp.concatenate([grad_expand.astype(LOW), grad_contract_cols.astype(LOW)], axis=1)
    ).astype(jnp.float32)

    grad_output_cols = dot_leading(grad_attn_own, mixed_rows)
    grad_mixed = to_true(dot_plain(grad_attn_own, w_output_t).astype(LOW))
    grad_block = grad_mixed.reshape(length, local_heads, VALD)
    grad_probs = jnp.einsum(
        "bhv,jhv->hbj", grad_block, value_heads, preferred_element_type=jnp.float32
    )
    centre = jnp.sum(attn_soft * grad_probs, axis=-1, keepdims=True)
    grad_scores = (attn_soft * (grad_probs - centre)).astype(LOW)
    value_sum = jnp.einsum("hbj,bhv->jhv", attn_low, grad_block, preferred_element_type=jnp.float32)
    key_sum = (
        jnp.einsum("hbj,bhk->jhk", grad_scores, content_heads, preferred_element_type=jnp.float32)
        * SCALE
    )
    grad_content = (
        jnp.einsum("hbj,jhk->bhk", grad_scores, key_heads, preferred_element_type=jnp.float32)
        * SCALE
    ).reshape(length, -1)
    grad_band = unskew_band(grad_scores, rel_heads.shape[0])
    grad_position = (
        jnp.einsum("hbw,whk->bhk", grad_band, rel_heads, preferred_element_type=jnp.float32)
        * SCALE
    ).reshape(length, -1)
    rel_sum = (
        jnp.einsum("hbw,bhk->whk", grad_band, position_heads, preferred_element_type=jnp.float32)
        * SCALE
    )
    grad_query = to_own((grad_content + grad_position).astype(LOW))
    grad_content_bias = jnp.sum(grad_content, axis=0).reshape(local_heads, KEYD).T
    grad_position_bias = jnp.sum(grad_position, axis=0).reshape(local_heads, KEYD).T
    grad_keys = to_own(key_sum.reshape(length, -1).astype(LOW))
    grad_values = to_own(value_sum.reshape(length, -1).astype(LOW))
    grad_rel = rel_sum.reshape(2 * length - 1, -1).astype(LOW)
    grad_position_weight = jnp.transpose(
        dot_leading(basis_low, grad_rel).reshape(BASIS, local_heads, KEYD), (2, 0, 1)
    )
    grad_qkv = jnp.concatenate([grad_query, grad_keys, grad_values], axis=1)
    grad_normed_part = dot_transposed(grad_qkv, w_attn[:, : 2 * keys + values])
    grad_normed_one = collect_rows(grad_normed_part)
    attn_out = scatter_dp(
        jnp.concatenate(
            [dot_leading(normed_all, grad_qkv).astype(LOW), grad_output_cols.astype(LOW)], axis=1
        )
    ).astype(jnp.float32)
    grad_resid_in = grad_resid_one + normalize_back(
        unit_one_all[:own], scale_one_all[:own], grad_normed_one * gain_vals[0]
    )

    table_part = jnp.sum(grad_resid_one, axis=0) + jnp.sum(
        normalize_back(unit_one_all, scale_one_all, grad_normed_part * gain_vals[0]), axis=0
    )
    norm_cols = jnp.concatenate(
        [
            jnp.sum(grad_normed_part * unit_one_all, axis=0)[None],
            grad_gain_two[None],
            jnp.sum(grad_normed_part, axis=0)[None],
            grad_shift_two[None],
            table_part[None] * species_mask[:, None],
        ],
        axis=0,
    )
    norm_cols = jnp.swapaxes(norm_cols.reshape(6, windows, channels), 0, 1)
    heads_cols = jnp.concatenate(
        [
            grad_position_weight.reshape(windows, -1),
            grad_content_bias.reshape(windows, -1),
            grad_position_bias.reshape(windows, -1),
        ],
        axis=1,
    )
    small_out = scatter_dp(jnp.concatenate([norm_cols.reshape(windows, -1), heads_cols], axis=1))[0]
    n_norm = 6 * channels
    group_cols = jnp.concatenate([small_out[:n_norm].reshape(6, channels), grad_section_small.T])
    group_cols = jnp.swapaxes(group_cols.reshape(10, count, -1), 0, 1)
    norm_out = scatter_tensor(group_cols)[0]
    heads_out = small_out[n_norm:]
    return (
        section_out[None],
        grad_resid_in[None],
        encoder_grad[None],
        norm_out[0:2],
        norm_out[2:4],
        norm_out[4:6],
        attn_out[:, :keys],
        attn_out[:, keys : 2 * keys],
        attn_out[:, 2 * keys : 2 * keys + values],
        attn_out[:, 2 * keys + values :].T,
        ffn_out[:, :hidden_count],
        ffn_out[:, hidden_count:].T,
        heads_out[:n_position].reshape(position_weight.shape),
        heads_out[n_position : n_position + n_bias].reshape(content_bias.shape),
        heads_out[n_position + n_bias :].reshape(position_bias.shape),
        upsample_cols.astype(jnp.float32).T,
        lateral_cols.astype(jnp.float32).T,
        norm_out[6:9],
        norm_out[9],
        point_out.astype(jnp.float32),
    )


def solution(mesh):
    rows = P("dp", "tensor", None)
    narrow = P(None, ("dp", "tensor"))
    split = P("dp", "tensor")
    turned = P("tensor", "dp")
    vector = P(("dp", "tensor"))
    tall = P(("dp", "tensor"), None)
    position = P("dp", None, "tensor")
    weights = (split, split, split, turned, split, turned, position, split, split)
    return jax.shard_map(
        body,
        mesh=mesh,
        in_specs=(rows, rows, P("dp"), rows, narrow, narrow, narrow)
        + weights
        + (narrow, narrow, narrow, vector, tall),
        out_specs=(rows, rows, rows, narrow, narrow, narrow)
        + weights
        + (narrow, narrow, narrow, vector, tall),
        check_vma=False,
    )
```

```python
import math

import jax
import jax.numpy as jnp
from jax import lax
from jax.experimental import pallas as pl
from jax.experimental.pallas import tpu as pltpu
from jax.sharding import PartitionSpec as P

KEYD = 64
VALD = 192
BASIS = 32
SPECIES = 2
SCALE = 1.0 / math.sqrt(KEYD)
LOW = jnp.bfloat16


def dot_plain(left_side, right_side):
    return jnp.dot(left_side, right_side, preferred_element_type=jnp.float32)


def dot_transposed(left_side, right_side):
    return lax.dot_general(
        left_side, right_side, (((1,), (1,)), ((), ())), preferred_element_type=jnp.float32
    )


def dot_leading(left_side, right_side):
    return lax.dot_general(
        left_side, right_side, (((0,), (0,)), ((), ())), preferred_element_type=jnp.float32
    )


def exact_gelu(values):
    return jax.nn.gelu(values, approximate=False)


def normalize(values):
    centred = values - jnp.mean(values, axis=-1, keepdims=True)
    variance = jnp.mean(centred * centred, axis=-1, keepdims=True)
    scale = lax.rsqrt(variance + 1e-05)
    return centred * scale, scale


def normalize_back(unit, scale, grad_unit):
    return scale * (
        grad_unit
        - jnp.mean(grad_unit, axis=-1, keepdims=True)
        - unit * jnp.mean(grad_unit * unit, axis=-1, keepdims=True)
    )


def basis_table(length, features):
    distance = jnp.arange(2 * length - 1).astype(jnp.float32) - (length - 1)
    halves = features // 2
    fraction = jnp.arange(halves).astype(jnp.float32) / (halves - 1)
    lifetimes = 3.0 * jnp.power(length / 3.0, fraction)
    decays = jnp.exp(-0.6931471805599453 * jnp.abs(distance)[:, None] / lifetimes[None, :])
    return jnp.concatenate([decays, jnp.sign(distance)[:, None] * decays], axis=1)


def dot_rows(left_side, right_side):
    return jnp.dot(left_side, right_side, preferred_element_type=jnp.float32)


def run_kernel(kernel, ins, outs, scalars=None, scratch=(), flops=0, name=None):
    whole = pl.BlockSpec(memory_space=pltpu.VMEM)
    specs = [whole] * len(ins)
    args = list(ins)
    if scalars is not None:
        specs = [pl.BlockSpec(memory_space=pltpu.SMEM)] + specs
        args = [scalars] + args
    shapes = [jax.ShapeDtypeStruct(shape, dtype) for shape, dtype in outs]
    moved = sum(x.size * x.dtype.itemsize for x in list(ins) + shapes)
    return pl.pallas_call(
        kernel,
        in_specs=specs,
        out_specs=[whole] * len(shapes),
        out_shape=shapes,
        scratch_shapes=scratch,
        compiler_params=pltpu.CompilerParams(vmem_limit_bytes=50 * 1024 * 1024),
        cost_estimate=pl.CostEstimate(flops=flops, bytes_accessed=moved, transcendentals=0),
        name=name,
    )(*args)


def lanes_of(head, width, shape):
    lane = lax.broadcasted_iota(jnp.int32, shape, len(shape) - 1)
    return (lane >= head * width) & (lane < (head + 1) * width)


def chunk_of(where_ref, step, count):
    return lax.rem(where_ref[1] + step, count)


def attention_forward(where, raw, row_params, rel_turned, blocks, local_heads):
    count, (own, width) = len(raw), raw[0].shape
    length = count * own
    rows, columns = blocks[0].shape
    keys, values = local_heads * KEYD, local_heads * VALD
    n_blocks = len(blocks)

    def kernel(where_ref, *refs):
        raw_refs, refs = refs[:count], refs[count:]
        species_ref, gain_ref, shift_ref, content_ref, position_ref, rel_ref = refs[:6]
        block_refs, refs = refs[6 : 6 + n_blocks], refs[6 + n_blocks :]
        own_ref, refs = refs[0], refs[1:]
        part_refs, refs = refs[: count - 1], refs[count - 1 :]
        (weight_ref, normed_ref, unit_ref, scale_ref, probs_ref, content_out, position_out) = refs[:7]
        key_out, value_out, mixed_out, total_ref = refs[7:]
        for m in range(n_blocks):
            spot = (where_ref[0] ^ m) * rows if n_blocks > 1 else 0
            weight_ref[pl.ds(pl.multiple_of(spot, rows), rows), :] = block_refs[m][...]
        for k in range(count):
            resid = raw_refs[k][...].astype(jnp.float32) + species_ref[...]
            unit, scale = normalize(resid)
            spot = pl.ds(pl.multiple_of(chunk_of(where_ref, k, count) * own, own), own)
            unit_ref[spot, :] = unit
            scale_ref[spot, :] = jnp.broadcast_to(scale, (own, 128))
            normed_ref[spot, :] = (unit * gain_ref[...] + shift_ref[...]).astype(LOW)
        normed = normed_ref[...]
        query = dot_rows(normed, weight_ref[:, :keys])
        content = (query + content_ref[...]).astype(LOW)
        position = (query + position_ref[...]).astype(LOW)
        key_low = dot_rows(normed, weight_ref[:, keys : 2 * keys]).astype(LOW)
        value_low = dot_rows(normed, weight_ref[:, 2 * keys : 2 * keys + values]).astype(LOW)
        content_out[...] = content
        position_out[...] = position
        key_out[...] = key_low
        value_out[...] = value_low
        mixed = jnp.zeros((length, values), jnp.float32)
        for h in range(local_heads):
            mine = lanes_of(h, KEYD, (length, keys))
            zero = jnp.zeros((), LOW)
            banded = dot_transposed(jnp.where(mine, position, zero), rel_ref[...])
            skewed = pltpu.roll(banded, length + 1, 1, stride=1, stride_axis=0)[:, :length]
            scores = (dot_transposed(jnp.where(mine, content, zero), key_low) + skewed) * SCALE
            exponent = jnp.exp(scores - jnp.max(scores, axis=-1, keepdims=True))
            probs = exponent / jnp.sum(exponent, axis=-1, keepdims=True)
            probs_ref[h] = probs
            mixed = jnp.where(
                lanes_of(h, VALD, (length, values)), dot_rows(probs.astype(LOW), value_low), mixed
            )
        mixed_out[...] = mixed.astype(LOW)
        total_ref[...] = dot_transposed(mixed.astype(LOW), weight_ref[:, 2 * keys + values :])
        for k in range(count):
            spot = pl.ds(pl.multiple_of(chunk_of(where_ref, k, count) * own, own), own)
            if k == 0:
                own_ref[...] = total_ref[spot, :]
            else:
                part_refs[k - 1][...] = total_ref[spot, :].astype(LOW)

    outs = (
        [((own, width), jnp.float32)]
        + [((own, width), LOW)] * (count - 1)
        + [
            ((width, columns), LOW),
            ((length, width), LOW),
            ((length, width), jnp.float32),
            ((length, 128), jnp.float32),
            ((local_heads, length, length), jnp.float32),
            ((length, keys), LOW),
            ((length, keys), LOW),
            ((length, keys), LOW),
            ((length, values), LOW),
            ((length, values), LOW),
        ]
    )
    found = run_kernel(
        kernel,
        list(raw) + list(row_params) + [rel_turned] + list(blocks),
        outs,
        scalars=where,
        scratch=[pltpu.VMEM((length, width), jnp.float32)],
        flops=2 * length * width * columns,
        name="attention_forward",
    )
    return found[:count], found[count:]


def attention_backward(where, grads, saved, rel_turned, basis_turned, local_heads):
    count, (own, width) = len(grads), grads[0].shape
    length = count * own
    weight, _, _, _, probs_all, content_all, position_all, key_all, value_all, _ = saved
    keys, values = local_heads * KEYD, local_heads * VALD
    narrow = 2 * keys + values

    def kernel(where_ref, *refs):
        grad_refs, refs = refs[:count], refs[count:]
        weight_ref, probs_ref, content_ref, position_ref, key_ref, value_ref = refs[:6]
        rel_ref, basis_ref = refs[6:8]
        own_ref, refs = refs[8], refs[9:]
        part_refs, refs = refs[: count - 1], refs[count - 1 :]
        attn_ref, heads_ref, total_ref, bias_ref, weight_out = refs
        for k in range(count):
            spot = pl.ds(pl.multiple_of(chunk_of(where_ref, k, count) * own, own), own)
            attn_ref[spot, :] = grad_refs[k][...]
        grad_mixed = dot_rows(attn_ref[...], weight_ref[:, narrow:]).astype(LOW)
        content, position = content_ref[...], position_ref[...]
        key_low, value_low = key_ref[...], value_ref[...]
        grad_content = jnp.zeros((length, keys), jnp.float32)
        grad_position = jnp.zeros((length, keys), jnp.float32)
        grad_key = jnp.zeros((length, keys), jnp.float32)
        grad_rel = jnp.zeros((2 * length, keys), jnp.float32)
        grad_value = jnp.zeros((length, values), jnp.float32)
        back = lax.broadcasted_iota(jnp.int32, (length, 2 * length), 0)
        for h in range(local_heads):
            mine = lanes_of(h, KEYD, (length, keys))
            ours = lanes_of(h, VALD, (length, values))
            probs = probs_ref[h]
            grad_probs = dot_transposed(
                jnp.where(ours, grad_mixed, jnp.zeros((), LOW)), value_low
            )
            centre = jnp.sum(probs * grad_probs, axis=-1, keepdims=True)
            grad_scores = (probs * (grad_probs - centre)).astype(LOW)
            grad_value = jnp.where(ours, dot_leading(probs.astype(LOW), grad_mixed), grad_value)
            grad_key = jnp.where(mine, dot_leading(grad_scores, content), grad_key)
            grad_content = jnp.where(mine, dot_rows(grad_scores, key_low), grad_content)
            band = jnp.concatenate(
                [grad_scores.astype(jnp.float32), jnp.zeros((length, length), jnp.float32)], axis=1
            )
            bit = 1
            while bit < length:
                turn = (length - 1 - back) & bit
                band = jnp.where(turn > 0, pltpu.roll(band, bit, 1), band)
                bit *= 2
            band = band.astype(LOW)
            grad_position = jnp.where(mine, dot_rows(band, rel_ref[...]), grad_position)
            grad_rel = jnp.where(
                lanes_of(h, KEYD, (2 * length, keys)), dot_leading(band, position), grad_rel
            )
        grad_content = grad_content * SCALE
        grad_position = grad_position * SCALE
        bias_ref[0:1, :] = jnp.sum(grad_content, axis=0, keepdims=True)
        bias_ref[1:2, :] = jnp.sum(grad_position, axis=0, keepdims=True)
        heads_ref[:, :keys] = (grad_content + grad_position).astype(LOW)
        heads_ref[:, keys : 2 * keys] = (grad_key * SCALE).astype(LOW)
        heads_ref[:, 2 * keys :] = grad_value.astype(LOW)
        weight_out[...] = dot_leading(basis_ref[...], (grad_rel * SCALE).astype(LOW))
        total_ref[...] = dot_transposed(heads_ref[...], weight_ref[:, :narrow])
        for k in range(count):
            spot = pl.ds(pl.multiple_of(chunk_of(where_ref, k, count) * own, own), own)
            if k == 0:
                own_ref[...] = total_ref[spot, :]
            else:
                part_refs[k - 1][...] = total_ref[spot, :].astype(LOW)

    outs = (
        [((own, width), jnp.float32)]
        + [((own, width), LOW)] * (count - 1)
        + [
            ((length, width), LOW),
            ((length, narrow), LOW),
            ((length, width), jnp.float32),
            ((2, keys), jnp.float32),
            ((BASIS, keys), jnp.float32),
        ]
    )
    found = run_kernel(
        kernel,
        list(grads)
        + [weight, probs_all, content_all, position_all, key_all, value_all]
        + [rel_turned, basis_turned],
        outs,
        scalars=where,
        flops=2 * length * width * (narrow + values),
        name="attention_backward",
    )
    return found[:count], found[count:]


def attention_weights(
    where, saved, grad_attn, grad_heads, grad_normed, gain, sums_two, bias_sums, rel_grad, n_blocks
):
    normed, unit_all, scale_all, mixed = saved[1], saved[2], saved[3], saved[9]
    width = normed.shape[1]
    rows = width // n_blocks
    narrow, values = grad_heads.shape[1], mixed.shape[1]
    columns = narrow + values
    keys = rel_grad.shape[1]
    spread = max(rows, keys)
    tall = 8 + -(-(2 + BASIS) // 8) * 8

    def kernel(where_ref, normed_ref, unit_ref, scale_ref, mixed_ref, attn_ref, *refs):
        heads_ref, grad_ref, gain_ref, two_ref, bias_ref, rel_ref = refs[:6]
        even_ref, odd_ref, small_even, small_odd, whole_ref, sums_ref = refs[6:]
        grad, unit = grad_ref[...], unit_ref[...]
        into = normalize_back(unit, scale_ref[:, :1], grad * gain_ref[...])
        sums_ref[0:1, :] = jnp.sum(grad * unit, axis=0, keepdims=True)
        sums_ref[1:2, :] = two_ref[0:1, :]
        sums_ref[2:3, :] = jnp.sum(grad, axis=0, keepdims=True)
        sums_ref[3:4, :] = two_ref[1:2, :]
        table = jnp.sum(into, axis=0, keepdims=True) + two_ref[2:3, :]
        for kind in range(SPECIES):
            sums_ref[4 + kind : 5 + kind, :] = jnp.where(where_ref[2] == kind, table, 0.0)
        sums = sums_ref[...]
        small_even[...] = jnp.zeros_like(small_even)
        small_odd[...] = jnp.zeros_like(small_odd)
        for m in range(n_blocks):
            spot = (where_ref[0] ^ m) if n_blocks > 1 else 0
            half = small_odd if m % 2 else small_even
            moved = pltpu.roll(sums, lax.rem(width - spot * rows, width), 1)
            half[m // 2, 0:8, :rows] = moved[:, :rows]
            turn = lax.rem(keys - spot * (KEYD // n_blocks), keys)
            half[m // 2, 8:10, :keys] = pltpu.roll(bias_ref[...], turn, 1)
            half[m // 2, 10 : 10 + BASIS, :keys] = pltpu.roll(rel_ref[...], turn, 1)
        whole_ref[:, :narrow] = dot_leading(normed_ref[...], heads_ref[...]).astype(LOW)
        whole_ref[:, narrow:] = dot_leading(attn_ref[...], mixed_ref[...]).astype(LOW)
        for m in range(n_blocks):
            spot = (where_ref[0] ^ m) * rows if n_blocks > 1 else 0
            half = odd_ref if m % 2 else even_ref
            half[m // 2] = whole_ref[pl.ds(pl.multiple_of(spot, rows), rows), :]

    half = max(n_blocks // 2, 1)
    return run_kernel(
        kernel,
        [normed, unit_all, scale_all, mixed, grad_attn, grad_heads, grad_normed, gain]
        + [sums_two, bias_sums, rel_grad],
        [((half, rows, columns), LOW)] * 2 + [((half, tall, spread), jnp.float32)] * 2,
        scalars=where,
        scratch=[pltpu.VMEM((width, columns), LOW), pltpu.VMEM((8, width), jnp.float32)],
        flops=2 * normed.shape[0] * width * columns,
        name="attention_weights",
    )


def unpack_small(where, blocks, basis_turned, width, local_heads):
    count, entries = blocks[0].shape
    n_blocks = len(blocks)
    total = n_blocks * count
    share = width // total
    n_rows = 8 + SPECIES
    group = width // n_blocks
    keys = local_heads * KEYD
    piece = keys // n_blocks
    part = KEYD // n_blocks
    length = basis_turned.shape[0]

    def kernel(where_ref, *refs):
        block_refs, basis_ref, refs = refs[:n_blocks], refs[n_blocks], refs[n_blocks + 1 :]
        row_refs, refs = refs[:5], refs[5:]
        taps_ref, bias_ref, rel_ref, content_ref, position_ref, found_ref, weight_ref = refs
        for m in range(n_blocks):
            found_ref[m * count : (m + 1) * count, :] = block_refs[m][...].astype(jnp.float32)

        def owner(shape):
            spot = lax.broadcasted_iota(jnp.int32, shape, 0)
            return (spot // count) ^ where_ref[0], lax.rem(spot % count + where_ref[1], count)

        def widen(start, size, span):
            column = lax.broadcasted_iota(jnp.int32, (size, span), 1)
            inner = lax.broadcasted_iota(jnp.int32, (size, span), 0)
            if size == share:
                chosen = column % share == inner
            else:
                chosen = (column // KEYD == inner // part) & (column % part == inner % part)
            return dot_rows(
                found_ref[:, start : start + size].astype(LOW),
                chosen.astype(jnp.float32).astype(LOW),
            )

        group_of, line_of = owner((total, width))
        column = lax.broadcasted_iota(jnp.int32, (total, width), 1) // share
        mask = group_of * count + line_of == column
        rows = [
            jnp.sum(jnp.where(mask, widen(r * share, share, width), 0.0), axis=0, keepdims=True)
            for r in range(4 + SPECIES)
        ]
        species = jnp.zeros((1, width), jnp.float32)
        for kind in range(SPECIES):
            species = jnp.where(where_ref[2] == kind, rows[4 + kind], species)
        for ref, row in zip(row_refs, rows[:4] + [species], strict=True):
            ref[...] = row
        group_of, line_of = owner((total, group))
        column = lax.broadcasted_iota(jnp.int32, (total, group), 1) // share
        mask = (group_of == where_ref[0]) & (line_of == column)
        rows = [
            jnp.sum(jnp.where(mask, widen(r * share, share, group), 0.0), axis=0, keepdims=True)
            for r in range(4 + SPECIES, n_rows)
        ]
        for r in range(3):
            taps_ref[r : r + 1, :] = rows[r]
        bias_ref[...] = rows[3]
        group_of, line_of = owner((total, keys))
        column = lax.broadcasted_iota(jnp.int32, (total, keys), 1) % KEYD // part
        mask = (line_of == where_ref[1]) & (group_of == column)
        start = n_rows * share
        for f in range(BASIS + 2):
            row = widen(start + f * piece, piece, keys)
            row = jnp.sum(jnp.where(mask, row, 0.0), axis=0, keepdims=True)
            if f < BASIS:
                weight_ref[f : f + 1, :] = row
            else:
                (content_ref if f == BASIS else position_ref)[...] = row
        rel_ref[...] = dot_rows(basis_ref[...], weight_ref[...].astype(LOW)).astype(LOW)

    found = run_kernel(
        kernel,
        list(blocks) + [basis_turned],
        [((1, width), jnp.float32)] * 5
        + [((3, group), jnp.float32), ((1, group), jnp.float32)]
        + [((length, keys), LOW)]
        + [((1, keys), jnp.float32)] * 2,
        scalars=where,
        scratch=[pltpu.VMEM((total, entries), jnp.float32), pltpu.VMEM((BASIS, keys), jnp.float32)],
        name="unpack_small",
    )
    return found[:5], found[5:]


def second_norm(own_part, parts, resid_in, gain, shift):
    own, width = own_part.shape

    def kernel(own_ref, *refs):
        part_refs, refs = refs[: len(parts)], refs[len(parts) :]
        raw_ref, species_ref, gain_ref, shift_ref, resid_ref, unit_ref, scale_ref, low_ref = refs
        total = own_ref[...]
        for ref in part_refs:
            total = total + ref[...].astype(jnp.float32)
        resid = raw_ref[...].astype(jnp.float32) + species_ref[...] + total
        unit, scale = normalize(resid)
        resid_ref[...] = resid
        unit_ref[...] = unit
        scale_ref[...] = jnp.broadcast_to(scale, (own, 128))
        low_ref[...] = (unit * gain_ref[...] + shift_ref[...]).astype(LOW)

    return run_kernel(
        kernel,
        [own_part] + list(parts) + list(resid_in) + [gain, shift],
        [
            ((own, width), jnp.float32),
            ((own, width), jnp.float32),
            ((own, 128), jnp.float32),
            ((own, width), LOW),
        ],
        name="second_norm",
    )


def second_norm_back(own_part, parts, unit, scale, gain, grad_resid):
    own, width = own_part.shape

    def kernel(own_ref, *refs):
        part_refs, refs = refs[: len(parts)], refs[len(parts) :]
        unit_ref, scale_ref, gain_ref, grad_ref, resid_ref, low_ref, sums_ref = refs
        total = own_ref[...]
        for ref in part_refs:
            total = total + ref[...].astype(jnp.float32)
        unit_rows = unit_ref[...]
        resid = grad_ref[...] + normalize_back(unit_rows, scale_ref[:, :1], total * gain_ref[...])
        resid_ref[...] = resid
        low_ref[...] = resid.astype(LOW)
        sums_ref[0:1, :] = jnp.sum(total * unit_rows, axis=0, keepdims=True)
        sums_ref[1:2, :] = jnp.sum(total, axis=0, keepdims=True)
        sums_ref[2:3, :] = jnp.sum(resid, axis=0, keepdims=True)

    return run_kernel(
        kernel,
        [own_part] + list(parts) + [unit, scale, gain, grad_resid],
        [((own, width), jnp.float32), ((own, width), LOW), ((3, width), jnp.float32)],
        name="second_norm_back",
    )


def first_norm_back(where, own_part, parts, unit_all, scale_all, gain, grad_resid):
    own, width = own_part.shape

    def kernel(where_ref, own_ref, *refs):
        part_refs, refs = refs[: len(parts)], refs[len(parts) :]
        unit_ref, scale_ref, gain_ref, grad_ref, out_ref = refs
        total = own_ref[...]
        for ref in part_refs:
            total = total + ref[...].astype(jnp.float32)
        spot = pl.ds(pl.multiple_of(where_ref[1] * own, own), own)
        out_ref[0] = grad_ref[...] + normalize_back(
            unit_ref[spot, :], scale_ref[spot, :1], total * gain_ref[...]
        )

    return run_kernel(
        kernel,
        [own_part] + list(parts) + [unit_all, scale_all, gain, grad_resid],
        [((1, own, width), jnp.float32)],
        scalars=where,
        name="first_norm_back",
    )[0]


def feed_forward_up(normed, weight):
    count, (own, width) = len(normed), normed[0].shape
    length = count * own
    hidden_count = weight.shape[1] // 2

    def kernel(*refs):
        normed_refs, weight_ref, own_ref, refs = refs[:count], refs[count], refs[count + 1], refs[count + 2 :]
        part_refs, (normed_out, hidden_out, slope_out) = refs[: count - 1], refs[count - 1 :]
        for k in range(count):
            normed_out[k * own : (k + 1) * own, :] = normed_refs[k][...]
        pre = dot_rows(normed_out[...], weight_ref[:, :hidden_count])
        below = 0.5 * (1.0 + lax.erf(pre * math.sqrt(0.5)))
        hidden_out[...] = (pre * below).astype(LOW)
        slope_out[...] = below + pre * jnp.exp(-0.5 * pre * pre) * (1.0 / math.sqrt(2.0 * math.pi))
        total = dot_transposed(hidden_out[...], weight_ref[:, hidden_count:])
        own_ref[...] = total[:own]
        for k in range(1, count):
            part_refs[k - 1][...] = total[k * own : (k + 1) * own].astype(LOW)

    found = run_kernel(
        kernel,
        list(normed) + [weight],
        [((own, width), jnp.float32)]
        + [((own, width), LOW)] * (count - 1)
        + [((length, width), LOW), ((length, hidden_count), LOW)]
        + [((length, hidden_count), jnp.float32)],
        flops=4 * length * width * hidden_count,
        name="feed_forward_up",
    )
    return found[:count], found[count:]


def feed_forward_back(grads, slope, weight):
    count, (own, width) = len(grads), grads[0].shape
    length = count * own
    hidden_count = weight.shape[1] // 2

    def kernel(*refs):
        grad_refs, (slope_ref, weight_ref, own_ref), refs = refs[:count], refs[count : count + 3], refs[count + 3 :]
        part_refs, (grad_out, pre_out) = refs[: count - 1], refs[count - 1 :]
        for k in range(count):
            grad_out[k * own : (k + 1) * own, :] = grad_refs[k][...]
        grad_hidden = dot_rows(grad_out[...], weight_ref[:, hidden_count:])
        pre_out[...] = (grad_hidden * slope_ref[...]).astype(LOW)
        total = dot_transposed(pre_out[...], weight_ref[:, :hidden_count])
        own_ref[...] = total[:own]
        for k in range(1, count):
            part_refs[k - 1][...] = total[k * own : (k + 1) * own].astype(LOW)

    found = run_kernel(
        kernel,
        list(grads) + [slope, weight],
        [((own, width), jnp.float32)]
        + [((own, width), LOW)] * (count - 1)
        + [((length, width), LOW), ((length, hidden_count), LOW)],
        flops=4 * length * width * hidden_count,
        name="feed_forward_back",
    )
    return found[:count], found[count:]


def feed_forward_weights(normed_all, grad_all, hidden, grad_pre):
    width = normed_all.shape[1]
    hidden_count = hidden.shape[1]

    def kernel(normed_ref, grad_ref, hidden_ref, pre_ref, out_ref):
        out_ref[:, :hidden_count] = dot_leading(normed_ref[...], pre_ref[...]).astype(LOW)
        out_ref[:, hidden_count:] = dot_leading(grad_ref[...], hidden_ref[...]).astype(LOW)

    return run_kernel(
        kernel,
        [normed_all, grad_all, hidden, grad_pre],
        [((width, 2 * hidden_count), LOW)],
        flops=4 * normed_all.shape[0] * width * hidden_count,
        name="feed_forward_weights",
    )[0]


def shifted(rows, first, last):
    count = rows.shape[0]
    place = lax.broadcasted_iota(jnp.int32, rows.shape, 0)
    before = jnp.where(place == 0, first, pltpu.roll(rows, 1, 0))
    after = jnp.where(place == count - 1, last, pltpu.roll(rows, count - 1, 0))
    return before, after


def group_weight(weight_ref, which, count, scratch_ref):
    share = weight_ref.shape[0] // (3 * count)
    for t in range(count):
        spot = (3 * t + which) * share
        scratch_ref[t * share : (t + 1) * share, :] = weight_ref[spot : spot + share, :]


def section_grad_deep(blocks, weight, count):
    fine, width = blocks[0].shape
    channels = weight.shape[0] // 3
    windows = len(blocks)

    def kernel(*refs):
        block_refs, refs = refs[:windows], refs[windows:]
        weight_ref, deep_ref, head_ref, tail_ref, point_ref = refs
        group_weight(weight_ref, 0, count, point_ref)
        for m in range(windows):
            deep = dot_transposed(block_refs[m][...], point_ref[...]).astype(LOW)
            deep_ref[m] = deep
            head_ref[m : m + 1, :] = deep[:1]
            tail_ref[m : m + 1, :] = deep[fine - 1 :]

    return run_kernel(
        kernel,
        list(blocks) + [weight],
        [((windows, fine, channels), LOW)] + [((windows, channels), LOW)] * 2,
        scratch=[pltpu.VMEM((channels, width), LOW)],
        flops=2 * windows * fine * width * channels,
        name="section_grad_deep",
    )


def section_grad_mix(deep, before, after, taps, weight, count):
    windows, fine, channels = deep.shape
    width = weight.shape[1]
    own = fine // 2

    def kernel(deep_ref, before_ref, after_ref, taps_ref, weight_ref, *refs):
        mix_ref, coarse_ref, even_ref, odd_ref, bias_ref, up_ref = refs
        group_weight(weight_ref, 1, count, up_ref)
        row = lax.broadcasted_iota(jnp.int32, (own, fine), 0)
        column = lax.broadcasted_iota(jnp.int32, (own, fine), 1)
        pool = (column // 2 == row).astype(jnp.float32).astype(LOW)
        bias = jnp.zeros((1, channels), jnp.float32)
        for m in range(windows):
            rows = deep_ref[m].astype(jnp.float32)
            previous, following = shifted(
                rows,
                before_ref[m : m + 1, :].astype(jnp.float32),
                after_ref[m : m + 1, :].astype(jnp.float32),
            )
            mix = (
                taps_ref[0:1, :] * following + taps_ref[1:2, :] * rows + taps_ref[2:3, :] * previous
            ).astype(LOW)
            mix_ref[m] = mix
            bias = bias + jnp.sum(mix.astype(jnp.float32), axis=0, keepdims=True)
            coarse = dot_rows(pool, mix).astype(LOW)
            coarse_ref[m] = coarse
            half = odd_ref if m % 2 else even_ref
            half[m // 2] = dot_rows(coarse, up_ref[...]).astype(LOW)
        bias_ref[...] = bias

    return run_kernel(
        kernel,
        [deep, before, after, taps, weight],
        [((windows, fine, channels), LOW), ((windows, own, channels), LOW)]
        + [((windows // 2, own, width), LOW)] * 2
        + [((1, channels), jnp.float32)],
        scratch=[pltpu.VMEM((channels, width), LOW)],
        flops=2 * windows * own * width * channels,
        name="section_grad_mix",
    )


def section_grad_encoder(mix, weight, count):
    windows, fine, channels = mix.shape
    width = weight.shape[1]

    def kernel(mix_ref, weight_ref, even_ref, odd_ref, lateral_ref):
        group_weight(weight_ref, 2, count, lateral_ref)
        for m in range(windows):
            half = odd_ref if m % 2 else even_ref
            half[m // 2] = dot_rows(mix_ref[m], lateral_ref[...]).astype(LOW)

    return run_kernel(
        kernel,
        [mix, weight],
        [((windows // 2, fine, width), LOW)] * 2,
        scratch=[pltpu.VMEM((channels, width), LOW)],
        flops=2 * windows * fine * width * channels,
        name="section_grad_encoder",
    )


def section_mixture(coarse_blocks, fine_blocks, weight, bias, count):
    fine, width = fine_blocks[0].shape
    own = fine // 2
    channels = weight.shape[0] // 3
    windows = len(fine_blocks)

    def kernel(*refs):
        coarse_refs, fine_refs, refs = refs[:windows], refs[windows : 2 * windows], refs[2 * windows :]
        weight_ref, bias_ref, mix_ref, head_ref, tail_ref, up_ref, lateral_ref = refs
        group_weight(weight_ref, 1, count, up_ref)
        group_weight(weight_ref, 2, count, lateral_ref)
        row = lax.broadcasted_iota(jnp.int32, (fine, own), 0)
        column = lax.broadcasted_iota(jnp.int32, (fine, own), 1)
        repeat = (row // 2 == column).astype(jnp.float32).astype(LOW)
        for m in range(windows):
            repeated = dot_rows(repeat, coarse_refs[m][...]).astype(LOW)
            mix = (
                dot_transposed(repeated, up_ref[...])
                + dot_transposed(fine_refs[m][...], lateral_ref[...])
                + bias_ref[...]
            ).astype(LOW)
            mix_ref[m] = mix
            head_ref[m : m + 1, :] = mix[:1]
            tail_ref[m : m + 1, :] = mix[fine - 1 :]

    return run_kernel(
        kernel,
        list(coarse_blocks) + list(fine_blocks) + [weight, bias],
        [((windows, fine, channels), LOW)] + [((windows, channels), LOW)] * 2,
        scratch=[pltpu.VMEM((channels, width), LOW)] * 2,
        flops=4 * windows * fine * width * channels,
        name="section_mixture",
    )


def section_deep(mix, before, after, taps, weight, grad_deep, count):
    windows, fine, channels = mix.shape
    width = weight.shape[1]

    def kernel(mix_ref, before_ref, after_ref, taps_ref, weight_ref, grad_ref, *refs):
        deep_ref, even_ref, odd_ref, sums_ref, point_ref = refs
        group_weight(weight_ref, 0, count, point_ref)
        sums = [jnp.zeros((1, channels), jnp.float32)] * 3
        for m in range(windows):
            rows = mix_ref[m].astype(jnp.float32)
            previous, following = shifted(
                rows,
                before_ref[m : m + 1, :].astype(jnp.float32),
                after_ref[m : m + 1, :].astype(jnp.float32),
            )
            deep = (
                taps_ref[0:1, :] * previous + taps_ref[1:2, :] * rows + taps_ref[2:3, :] * following
            ).astype(LOW)
            deep_ref[m] = deep
            half = odd_ref if m % 2 else even_ref
            half[m // 2] = dot_rows(deep, point_ref[...]).astype(LOW)
            grad = grad_ref[m].astype(jnp.float32)
            sums = [
                total + jnp.sum(part * grad, axis=0, keepdims=True)
                for total, part in zip(sums, (previous, rows, following), strict=True)
            ]
        for s, total in enumerate(sums):
            sums_ref[s : s + 1, :] = total

    return run_kernel(
        kernel,
        [mix, before, after, taps, weight, grad_deep],
        [((windows, fine, channels), LOW)]
        + [((windows // 2, fine, width), LOW)] * 2
        + [((3, channels), jnp.float32)],
        scratch=[pltpu.VMEM((channels, width), LOW)],
        flops=2 * windows * fine * width * channels,
        name="section_deep",
    )


def section_weights(deep, grad_coarse, grad_mix, cot_blocks, coarse_blocks, fine_blocks, count):
    windows, fine, channels = deep.shape
    width = cot_blocks[0].shape[1]
    share = channels // count

    def kernel(deep_ref, coarse_ref, mix_ref, *refs):
        cot_refs, refs = refs[:windows], refs[windows:]
        row_refs, refs = refs[:windows], refs[windows:]
        fine_refs, (out_ref,) = refs[:windows], refs[windows:]
        pairs = ((deep_ref, cot_refs), (coarse_ref, row_refs), (mix_ref, fine_refs))
        for which, (left_ref, right_refs) in enumerate(pairs):
            total = dot_leading(left_ref[0], right_refs[0][...])
            for m in range(1, windows):
                total = total + dot_leading(left_ref[m], right_refs[m][...])
            low = total.astype(LOW)
            for t in range(count):
                out_ref[t, which * share : (which + 1) * share, :] = low[t * share : (t + 1) * share]

    return run_kernel(
        kernel,
        [deep, grad_coarse, grad_mix] + list(cot_blocks) + list(coarse_blocks) + list(fine_blocks),
        [((count, 3 * share, width), LOW)],
        flops=5 * windows * fine * width * channels,
        name="section_weights",
    )[0]


def from_ahead(rows, step):
    count = lax.axis_size("tensor")
    return lax.ppermute(rows, "tensor", [((i + step) % count, i) for i in range(count)])


def spread_blocks(rows):
    return [rows] + [from_ahead(rows, k) for k in range(1, lax.axis_size("tensor"))]


def collect_blocks(parts):
    count = lax.axis_size("tensor")
    return [from_ahead(parts[k - 1], count - k) for k in range(1, count)]


def to_own(rows):
    return jnp.roll(rows, -lax.axis_index("tensor") * (rows.shape[0] // lax.axis_size("tensor")), 0)


def dp_flip(cells, mask):
    count = lax.axis_size("dp")
    return lax.ppermute(cells, "dp", [(i, i ^ mask) for i in range(count)])


def direct_dp():
    return lax.axis_size("dp") == 8


def gather_blocks(shard):
    blocks = {0: shard, 1: dp_flip(shard, 1)}
    for mask in (2, 4, 6):
        blocks[mask] = dp_flip(shard, mask)
    for mask in (2, 4, 6):
        blocks[mask + 1] = dp_flip(blocks[mask], 1)
    return [blocks[mask] for mask in range(8)]


def gather_rows(shard):
    if not direct_dp():
        return lax.all_gather(shard, "dp", axis=0, tiled=True)
    return jnp.concatenate(gather_blocks(shard), axis=0)


def scatter_halves(even, odd):
    if not direct_dp():
        return lax.psum_scatter(even[0], "dp", scatter_dimension=0, tiled=True).astype(jnp.float32)
    pairs = even.astype(jnp.float32) + dp_flip(odd, 1).astype(jnp.float32)
    total = pairs[0]
    for chip in range(1, even.shape[0]):
        total = total + dp_flip(pairs[chip].astype(even.dtype), 2 * chip).astype(jnp.float32)
    return total


def scatter_rows(parts):
    if not direct_dp():
        return lax.psum_scatter(parts, "dp", scatter_dimension=0, tiled=True).astype(jnp.float32)
    blocks = parts.reshape(8, -1, parts.shape[1])
    pairs = {
        mask: blocks[mask].astype(jnp.float32)
        + dp_flip(blocks[mask + 1], 1).astype(jnp.float32)
        for mask in (2, 4, 6, 0)
    }
    total = pairs[0]
    for mask in (2, 4, 6):
        total = total + dp_flip(pairs[mask].astype(parts.dtype), mask).astype(jnp.float32)
    return total


def gather_true(shard):
    if not direct_dp():
        return lax.all_gather(shard, "dp", axis=0, tiled=True)
    me = lax.axis_index("dp")
    rows = shard.shape[0]
    whole = jnp.zeros((8 * rows, shard.shape[1]), shard.dtype)
    for mask, block in enumerate(gather_blocks(shard)):
        whole = lax.dynamic_update_slice(whole, block, ((me ^ mask) * rows, 0))
    return whole


def scatter_true(whole):
    if not direct_dp():
        return lax.psum_scatter(whole, "dp", scatter_dimension=0, tiled=True).astype(jnp.float32)
    me = lax.axis_index("dp")
    rows = whole.shape[0] // 8
    blocks = [
        lax.dynamic_slice_in_dim(whole, (me ^ mask) * rows, rows, 0) for mask in range(8)
    ]
    return scatter_rows(jnp.concatenate(blocks, axis=0))


def gather_dp(shard):
    return lax.all_gather(shard, "dp", axis=0, tiled=True)


def scatter_dp(whole):
    return lax.psum_scatter(whole, "dp", scatter_dimension=0, tiled=True)


def scatter_tensor(whole):
    return lax.psum_scatter(whole, "tensor", scatter_dimension=0, tiled=True)


def gather_small(cells):
    count = lax.axis_size("tensor")
    line = jnp.stack([cells] + [from_ahead(cells, k) for k in range(1, count)], axis=0)
    if not direct_dp():
        line = jnp.roll(line, lax.axis_index("tensor"), 0)
        return lax.all_gather(line, "dp", axis=0)
    spots = jnp.arange(8 * count, dtype=jnp.int32)
    source = (spots // count ^ lax.axis_index("dp")) * count + (
        spots % count - lax.axis_index("tensor")
    ) % count
    found = jnp.concatenate(gather_blocks(line), axis=0)
    chosen = (source[:, None] == spots[None, :]).astype(LOW)
    return dot_plain(chosen, found).astype(LOW).reshape(8, count, -1)


def after(cells, *done):
    return lax.optimization_barrier((cells, done))[0]


def edges(head, tail):
    ends = lax.axis_size("tensor") - 1
    return (
        lax.ppermute(tail, "tensor", [(i, i + 1) for i in range(ends)]),
        lax.ppermute(head, "tensor", [(i + 1, i) for i in range(ends)]),
    )


def halo(cells):
    count = lax.axis_size("tensor")
    ends = count - 1
    before = lax.ppermute(cells[:, -1:], "tensor", [(i, i + 1) for i in range(ends)])
    after = lax.ppermute(cells[:, :1], "tensor", [(i + 1, i) for i in range(ends)])
    return jnp.concatenate([before, cells, after], axis=1)


def body_plain(
    activations,
    encoder,
    species,
    cotangent,
    norm_gain,
    norm_shift,
    species_table,
    query_weight,
    key_weight,
    value_weight,
    output_weight,
    expand_weight,
    contract_weight,
    position_weight,
    content_bias,
    position_bias,
    upsample_weight,
    lateral_weight,
    depthwise_weight,
    section_bias,
    pointwise_weight,
):
    windows = lax.axis_size("dp")
    count = lax.axis_size("tensor")
    own = activations.shape[1]
    length = own * count
    width = activations.shape[2]
    local_heads = query_weight.shape[1] // KEYD
    keys = local_heads * KEYD
    values = local_heads * VALD

    raw = spread_blocks(activations[0])
    attn_shard = jnp.concatenate([query_weight, key_weight, value_weight, output_weight.T], axis=1)
    attn_blocks = [gather_dp(attn_shard)]
    where = jnp.stack([lax.axis_index("dp"), lax.axis_index("tensor"), species[0]])

    small = jnp.concatenate(
        [norm_gain, norm_shift, species_table, depthwise_weight, section_bias[None]], axis=0
    )
    n_small = small.size
    n_position = position_weight.size
    n_bias = content_bias.size
    packed = gather_small(
        jnp.concatenate(
            [
                small.reshape(-1),
                position_weight.reshape(-1),
                content_bias.reshape(-1),
                position_bias.reshape(-1),
            ]
        )
    )
    small_all = packed[:, :, :n_small].reshape(windows, count, 10, -1)
    norm_all = jnp.transpose(small_all[:, :, :6], (2, 0, 1, 3)).reshape(6, width)
    norm_all = norm_all.astype(jnp.float32)
    gain_vals, shift_vals, table_rows = norm_all[:2], norm_all[2:4], norm_all[4:]
    small_group = lax.dynamic_index_in_dim(small_all, lax.axis_index("dp"), 0, False)
    small_group = jnp.swapaxes(small_group, 0, 1).reshape(10, -1).astype(jnp.float32)
    channels = small_group.shape[1]
    depth_taps = small_group[6:9]
    bias_section = small_group[9]
    heads_all = lax.dynamic_index_in_dim(packed, lax.axis_index("tensor"), 1, False)[:, n_small:]
    w_position = heads_all[:, :n_position].reshape(KEYD, BASIS, local_heads)
    bias_content = heads_all[:, n_position : n_position + n_bias].reshape(KEYD, local_heads)
    bias_position = heads_all[:, n_position + n_bias :].reshape(KEYD, local_heads)

    section_shard = jnp.concatenate([pointwise_weight, upsample_weight.T, lateral_weight.T], axis=0)
    w_section = lax.all_gather(section_shard, "tensor", axis=0).reshape(count, 3, -1, width)
    w_point = w_section[:, 0].reshape(channels, width)
    w_up = w_section[:, 1].reshape(channels, width)
    w_lat = w_section[:, 2].reshape(channels, width)
    cot_all = gather_dp(cotangent[0])
    ffn_shard = jnp.concatenate([expand_weight, contract_weight.T], axis=1)
    w_ffn = lax.all_gather(ffn_shard, "dp", axis=0, tiled=True)
    hidden_count = expand_weight.shape[1]
    enc_all = gather_dp(encoder[0])

    fine = 2 * own
    grad_deep = dot_transposed(cot_all, w_point).astype(LOW)
    grad_wide = halo(grad_deep.reshape(windows, fine, channels)).astype(jnp.float32)
    grad_mix = (
        depth_taps[0] * grad_wide[:, 2:]
        + depth_taps[1] * grad_wide[:, 1:-1]
        + depth_taps[2] * grad_wide[:, :-2]
    ).astype(LOW)
    grad_coarse = jnp.sum(
        grad_mix.astype(jnp.float32).reshape(windows * own, 2, channels), axis=1
    ).astype(LOW)
    grad_resid_two = scatter_dp(dot_plain(grad_coarse, w_up).astype(LOW)).astype(jnp.float32)
    grad_ffn = spread_blocks(grad_resid_two.astype(LOW))

    species_mask = (jnp.arange(SPECIES, dtype=jnp.int32) == species[0]).astype(jnp.float32)
    species_row = jnp.sum(species_mask[:, None] * table_rows, axis=0)
    content_flat = bias_content.astype(jnp.float32).T.reshape(1, -1)
    position_flat = bias_position.astype(jnp.float32).T.reshape(1, -1)
    basis_turned = jnp.pad(basis_table(length, BASIS).astype(LOW)[::-1], ((0, 1), (0, 0)))
    rel_weight = jnp.transpose(w_position, (1, 2, 0)).reshape(BASIS, -1)
    rel_turned = dot_plain(basis_turned, rel_weight).astype(LOW)
    attn_parts, saved = attention_forward(
        where,
        raw,
        [species_row[None], gain_vals[:1], shift_vals[:1], content_flat, position_flat],
        rel_turned,
        attn_blocks,
        local_heads,
    )
    resid_one, unit_two, scale_two, normed_two = second_norm(
        attn_parts[0],
        collect_blocks(attn_parts[1:]),
        [raw[0], species_row[None]],
        gain_vals[1:],
        shift_vals[1:],
    )

    contract_parts, (normed_two_all, hidden_low, slope) = feed_forward_up(
        spread_blocks(normed_two), w_ffn
    )
    ffn_parts, (grad_ffn_all, grad_hidden_pre) = feed_forward_back(grad_ffn, slope, w_ffn)
    grad_resid_one, grad_attn, sums_two = second_norm_back(
        ffn_parts[0],
        collect_blocks(ffn_parts[1:]),
        unit_two,
        scale_two,
        gain_vals[1:],
        grad_resid_two,
    )

    resid_two = resid_one + contract_parts[0]
    for block in collect_blocks(contract_parts[1:]):
        resid_two = resid_two + block.astype(jnp.float32)
    section_all = gather_dp(resid_two.astype(LOW))
    coarse = dot_transposed(section_all, w_up).reshape(windows, own, channels)
    section_mix = (
        jnp.repeat(coarse, 2, axis=1)
        + dot_transposed(enc_all, w_lat).reshape(windows, fine, channels)
        + bias_section
    ).astype(LOW)
    mix_wide = halo(section_mix).astype(jnp.float32)
    deep_rows = (
        depth_taps[0] * mix_wide[:, :-2]
        + depth_taps[1] * mix_wide[:, 1:-1]
        + depth_taps[2] * mix_wide[:, 2:]
    ).astype(LOW)
    deep_rows = deep_rows.reshape(windows * fine, channels)
    section_out = scatter_dp(dot_plain(deep_rows, w_point).astype(LOW)).astype(LOW)
    grad_mix_rows = grad_mix.reshape(windows * fine, channels)
    encoder_grad = scatter_dp(dot_plain(grad_mix_rows, w_lat).astype(LOW)).astype(jnp.float32)
    grad_centre = grad_wide[:, 1:-1]
    grad_section_small = jnp.stack(
        [jnp.sum(mix_wide[:, s : s + fine] * grad_centre, axis=(0, 1)) for s in range(3)]
        + [jnp.sum(grad_mix.astype(jnp.float32), axis=(0, 1))],
        axis=1,
    )
    section_cols = jnp.stack(
        [
            dot_leading(deep_rows, cot_all).astype(LOW).reshape(count, -1, width),
            dot_leading(grad_coarse, section_all).astype(LOW).reshape(count, -1, width),
            dot_leading(grad_mix_rows, enc_all).astype(LOW).reshape(count, -1, width),
        ],
        axis=1,
    )
    section_cols = scatter_tensor(section_cols)[0].astype(jnp.float32)

    ffn_out = scatter_dp(
        feed_forward_weights(normed_two_all, grad_ffn_all, hidden_low, grad_hidden_pre)
    ).astype(jnp.float32)

    head_parts, (grad_attn_all, grad_heads, grad_normed_part, bias_sums, rel_grad) = (
        attention_backward(
            where, spread_blocks(grad_attn), saved, rel_turned, basis_turned, local_heads
        )
    )
    grad_resid_in = first_norm_back(
        where,
        head_parts[0],
        collect_blocks(head_parts[1:]),
        saved[2],
        saved[3],
        gain_vals[:1],
        grad_resid_one,
    )
    weights, _, small, _ = attention_weights(
        where, saved, grad_attn_all, grad_heads, grad_normed_part, gain_vals[:1], sums_two,
        bias_sums, rel_grad, 1,
    )
    attn_out = scatter_dp(weights[0]).astype(jnp.float32)
    norm_cols = jnp.swapaxes(small[0, :6].reshape(6, windows, channels), 0, 1)
    head_cols = small[0, 8 : 10 + BASIS, :keys].reshape(2 + BASIS, local_heads, KEYD)
    head_cols = jnp.transpose(head_cols, (2, 0, 1))
    heads_cols = jnp.concatenate(
        [
            head_cols[:, 2:].reshape(windows, -1),
            head_cols[:, 0].reshape(windows, -1),
            head_cols[:, 1].reshape(windows, -1),
        ],
        axis=1,
    )
    small_out = scatter_dp(jnp.concatenate([norm_cols.reshape(windows, -1), heads_cols], axis=1))
    small_out = small_out[0]
    n_norm = 6 * channels
    group_cols = jnp.concatenate([small_out[:n_norm].reshape(6, channels), grad_section_small.T])
    group_cols = jnp.swapaxes(group_cols.reshape(10, count, -1), 0, 1).reshape(count, -1)
    group_cols = to_own(group_cols)
    norm_out = group_cols[0]
    for k in range(1, count):
        norm_out = norm_out + from_ahead(group_cols[k], count - k)
    norm_out = norm_out.reshape(10, -1)
    heads_out = small_out[n_norm:]
    return (
        section_out[None],
        grad_resid_in,
        encoder_grad[None],
        norm_out[0:2],
        norm_out[2:4],
        norm_out[4:6],
        attn_out[:, :keys],
        attn_out[:, keys : 2 * keys],
        attn_out[:, 2 * keys : 2 * keys + values],
        attn_out[:, 2 * keys + values :].T,
        ffn_out[:, :hidden_count],
        ffn_out[:, hidden_count:].T,
        heads_out[:n_position].reshape(position_weight.shape),
        heads_out[n_position : n_position + n_bias].reshape(content_bias.shape),
        heads_out[n_position + n_bias :].reshape(position_bias.shape),
        section_cols[1].T,
        section_cols[2].T,
        norm_out[6:9],
        norm_out[9],
        section_cols[0],
    )


def body_direct(
    activations,
    encoder,
    species,
    cotangent,
    norm_gain,
    norm_shift,
    species_table,
    query_weight,
    key_weight,
    value_weight,
    output_weight,
    expand_weight,
    contract_weight,
    position_weight,
    content_bias,
    position_bias,
    upsample_weight,
    lateral_weight,
    depthwise_weight,
    section_bias,
    pointwise_weight,
):
    count = lax.axis_size("tensor")
    own, width = activations.shape[1:]
    length = own * count
    local_heads = query_weight.shape[1] // KEYD
    keys = local_heads * KEYD
    values = local_heads * VALD
    hidden_count = expand_weight.shape[1]
    share = section_bias.shape[0]
    where = jnp.stack([lax.axis_index("dp"), lax.axis_index("tensor"), species[0]])

    packed = jnp.concatenate(
        [
            norm_gain.reshape(-1),
            norm_shift.reshape(-1),
            species_table.reshape(-1),
            depthwise_weight.reshape(-1),
            section_bias,
            jnp.transpose(position_weight, (1, 2, 0)).reshape(-1),
            content_bias.T.reshape(-1),
            position_bias.T.reshape(-1),
        ]
    )[None]
    line = jnp.concatenate(spread_blocks(packed), axis=0)
    raw = spread_blocks(activations[0])
    attn_shard = jnp.concatenate([query_weight, key_weight, value_weight, output_weight.T], axis=1)
    attn_blocks = gather_blocks(attn_shard)
    small_blocks = gather_blocks(line)
    section_shard = jnp.concatenate([pointwise_weight, upsample_weight.T, lateral_weight.T], axis=0)
    w_section = lax.all_gather(section_shard, "tensor", axis=0, tiled=True)
    small_blocks, raw, attn_blocks = lax.optimization_barrier((small_blocks, raw, attn_blocks))
    ffn_shard = jnp.concatenate([expand_weight, contract_weight.T], axis=1)
    w_ffn = lax.all_gather(ffn_shard, "dp", axis=0, tiled=True)

    basis_turned = jnp.pad(basis_table(length, BASIS).astype(LOW)[::-1], ((0, 1), (0, 0)))
    rows, (depth_taps, bias_section, rel_turned, content_flat, position_flat) = unpack_small(
        where, small_blocks, basis_turned, width, local_heads
    )
    gain_one, gain_two, shift_one, shift_two, species_row = rows
    attn_parts, saved = attention_forward(
        where,
        raw,
        [species_row, gain_one, shift_one, content_flat, position_flat],
        rel_turned,
        attn_blocks,
        local_heads,
    )
    attn_received = collect_blocks(attn_parts[1:])

    cot_blocks = gather_blocks(after(cotangent[0], attn_blocks))
    grad_deep, head, tail = section_grad_deep(cot_blocks, w_section, count)
    before, following = edges(head, tail)
    grad_mix, grad_coarse, even, odd, bias_grad = section_grad_mix(
        grad_deep, before, following, depth_taps, w_section, count
    )
    grad_resid_two = scatter_halves(even, odd)
    grad_ffn = spread_blocks(grad_resid_two.astype(LOW))

    resid_one, unit_two, scale_two, normed_two = second_norm(
        attn_parts[0], attn_received, [raw[0], species_row], gain_two, shift_two
    )
    contract_parts, (normed_two_all, hidden_low, slope) = feed_forward_up(
        spread_blocks(normed_two), w_ffn
    )
    ffn_parts, (grad_ffn_all, grad_hidden_pre) = feed_forward_back(grad_ffn, slope, w_ffn)
    grad_resid_one, grad_attn, sums_two = second_norm_back(
        ffn_parts[0], collect_blocks(ffn_parts[1:]), unit_two, scale_two, gain_two, grad_resid_two
    )

    enc_blocks = gather_blocks(after(encoder[0], grad_resid_two))
    resid_two = resid_one + contract_parts[0]
    for block in collect_blocks(contract_parts[1:]):
        resid_two = resid_two + block.astype(jnp.float32)
    section_blocks = gather_blocks(resid_two.astype(LOW))
    section_mix, head, tail = section_mixture(
        section_blocks, enc_blocks, w_section, bias_section, count
    )
    before, following = edges(head, tail)
    deep_rows, out_even, out_odd, taps_grad = section_deep(
        section_mix, before, following, depth_taps, w_section, grad_deep, count
    )
    encoder_grad = scatter_halves(*section_grad_encoder(grad_mix, w_section, count))
    section_out = scatter_halves(out_even, out_odd).astype(LOW)
    section_cols = section_weights(
        deep_rows, grad_coarse, grad_mix, cot_blocks, section_blocks, enc_blocks, count
    )
    section_cols = scatter_tensor(section_cols)[0].astype(jnp.float32)
    ffn_out = scatter_dp(
        feed_forward_weights(normed_two_all, grad_ffn_all, hidden_low, grad_hidden_pre)
    ).astype(jnp.float32)

    head_parts, (grad_attn_all, grad_heads, grad_normed_part, bias_sums, rel_grad) = (
        attention_backward(
            where, spread_blocks(grad_attn), saved, rel_turned, basis_turned, local_heads
        )
    )
    grad_resid_in = first_norm_back(
        where,
        head_parts[0],
        collect_blocks(head_parts[1:]),
        saved[2],
        saved[3],
        gain_one,
        grad_resid_one,
    )
    even, odd, small_even, small_odd = attention_weights(
        where,
        saved,
        grad_attn_all,
        grad_heads,
        grad_normed_part,
        gain_one,
        sums_two,
        bias_sums,
        rel_grad,
        len(attn_blocks),
    )
    small_out = scatter_halves(small_even, small_odd)
    attn_out = scatter_halves(even, odd)

    n_norm = 4 + SPECIES
    group = share * count
    group_cols = jnp.concatenate([small_out[:n_norm, :group], taps_grad, bias_grad], axis=0)
    norm_out = group_cols
    for k in range(1, count):
        norm_out = norm_out + from_ahead(group_cols, k)
    norm_out = lax.dynamic_slice_in_dim(norm_out, lax.axis_index("tensor") * share, share, 1)
    part = KEYD // lax.axis_size("dp")
    heads_out = small_out[8 : 10 + BASIS, :keys].reshape(2 + BASIS, local_heads, KEYD)[:, :, :part]
    heads_out = jnp.transpose(heads_out, (2, 0, 1))
    return (
        section_out[None],
        grad_resid_in,
        encoder_grad[None],
        norm_out[0:2],
        norm_out[2:4],
        norm_out[4:n_norm],
        attn_out[:, :keys],
        attn_out[:, keys : 2 * keys],
        attn_out[:, 2 * keys : 2 * keys + values],
        attn_out[:, 2 * keys + values :].T,
        ffn_out[:, :hidden_count],
        ffn_out[:, hidden_count:].T,
        heads_out[:, 2:],
        heads_out[:, 0],
        heads_out[:, 1],
        section_cols[share : 2 * share].T,
        section_cols[2 * share :].T,
        norm_out[n_norm : n_norm + 3],
        norm_out[n_norm + 3],
        section_cols[:share],
    )


def solution(mesh):
    rows = P("dp", "tensor", None)
    narrow = P(None, ("dp", "tensor"))
    split = P("dp", "tensor")
    turned = P("tensor", "dp")
    vector = P(("dp", "tensor"))
    tall = P(("dp", "tensor"), None)
    position = P("dp", None, "tensor")
    weights = (split, split, split, turned, split, turned, position, split, split)
    return jax.shard_map(
        body_direct if mesh.shape["dp"] == 8 else body_plain,
        mesh=mesh,
        in_specs=(rows, rows, P("dp"), rows, narrow, narrow, narrow)
        + weights
        + (narrow, narrow, narrow, vector, tall),
        out_specs=(rows, rows, rows, narrow, narrow, narrow)
        + weights
        + (narrow, narrow, narrow, vector, tall),
        check_vma=False,
    )
```

```python
import math

import jax
import jax.numpy as jnp
from jax import lax
from jax.experimental import pallas as pl
from jax.experimental.pallas import tpu as pltpu
from jax.sharding import PartitionSpec as P

KEYD = 64
VALD = 192
BASIS = 32
SPECIES = 2
SCALE = 1.0 / math.sqrt(KEYD)
LOW = jnp.bfloat16


def dot_plain(left_side, right_side):
    return jnp.dot(left_side, right_side, preferred_element_type=jnp.float32)


def dot_transposed(left_side, right_side):
    return lax.dot_general(
        left_side, right_side, (((1,), (1,)), ((), ())), preferred_element_type=jnp.float32
    )


def dot_leading(left_side, right_side):
    return lax.dot_general(
        left_side, right_side, (((0,), (0,)), ((), ())), preferred_element_type=jnp.float32
    )


def exact_gelu(values):
    return jax.nn.gelu(values, approximate=False)


def normalize(values):
    centred = values - jnp.mean(values, axis=-1, keepdims=True)
    variance = jnp.mean(centred * centred, axis=-1, keepdims=True)
    scale = lax.rsqrt(variance + 1e-05)
    return centred * scale, scale


def normalize_back(unit, scale, grad_unit):
    return scale * (
        grad_unit
        - jnp.mean(grad_unit, axis=-1, keepdims=True)
        - unit * jnp.mean(grad_unit * unit, axis=-1, keepdims=True)
    )


def basis_table(length, features):
    distance = jnp.arange(2 * length - 1).astype(jnp.float32) - (length - 1)
    halves = features // 2
    fraction = jnp.arange(halves).astype(jnp.float32) / (halves - 1)
    lifetimes = 3.0 * jnp.power(length / 3.0, fraction)
    decays = jnp.exp(-0.6931471805599453 * jnp.abs(distance)[:, None] / lifetimes[None, :])
    return jnp.concatenate([decays, jnp.sign(distance)[:, None] * decays], axis=1)


def dot_rows(left_side, right_side):
    return jnp.dot(left_side, right_side, preferred_element_type=jnp.float32)


def run_kernel(kernel, ins, outs, scalars=None, scratch=(), flops=0, name=None, spare=8):
    whole = pl.BlockSpec(memory_space=pltpu.VMEM)
    specs = [whole] * len(ins)
    args = list(ins)
    if scalars is not None:
        specs = [pl.BlockSpec(memory_space=pltpu.SMEM)] + specs
        args = [scalars] + args
    shapes = [jax.ShapeDtypeStruct(shape, dtype) for shape, dtype in outs]
    moved = sum(x.size * x.dtype.itemsize for x in list(ins) + shapes)
    held = sum(math.prod(x.shape) * jnp.dtype(x.dtype).itemsize for x in scratch)
    room = 56 * 1024 * 1024
    return pl.pallas_call(
        kernel,
        in_specs=specs,
        out_specs=[whole] * len(shapes),
        out_shape=shapes,
        scratch_shapes=scratch,
        compiler_params=pltpu.CompilerParams(vmem_limit_bytes=room),
        cost_estimate=pl.CostEstimate(flops=flops, bytes_accessed=moved, transcendentals=0),
        name=name,
    )(*args)


def lanes_of(head, width, shape):
    lane = lax.broadcasted_iota(jnp.int32, shape, len(shape) - 1)
    return (lane >= head * width) & (lane < (head + 1) * width)


def chunk_of(where_ref, step, count):
    return lax.rem(where_ref[1] + step, count)


def attention_forward(where, raw, row_params, rel_turned, blocks, local_heads):
    count, (own, width) = len(raw), raw[0].shape
    length = count * own
    n_blocks, columns = len(blocks), blocks[0].shape[1]
    rows = width // n_blocks
    keys, values = local_heads * KEYD, local_heads * VALD

    def kernel(where_ref, *refs):
        raw_refs, refs = refs[:count], refs[count:]
        species_ref, gain_ref, shift_ref, content_ref, position_ref, rel_ref = refs[:6]
        block_refs, refs = refs[6 : 6 + n_blocks], refs[6 + n_blocks :]
        own_ref, refs = refs[0], refs[1:]
        part_refs, refs = refs[: count - 1], refs[count - 1 :]
        (weight_ref, normed_ref, unit_ref, scale_ref, probs_ref, content_out, position_out) = refs[:7]
        key_out, value_out, mixed_out, total_ref = refs[7:]
        for m in range(n_blocks):
            spot = (where_ref[0] ^ m) * rows if n_blocks > 1 else 0
            weight_ref[pl.ds(pl.multiple_of(spot, rows), rows), :] = block_refs[m][:rows, :]
        for k in range(count):
            resid = raw_refs[k][...].astype(jnp.float32) + species_ref[...]
            unit, scale = normalize(resid)
            spot = pl.ds(pl.multiple_of(chunk_of(where_ref, k, count) * own, own), own)
            unit_ref[spot, :] = unit
            scale_ref[spot, :] = jnp.broadcast_to(scale, (own, 128))
            normed_ref[spot, :] = (unit * gain_ref[...] + shift_ref[...]).astype(LOW)
        normed = normed_ref[...]
        query = dot_rows(normed, weight_ref[:, :keys])
        content = (query + content_ref[...]).astype(LOW)
        position = (query + position_ref[...]).astype(LOW)
        key_low = dot_rows(normed, weight_ref[:, keys : 2 * keys]).astype(LOW)
        value_low = dot_rows(normed, weight_ref[:, 2 * keys : 2 * keys + values]).astype(LOW)
        content_out[...] = content
        position_out[...] = position
        key_out[...] = key_low
        value_out[...] = value_low
        mixed = jnp.zeros((length, values), jnp.float32)
        for h in range(local_heads):
            mine = lanes_of(h, KEYD, (length, keys))
            zero = jnp.zeros((), LOW)
            banded = dot_transposed(jnp.where(mine, position, zero), rel_ref[...])
            skewed = pltpu.roll(banded, length + 1, 1, stride=1, stride_axis=0)[:, :length]
            scores = (dot_transposed(jnp.where(mine, content, zero), key_low) + skewed) * SCALE
            exponent = jnp.exp(scores - jnp.max(scores, axis=-1, keepdims=True))
            probs = exponent / jnp.sum(exponent, axis=-1, keepdims=True)
            probs_ref[h] = probs
            mixed = jnp.where(
                lanes_of(h, VALD, (length, values)), dot_rows(probs.astype(LOW), value_low), mixed
            )
        mixed_out[...] = mixed.astype(LOW)
        total_ref[...] = dot_transposed(mixed.astype(LOW), weight_ref[:, 2 * keys + values :])
        for k in range(count):
            spot = pl.ds(pl.multiple_of(chunk_of(where_ref, k, count) * own, own), own)
            if k == 0:
                own_ref[...] = total_ref[spot, :]
            else:
                part_refs[k - 1][...] = total_ref[spot, :].astype(LOW)

    outs = (
        [((own, width), jnp.float32)]
        + [((own, width), LOW)] * (count - 1)
        + [
            ((width, columns), LOW),
            ((length, width), LOW),
            ((length, width), jnp.float32),
            ((length, 128), jnp.float32),
            ((local_heads, length, length), jnp.float32),
            ((length, keys), LOW),
            ((length, keys), LOW),
            ((length, keys), LOW),
            ((length, values), LOW),
            ((length, values), LOW),
        ]
    )
    found = run_kernel(
        kernel,
        list(raw) + list(row_params) + [rel_turned] + list(blocks),
        outs,
        scalars=where,
        scratch=[pltpu.VMEM((length, width), jnp.float32)],
        flops=2 * length * width * columns,
        name="attention_forward",
    )
    return found[:count], found[count:]


def attention_backward(where, grads, saved, rel_turned, basis_turned, local_heads):
    count, (own, width) = len(grads), grads[0].shape
    length = count * own
    weight, _, _, _, probs_all, content_all, position_all, key_all, value_all, _ = saved
    keys, values = local_heads * KEYD, local_heads * VALD
    narrow = 2 * keys + values

    def kernel(where_ref, *refs):
        grad_refs, refs = refs[:count], refs[count:]
        weight_ref, probs_ref, content_ref, position_ref, key_ref, value_ref = refs[:6]
        rel_ref, basis_ref = refs[6:8]
        own_ref, refs = refs[8], refs[9:]
        part_refs, refs = refs[: count - 1], refs[count - 1 :]
        attn_ref, heads_ref, total_ref, bias_ref, weight_out = refs
        for k in range(count):
            spot = pl.ds(pl.multiple_of(chunk_of(where_ref, k, count) * own, own), own)
            attn_ref[spot, :] = grad_refs[k][...]
        grad_mixed = dot_rows(attn_ref[...], weight_ref[:, narrow:]).astype(LOW)
        content, position = content_ref[...], position_ref[...]
        key_low, value_low = key_ref[...], value_ref[...]
        grad_content = jnp.zeros((length, keys), jnp.float32)
        grad_position = jnp.zeros((length, keys), jnp.float32)
        grad_key = jnp.zeros((length, keys), jnp.float32)
        grad_rel = jnp.zeros((2 * length, keys), jnp.float32)
        grad_value = jnp.zeros((length, values), jnp.float32)
        back = lax.broadcasted_iota(jnp.int32, (length, 2 * length), 0)
        for h in range(local_heads):
            mine = lanes_of(h, KEYD, (length, keys))
            ours = lanes_of(h, VALD, (length, values))
            probs = probs_ref[h]
            grad_probs = dot_transposed(
                jnp.where(ours, grad_mixed, jnp.zeros((), LOW)), value_low
            )
            centre = jnp.sum(probs * grad_probs, axis=-1, keepdims=True)
            grad_scores = (probs * (grad_probs - centre)).astype(LOW)
            grad_value = jnp.where(ours, dot_leading(probs.astype(LOW), grad_mixed), grad_value)
            grad_key = jnp.where(mine, dot_leading(grad_scores, content), grad_key)
            grad_content = jnp.where(mine, dot_rows(grad_scores, key_low), grad_content)
            band = jnp.concatenate(
                [grad_scores.astype(jnp.float32), jnp.zeros((length, length), jnp.float32)], axis=1
            )
            bit = 1
            while bit < length:
                turn = (length - 1 - back) & bit
                band = jnp.where(turn > 0, pltpu.roll(band, bit, 1), band)
                bit *= 2
            band = band.astype(LOW)
            grad_position = jnp.where(mine, dot_rows(band, rel_ref[...]), grad_position)
            grad_rel = jnp.where(
                lanes_of(h, KEYD, (2 * length, keys)), dot_leading(band, position), grad_rel
            )
        grad_content = grad_content * SCALE
        grad_position = grad_position * SCALE
        bias_ref[0:1, :] = jnp.sum(grad_content, axis=0, keepdims=True)
        bias_ref[1:2, :] = jnp.sum(grad_position, axis=0, keepdims=True)
        heads_ref[:, :keys] = (grad_content + grad_position).astype(LOW)
        heads_ref[:, keys : 2 * keys] = (grad_key * SCALE).astype(LOW)
        heads_ref[:, 2 * keys :] = grad_value.astype(LOW)
        weight_out[...] = dot_leading(basis_ref[...], (grad_rel * SCALE).astype(LOW))
        total_ref[...] = dot_transposed(heads_ref[...], weight_ref[:, :narrow])
        for k in range(count):
            spot = pl.ds(pl.multiple_of(chunk_of(where_ref, k, count) * own, own), own)
            if k == 0:
                own_ref[...] = total_ref[spot, :]
            else:
                part_refs[k - 1][...] = total_ref[spot, :].astype(LOW)

    outs = (
        [((own, width), jnp.float32)]
        + [((own, width), LOW)] * (count - 1)
        + [
            ((length, width), LOW),
            ((length, narrow), LOW),
            ((length, width), jnp.float32),
            ((2, keys), jnp.float32),
            ((BASIS, keys), jnp.float32),
        ]
    )
    found = run_kernel(
        kernel,
        list(grads)
        + [weight, probs_all, content_all, position_all, key_all, value_all]
        + [rel_turned, basis_turned],
        outs,
        scalars=where,
        flops=2 * length * width * (narrow + values),
        name="attention_backward",
    )
    return found[:count], found[count:]


def attention_weights(
    where, saved, grad_attn, grad_heads, grad_normed, gain, sums_two, bias_sums, rel_grad, n_blocks
):
    normed, unit_all, scale_all, mixed = saved[1], saved[2], saved[3], saved[9]
    width = normed.shape[1]
    rows = width // n_blocks
    narrow, values = grad_heads.shape[1], mixed.shape[1]
    columns = narrow + values
    keys = rel_grad.shape[1]
    spread = max(rows, keys)
    tall = 8 + -(-(2 + BASIS) // 8) * 8

    def kernel(where_ref, normed_ref, unit_ref, scale_ref, mixed_ref, attn_ref, *refs):
        heads_ref, grad_ref, gain_ref, two_ref, bias_ref, rel_ref = refs[:6]
        even_ref, odd_ref, small_even, small_odd, whole_ref, sums_ref = refs[6:]
        grad, unit = grad_ref[...], unit_ref[...]
        into = normalize_back(unit, scale_ref[:, :1], grad * gain_ref[...])
        sums_ref[0:1, :] = jnp.sum(grad * unit, axis=0, keepdims=True)
        sums_ref[1:2, :] = two_ref[0:1, :]
        sums_ref[2:3, :] = jnp.sum(grad, axis=0, keepdims=True)
        sums_ref[3:4, :] = two_ref[1:2, :]
        table = jnp.sum(into, axis=0, keepdims=True) + two_ref[2:3, :]
        for kind in range(SPECIES):
            sums_ref[4 + kind : 5 + kind, :] = jnp.where(where_ref[2] == kind, table, 0.0)
        sums = sums_ref[...]
        small_even[...] = jnp.zeros_like(small_even)
        small_odd[...] = jnp.zeros_like(small_odd)
        for m in range(n_blocks):
            spot = (where_ref[0] ^ m) if n_blocks > 1 else 0
            half = small_odd if m % 2 else small_even
            moved = pltpu.roll(sums, lax.rem(width - spot * rows, width), 1)
            half[m // 2, 0:8, :rows] = moved[:, :rows]
            turn = lax.rem(keys - spot * (KEYD // n_blocks), keys)
            half[m // 2, 8:10, :keys] = pltpu.roll(bias_ref[...], turn, 1)
            half[m // 2, 10 : 10 + BASIS, :keys] = pltpu.roll(rel_ref[...], turn, 1)
        whole_ref[:, :narrow] = dot_leading(normed_ref[...], heads_ref[...]).astype(LOW)
        whole_ref[:, narrow:] = dot_leading(attn_ref[...], mixed_ref[...]).astype(LOW)
        for m in range(n_blocks):
            spot = (where_ref[0] ^ m) * rows if n_blocks > 1 else 0
            half = odd_ref if m % 2 else even_ref
            half[m // 2] = whole_ref[pl.ds(pl.multiple_of(spot, rows), rows), :]

    half = max(n_blocks // 2, 1)
    return run_kernel(
        kernel,
        [normed, unit_all, scale_all, mixed, grad_attn, grad_heads, grad_normed, gain]
        + [sums_two, bias_sums, rel_grad],
        [((half, rows, columns), LOW)] * 2 + [((half, tall, spread), jnp.float32)] * 2,
        scalars=where,
        scratch=[pltpu.VMEM((width, columns), LOW), pltpu.VMEM((8, width), jnp.float32)],
        flops=2 * normed.shape[0] * width * columns,
        name="attention_weights",
    )


def unpack_small(where, blocks, basis_turned, width, local_heads, count):
    half, entries = blocks[0].shape
    total = 2 * half
    n_blocks = total // count
    share = width // total
    n_rows = 8 + SPECIES
    group = width // n_blocks
    keys = local_heads * KEYD
    piece = keys // n_blocks
    part = KEYD // n_blocks
    length = basis_turned.shape[0]

    def kernel(where_ref, *refs):
        block_refs, basis_ref, refs = refs[:2], refs[2], refs[3:]
        row_refs, refs = refs[:5], refs[5:]
        taps_ref, bias_ref, rel_ref, content_ref, position_ref, found_ref, weight_ref = refs
        for core in range(2):
            found_ref[core * half : (core + 1) * half, :] = block_refs[core][...].astype(jnp.float32)

        def owner(shape):
            spot = lax.broadcasted_iota(jnp.int32, shape, 0)
            block = 2 * (spot % half // count) + spot // half
            return block ^ where_ref[0], lax.rem(spot % count + where_ref[1], count)

        def widen(start, size, span):
            column = lax.broadcasted_iota(jnp.int32, (size, span), 1)
            inner = lax.broadcasted_iota(jnp.int32, (size, span), 0)
            if size == share:
                chosen = column % share == inner
            else:
                chosen = (column // KEYD == inner // part) & (column % part == inner % part)
            return dot_rows(
                found_ref[:, start : start + size].astype(LOW),
                chosen.astype(jnp.float32).astype(LOW),
            )

        group_of, line_of = owner((total, width))
        column = lax.broadcasted_iota(jnp.int32, (total, width), 1) // share
        mask = group_of * count + line_of == column
        rows = [
            jnp.sum(jnp.where(mask, widen(r * share, share, width), 0.0), axis=0, keepdims=True)
            for r in range(4 + SPECIES)
        ]
        species = jnp.zeros((1, width), jnp.float32)
        for kind in range(SPECIES):
            species = jnp.where(where_ref[2] == kind, rows[4 + kind], species)
        for ref, row in zip(row_refs, rows[:4] + [species], strict=True):
            ref[...] = row
        group_of, line_of = owner((total, group))
        column = lax.broadcasted_iota(jnp.int32, (total, group), 1) // share
        mask = (group_of == where_ref[0]) & (line_of == column)
        rows = [
            jnp.sum(jnp.where(mask, widen(r * share, share, group), 0.0), axis=0, keepdims=True)
            for r in range(4 + SPECIES, n_rows)
        ]
        for r in range(3):
            taps_ref[r : r + 1, :] = rows[r]
        bias_ref[...] = rows[3]
        group_of, line_of = owner((total, keys))
        column = lax.broadcasted_iota(jnp.int32, (total, keys), 1) % KEYD // part
        mask = (line_of == where_ref[1]) & (group_of == column)
        start = n_rows * share
        for f in range(BASIS + 2):
            row = widen(start + f * piece, piece, keys)
            row = jnp.sum(jnp.where(mask, row, 0.0), axis=0, keepdims=True)
            if f < BASIS:
                weight_ref[f : f + 1, :] = row
            else:
                (content_ref if f == BASIS else position_ref)[...] = row
        rel_ref[...] = dot_rows(basis_ref[...], weight_ref[...].astype(LOW)).astype(LOW)

    found = run_kernel(
        kernel,
        list(blocks) + [basis_turned],
        [((1, width), jnp.float32)] * 5
        + [((3, group), jnp.float32), ((1, group), jnp.float32)]
        + [((length, keys), LOW)]
        + [((1, keys), jnp.float32)] * 2,
        scalars=where,
        scratch=[pltpu.VMEM((total, entries), jnp.float32), pltpu.VMEM((BASIS, keys), jnp.float32)],
        name="unpack_small",
    )
    return found[:5], found[5:]


def second_norm(own_part, parts, resid_in, gain, shift):
    own, width = own_part.shape

    def kernel(own_ref, *refs):
        part_refs, refs = refs[: len(parts)], refs[len(parts) :]
        raw_ref, species_ref, gain_ref, shift_ref, resid_ref, unit_ref, scale_ref, low_ref = refs
        total = own_ref[...]
        for ref in part_refs:
            total = total + ref[...].astype(jnp.float32)
        resid = raw_ref[...].astype(jnp.float32) + species_ref[...] + total
        unit, scale = normalize(resid)
        resid_ref[...] = resid
        unit_ref[...] = unit
        scale_ref[...] = jnp.broadcast_to(scale, (own, 128))
        low_ref[...] = (unit * gain_ref[...] + shift_ref[...]).astype(LOW)

    return run_kernel(
        kernel,
        [own_part] + list(parts) + list(resid_in) + [gain, shift],
        [
            ((own, width), jnp.float32),
            ((own, width), jnp.float32),
            ((own, 128), jnp.float32),
            ((own, width), LOW),
        ],
        name="second_norm",
    )


def second_norm_back(own_part, parts, unit, scale, gain, grad_resid):
    own, width = own_part.shape

    def kernel(own_ref, *refs):
        part_refs, refs = refs[: len(parts)], refs[len(parts) :]
        unit_ref, scale_ref, gain_ref, grad_ref, resid_ref, low_ref, sums_ref = refs
        total = own_ref[...]
        for ref in part_refs:
            total = total + ref[...].astype(jnp.float32)
        unit_rows = unit_ref[...]
        resid = grad_ref[...] + normalize_back(unit_rows, scale_ref[:, :1], total * gain_ref[...])
        resid_ref[...] = resid
        low_ref[...] = resid.astype(LOW)
        sums_ref[0:1, :] = jnp.sum(total * unit_rows, axis=0, keepdims=True)
        sums_ref[1:2, :] = jnp.sum(total, axis=0, keepdims=True)
        sums_ref[2:3, :] = jnp.sum(resid, axis=0, keepdims=True)

    return run_kernel(
        kernel,
        [own_part] + list(parts) + [unit, scale, gain, grad_resid],
        [((own, width), jnp.float32), ((own, width), LOW), ((3, width), jnp.float32)],
        name="second_norm_back",
    )


def first_norm_back(where, own_part, parts, unit_all, scale_all, gain, grad_resid):
    own, width = own_part.shape

    def kernel(where_ref, own_ref, *refs):
        part_refs, refs = refs[: len(parts)], refs[len(parts) :]
        unit_ref, scale_ref, gain_ref, grad_ref, out_ref = refs
        total = own_ref[...]
        for ref in part_refs:
            total = total + ref[...].astype(jnp.float32)
        spot = pl.ds(pl.multiple_of(where_ref[1] * own, own), own)
        out_ref[0] = grad_ref[...] + normalize_back(
            unit_ref[spot, :], scale_ref[spot, :1], total * gain_ref[...]
        )

    return run_kernel(
        kernel,
        [own_part] + list(parts) + [unit_all, scale_all, gain, grad_resid],
        [((1, own, width), jnp.float32)],
        scalars=where,
        name="first_norm_back",
    )[0]


def feed_forward_up(where, normed, weight):
    count, (own, width) = len(normed), normed[0].shape
    length = count * own
    hidden_count = weight.shape[1] // 2

    def kernel(where_ref, *refs):
        normed_refs, (weight_ref, part_ref, normed_out, hidden_out, slope_out) = refs[:count], refs[count:]
        for k in range(count):
            normed_out[k * own : (k + 1) * own, :] = normed_refs[k][...]
        pre = dot_rows(normed_out[...], weight_ref[:, :hidden_count])
        below = 0.5 * (1.0 + lax.erf(pre * math.sqrt(0.5)))
        hidden_out[...] = (pre * below).astype(LOW)
        slope_out[...] = below + pre * jnp.exp(-0.5 * pre * pre) * (1.0 / math.sqrt(2.0 * math.pi))
        total = dot_transposed(hidden_out[...], weight_ref[:, hidden_count:])
        for k in range(count):
            spot = pl.ds(pl.multiple_of(chunk_of(where_ref, k, count) * own, own), own)
            part_ref[spot, :] = total[k * own : (k + 1) * own].astype(LOW)

    return run_kernel(
        kernel,
        list(normed) + [weight],
        [((length, width), LOW)] * 2
        + [((length, hidden_count), LOW), ((length, hidden_count), jnp.float32)],
        scalars=where,
        flops=4 * length * width * hidden_count,
        name="feed_forward_up",
    )


def feed_forward_back(grads, slope, weight):
    count, (own, width) = len(grads), grads[0].shape
    length = count * own
    hidden_count = weight.shape[1] // 2

    def kernel(*refs):
        grad_refs, (slope_ref, weight_ref, own_ref), refs = refs[:count], refs[count : count + 3], refs[count + 3 :]
        part_refs, (grad_out, pre_out) = refs[: count - 1], refs[count - 1 :]
        for k in range(count):
            grad_out[k * own : (k + 1) * own, :] = grad_refs[k][...]
        grad_hidden = dot_rows(grad_out[...], weight_ref[:, hidden_count:])
        pre_out[...] = (grad_hidden * slope_ref[...]).astype(LOW)
        total = dot_transposed(pre_out[...], weight_ref[:, :hidden_count])
        own_ref[...] = total[:own]
        for k in range(1, count):
            part_refs[k - 1][...] = total[k * own : (k + 1) * own].astype(LOW)

    found = run_kernel(
        kernel,
        list(grads) + [slope, weight],
        [((own, width), jnp.float32)]
        + [((own, width), LOW)] * (count - 1)
        + [((length, width), LOW), ((length, hidden_count), LOW)],
        flops=4 * length * width * hidden_count,
        name="feed_forward_back",
    )
    return found[:count], found[count:]


def feed_forward_weights(where, normed_all, grad_all, hidden, grad_pre, n_blocks):
    width = normed_all.shape[1]
    hidden_count = hidden.shape[1]
    rows = width // n_blocks

    def kernel(where_ref, normed_ref, grad_ref, hidden_ref, pre_ref, even_ref, odd_ref, whole_ref):
        whole_ref[:, :hidden_count] = dot_leading(normed_ref[...], pre_ref[...]).astype(LOW)
        whole_ref[:, hidden_count:] = dot_leading(grad_ref[...], hidden_ref[...]).astype(LOW)
        for m in range(n_blocks):
            spot = (where_ref[0] ^ m) * rows if n_blocks > 1 else 0
            half = odd_ref if m % 2 else even_ref
            half[m // 2] = whole_ref[pl.ds(pl.multiple_of(spot, rows), rows), :]

    half = max(n_blocks // 2, 1)
    return run_kernel(
        kernel,
        [normed_all, grad_all, hidden, grad_pre],
        [((half, rows, 2 * hidden_count), LOW)] * 2,
        scalars=where,
        scratch=[pltpu.VMEM((width, 2 * hidden_count), LOW)],
        flops=4 * normed_all.shape[0] * width * hidden_count,
        name="feed_forward_weights",
    )


def shifted(rows, first, last):
    count = rows.shape[0]
    place = lax.broadcasted_iota(jnp.int32, rows.shape, 0)
    before = jnp.where(place == 0, first, pltpu.roll(rows, 1, 0))
    after = jnp.where(place == count - 1, last, pltpu.roll(rows, count - 1, 0))
    return before, after


def section_grad_deep(blocks, weight, count):
    fine, width = blocks[0].shape
    channels = weight.shape[0] // 3
    share = channels // count
    windows = len(blocks)

    def kernel(*refs):
        block_refs, weight_ref, refs = refs[:windows], refs[windows], refs[windows + 1 :]
        deep_ref, head_ref, tail_ref, *whole_refs = refs
        for which, ref in enumerate(whole_refs):
            for t in range(count):
                spot = (3 * t + which) * share
                ref[t * share : (t + 1) * share, :] = weight_ref[spot : spot + share, :]
        for m in range(windows):
            deep = dot_transposed(block_refs[m][...], whole_refs[0][...]).astype(LOW)
            deep_ref[m] = deep
            head_ref[m : m + 1, :] = deep[:1]
            tail_ref[m : m + 1, :] = deep[fine - 1 :]

    return run_kernel(
        kernel,
        list(blocks) + [weight],
        [((windows, fine, channels), LOW)]
        + [((windows, channels), LOW)] * 2
        + [((channels, width), LOW)] * 3,
        flops=2 * windows * fine * width * channels,
        name="section_grad_deep",
    )


def section_grad_mix(deep, before, after, taps, up):
    windows, fine, channels = deep.shape
    width = up.shape[1]
    own = fine // 2

    def kernel(deep_ref, before_ref, after_ref, taps_ref, up_ref, *refs):
        mix_ref, coarse_ref, even_ref, odd_ref, bias_ref = refs
        row = lax.broadcasted_iota(jnp.int32, (own, fine), 0)
        column = lax.broadcasted_iota(jnp.int32, (own, fine), 1)
        pool = (column // 2 == row).astype(jnp.float32).astype(LOW)
        bias = jnp.zeros((1, channels), jnp.float32)
        for m in range(windows):
            rows = deep_ref[m].astype(jnp.float32)
            previous, following = shifted(
                rows,
                before_ref[m : m + 1, :].astype(jnp.float32),
                after_ref[m : m + 1, :].astype(jnp.float32),
            )
            mix = (
                taps_ref[0:1, :] * following + taps_ref[1:2, :] * rows + taps_ref[2:3, :] * previous
            ).astype(LOW)
            mix_ref[m] = mix
            bias = bias + jnp.sum(mix.astype(jnp.float32), axis=0, keepdims=True)
            coarse = dot_rows(pool, mix).astype(LOW)
            coarse_ref[m] = coarse
            half = odd_ref if m % 2 else even_ref
            half[m // 2] = dot_rows(coarse, up_ref[...]).astype(LOW)
        bias_ref[...] = bias

    return run_kernel(
        kernel,
        [deep, before, after, taps, up],
        [((windows, fine, channels), LOW), ((windows, own, channels), LOW)]
        + [((windows // 2, own, width), LOW)] * 2
        + [((1, channels), jnp.float32)],
        flops=2 * windows * own * width * channels,
        name="section_grad_mix",
    )


def section_grad_encoder(mix, lateral):
    windows, fine, channels = mix.shape
    width = lateral.shape[1]

    def kernel(mix_ref, lateral_ref, even_ref, odd_ref):
        for m in range(windows):
            half = odd_ref if m % 2 else even_ref
            half[m // 2] = dot_rows(mix_ref[m], lateral_ref[...]).astype(LOW)

    return run_kernel(
        kernel,
        [mix, lateral],
        [((windows // 2, fine, width), LOW)] * 2,
        flops=2 * windows * fine * width * channels,
        name="section_grad_encoder",
    )


def section_mixture(coarse_blocks, fine_blocks, up, lateral, bias):
    own, width = coarse_blocks[0].shape
    fine = 2 * own
    channels = lateral.shape[0]
    windows = len(coarse_blocks)

    def kernel(*refs):
        coarse_refs, fine_refs, refs = refs[:windows], refs[windows : 2 * windows], refs[2 * windows :]
        up_ref, lateral_ref, bias_ref, mix_ref, head_ref, tail_ref = refs
        row = lax.broadcasted_iota(jnp.int32, (fine, own), 0)
        column = lax.broadcasted_iota(jnp.int32, (fine, own), 1)
        repeat = (row // 2 == column).astype(jnp.float32).astype(LOW)
        for m in range(windows):
            repeated = dot_rows(repeat, coarse_refs[m][...]).astype(LOW)
            mix = (
                dot_transposed(repeated, up_ref[...])
                + dot_transposed(fine_refs[m][...], lateral_ref[...])
                + bias_ref[...]
            ).astype(LOW)
            mix_ref[m] = mix
            head_ref[m : m + 1, :] = mix[:1]
            tail_ref[m : m + 1, :] = mix[fine - 1 :]

    return run_kernel(
        kernel,
        list(coarse_blocks) + list(fine_blocks) + [up, lateral, bias],
        [((windows, fine, channels), LOW)] + [((windows, channels), LOW)] * 2,
        flops=4 * windows * fine * width * channels,
        name="section_mixture",
    )


def section_deep(mix, before, after, taps, point, grad_deep):
    windows, fine, channels = mix.shape
    width = point.shape[1]

    def kernel(mix_ref, before_ref, after_ref, taps_ref, point_ref, grad_ref, *refs):
        deep_ref, even_ref, odd_ref, sums_ref = refs
        sums = [jnp.zeros((1, channels), jnp.float32)] * 3
        for m in range(windows):
            rows = mix_ref[m].astype(jnp.float32)
            previous, following = shifted(
                rows,
                before_ref[m : m + 1, :].astype(jnp.float32),
                after_ref[m : m + 1, :].astype(jnp.float32),
            )
            deep = (
                taps_ref[0:1, :] * previous + taps_ref[1:2, :] * rows + taps_ref[2:3, :] * following
            ).astype(LOW)
            deep_ref[m] = deep
            half = odd_ref if m % 2 else even_ref
            half[m // 2] = dot_rows(deep, point_ref[...]).astype(LOW)
            grad = grad_ref[m].astype(jnp.float32)
            sums = [
                total + jnp.sum(part * grad, axis=0, keepdims=True)
                for total, part in zip(sums, (previous, rows, following), strict=True)
            ]
        for s, total in enumerate(sums):
            sums_ref[s : s + 1, :] = total

    return run_kernel(
        kernel,
        [mix, before, after, taps, point, grad_deep],
        [((windows, fine, channels), LOW)]
        + [((windows // 2, fine, width), LOW)] * 2
        + [((3, channels), jnp.float32)],
        flops=2 * windows * fine * width * channels,
        name="section_deep",
    )


def section_weights(deep, grad_coarse, grad_mix, cot_blocks, coarse_blocks, fine_blocks, count):
    windows, fine, channels = deep.shape
    width = cot_blocks[0].shape[1]
    share = channels // count

    def kernel(deep_ref, coarse_ref, mix_ref, *refs):
        cot_refs, refs = refs[:windows], refs[windows:]
        row_refs, refs = refs[:windows], refs[windows:]
        fine_refs, (out_ref,) = refs[:windows], refs[windows:]
        pairs = ((deep_ref, cot_refs), (coarse_ref, row_refs), (mix_ref, fine_refs))
        for which, (left_ref, right_refs) in enumerate(pairs):
            total = dot_leading(left_ref[0], right_refs[0][...])
            for m in range(1, windows):
                total = total + dot_leading(left_ref[m], right_refs[m][...])
            low = total.astype(LOW)
            for t in range(count):
                out_ref[t, which * share : (which + 1) * share, :] = low[t * share : (t + 1) * share]

    return run_kernel(
        kernel,
        [deep, grad_coarse, grad_mix] + list(cot_blocks) + list(coarse_blocks) + list(fine_blocks),
        [((count, 3 * share, width), LOW)],
        flops=5 * windows * fine * width * channels,
        name="section_weights",
    )[0]


def from_ahead(rows, step):
    count = lax.axis_size("tensor")
    return lax.ppermute(rows, "tensor", [((i + step) % count, i) for i in range(count)])


def spread_blocks(rows):
    return [rows] + [from_ahead(rows, k) for k in range(1, lax.axis_size("tensor"))]


def collect_blocks(parts):
    count = lax.axis_size("tensor")
    return [from_ahead(parts[k - 1], count - k) for k in range(1, count)]


def to_own(rows):
    return jnp.roll(rows, -lax.axis_index("tensor") * (rows.shape[0] // lax.axis_size("tensor")), 0)


def dp_flip(cells, mask):
    count = lax.axis_size("dp")
    return lax.ppermute(cells, "dp", [(i, i ^ mask) for i in range(count)])


def half_rows(cells, axis=0):
    return cells.shape[axis] // 32 * 16


def both_cores(*chips):
    return [block for chip in chips for block in (chip, dp_flip(chip, 1))]


def chips_of(shard):
    return [shard] + [dp_flip(shard, mask) for mask in (2, 4, 6)]


def send_sum(cells, mask, dtype):
    return dp_flip(cells.astype(dtype), mask).astype(jnp.float32)


def core_pairs(even, odd):
    return even.astype(jnp.float32) + dp_flip(odd, 1).astype(jnp.float32)


def corner_sums(pairs, dtype):
    half = half_rows(pairs, 1)
    return send_sum(pairs[3, :half], 2, dtype), send_sum(pairs[3, half:], 4, dtype)


def chip_sums(pairs, corners, dtype):
    half = half_rows(pairs, 1)
    near = jnp.concatenate([pairs[1, :half], pairs[1, half:] + corners[1]], axis=0)
    far = jnp.concatenate([pairs[2, :half] + corners[0], pairs[2, half:]], axis=0)
    return pairs[0] + send_sum(near, 2, dtype) + send_sum(far, 4, dtype)


def direct_sums(pairs, dtype):
    return pairs[0] + sum(send_sum(pairs[chip], 2 * chip, dtype) for chip in (1, 2, 3))


def scatter_halves(even, odd, small=False):
    pairs, dtype = core_pairs(even, odd), even.dtype
    if small:
        return direct_sums(pairs, dtype)
    return chip_sums(pairs, corner_sums(pairs, dtype), dtype)


def gather_dp(shard):
    return lax.all_gather(shard, "dp", axis=0, tiled=True)


def scatter_dp(whole):
    return lax.psum_scatter(whole, "dp", scatter_dimension=0, tiled=True)


def scatter_tensor(whole):
    return lax.psum_scatter(whole, "tensor", scatter_dimension=0, tiled=True)


def gather_small(cells):
    line = jnp.stack(spread_blocks(cells), axis=0)
    return lax.all_gather(jnp.roll(line, lax.axis_index("tensor"), 0), "dp", axis=0)


def join(*arrays):
    return lax.optimization_barrier(arrays)


def edges(head, tail):
    ends = lax.axis_size("tensor") - 1
    return (
        lax.ppermute(tail, "tensor", [(i, i + 1) for i in range(ends)]),
        lax.ppermute(head, "tensor", [(i + 1, i) for i in range(ends)]),
    )


def halo(cells):
    count = lax.axis_size("tensor")
    ends = count - 1
    before = lax.ppermute(cells[:, -1:], "tensor", [(i, i + 1) for i in range(ends)])
    after = lax.ppermute(cells[:, :1], "tensor", [(i + 1, i) for i in range(ends)])
    return jnp.concatenate([before, cells, after], axis=1)


def body_plain(
    activations,
    encoder,
    species,
    cotangent,
    norm_gain,
    norm_shift,
    species_table,
    query_weight,
    key_weight,
    value_weight,
    output_weight,
    expand_weight,
    contract_weight,
    position_weight,
    content_bias,
    position_bias,
    upsample_weight,
    lateral_weight,
    depthwise_weight,
    section_bias,
    pointwise_weight,
):
    windows = lax.axis_size("dp")
    count = lax.axis_size("tensor")
    own = activations.shape[1]
    length = own * count
    width = activations.shape[2]
    local_heads = query_weight.shape[1] // KEYD
    keys = local_heads * KEYD
    values = local_heads * VALD

    raw = spread_blocks(activations[0])
    attn_shard = jnp.concatenate([query_weight, key_weight, value_weight, output_weight.T], axis=1)
    attn_blocks = [gather_dp(attn_shard)]
    where = jnp.stack([lax.axis_index("dp"), lax.axis_index("tensor"), species[0]])

    small = jnp.concatenate(
        [norm_gain, norm_shift, species_table, depthwise_weight, section_bias[None]], axis=0
    )
    n_small = small.size
    n_position = position_weight.size
    n_bias = content_bias.size
    packed = gather_small(
        jnp.concatenate(
            [
                small.reshape(-1),
                position_weight.reshape(-1),
                content_bias.reshape(-1),
                position_bias.reshape(-1),
            ]
        )
    )
    small_all = packed[:, :, :n_small].reshape(windows, count, 10, -1)
    norm_all = jnp.transpose(small_all[:, :, :6], (2, 0, 1, 3)).reshape(6, width)
    norm_all = norm_all.astype(jnp.float32)
    gain_vals, shift_vals, table_rows = norm_all[:2], norm_all[2:4], norm_all[4:]
    small_group = lax.dynamic_index_in_dim(small_all, lax.axis_index("dp"), 0, False)
    small_group = jnp.swapaxes(small_group, 0, 1).reshape(10, -1).astype(jnp.float32)
    channels = small_group.shape[1]
    depth_taps = small_group[6:9]
    bias_section = small_group[9]
    heads_all = lax.dynamic_index_in_dim(packed, lax.axis_index("tensor"), 1, False)[:, n_small:]
    w_position = heads_all[:, :n_position].reshape(KEYD, BASIS, local_heads)
    bias_content = heads_all[:, n_position : n_position + n_bias].reshape(KEYD, local_heads)
    bias_position = heads_all[:, n_position + n_bias :].reshape(KEYD, local_heads)

    section_shard = jnp.concatenate([pointwise_weight, upsample_weight.T, lateral_weight.T], axis=0)
    w_section = lax.all_gather(section_shard, "tensor", axis=0).reshape(count, 3, -1, width)
    w_point = w_section[:, 0].reshape(channels, width)
    w_up = w_section[:, 1].reshape(channels, width)
    w_lat = w_section[:, 2].reshape(channels, width)
    cot_all = gather_dp(cotangent[0])
    ffn_shard = jnp.concatenate([expand_weight, contract_weight.T], axis=1)
    w_ffn = lax.all_gather(ffn_shard, "dp", axis=0, tiled=True)
    hidden_count = expand_weight.shape[1]
    enc_all = gather_dp(encoder[0])

    fine = 2 * own
    grad_deep = dot_transposed(cot_all, w_point).astype(LOW)
    grad_wide = halo(grad_deep.reshape(windows, fine, channels)).astype(jnp.float32)
    grad_mix = (
        depth_taps[0] * grad_wide[:, 2:]
        + depth_taps[1] * grad_wide[:, 1:-1]
        + depth_taps[2] * grad_wide[:, :-2]
    ).astype(LOW)
    grad_coarse = jnp.sum(
        grad_mix.astype(jnp.float32).reshape(windows * own, 2, channels), axis=1
    ).astype(LOW)
    grad_resid_two = scatter_dp(dot_plain(grad_coarse, w_up).astype(LOW)).astype(jnp.float32)
    grad_ffn = spread_blocks(grad_resid_two.astype(LOW))

    species_mask = (jnp.arange(SPECIES, dtype=jnp.int32) == species[0]).astype(jnp.float32)
    species_row = jnp.sum(species_mask[:, None] * table_rows, axis=0)
    content_flat = bias_content.astype(jnp.float32).T.reshape(1, -1)
    position_flat = bias_position.astype(jnp.float32).T.reshape(1, -1)
    basis_turned = jnp.pad(basis_table(length, BASIS).astype(LOW)[::-1], ((0, 1), (0, 0)))
    rel_weight = jnp.transpose(w_position, (1, 2, 0)).reshape(BASIS, -1)
    rel_turned = dot_plain(basis_turned, rel_weight).astype(LOW)
    attn_parts, saved = attention_forward(
        where,
        raw,
        [species_row[None], gain_vals[:1], shift_vals[:1], content_flat, position_flat],
        rel_turned,
        attn_blocks,
        local_heads,
    )
    resid_one, unit_two, scale_two, normed_two = second_norm(
        attn_parts[0],
        collect_blocks(attn_parts[1:]),
        [raw[0], species_row[None]],
        gain_vals[1:],
        shift_vals[1:],
    )

    contract_part, normed_two_all, hidden_low, slope = feed_forward_up(
        where, spread_blocks(normed_two), w_ffn
    )
    ffn_parts, (grad_ffn_all, grad_hidden_pre) = feed_forward_back(grad_ffn, slope, w_ffn)
    grad_resid_one, grad_attn, sums_two = second_norm_back(
        ffn_parts[0],
        collect_blocks(ffn_parts[1:]),
        unit_two,
        scale_two,
        gain_vals[1:],
        grad_resid_two,
    )

    resid_two = resid_one + scatter_tensor(contract_part).astype(jnp.float32)
    section_all = gather_dp(resid_two.astype(LOW))
    coarse = dot_transposed(section_all, w_up).reshape(windows, own, channels)
    section_mix = (
        jnp.repeat(coarse, 2, axis=1)
        + dot_transposed(enc_all, w_lat).reshape(windows, fine, channels)
        + bias_section
    ).astype(LOW)
    mix_wide = halo(section_mix).astype(jnp.float32)
    deep_rows = (
        depth_taps[0] * mix_wide[:, :-2]
        + depth_taps[1] * mix_wide[:, 1:-1]
        + depth_taps[2] * mix_wide[:, 2:]
    ).astype(LOW)
    deep_rows = deep_rows.reshape(windows * fine, channels)
    section_out = scatter_dp(dot_plain(deep_rows, w_point).astype(LOW)).astype(LOW)
    grad_mix_rows = grad_mix.reshape(windows * fine, channels)
    encoder_grad = scatter_dp(dot_plain(grad_mix_rows, w_lat).astype(LOW)).astype(jnp.float32)
    grad_centre = grad_wide[:, 1:-1]
    grad_section_small = jnp.stack(
        [jnp.sum(mix_wide[:, s : s + fine] * grad_centre, axis=(0, 1)) for s in range(3)]
        + [jnp.sum(grad_mix.astype(jnp.float32), axis=(0, 1))],
        axis=1,
    )
    section_cols = jnp.stack(
        [
            dot_leading(deep_rows, cot_all).astype(LOW).reshape(count, -1, width),
            dot_leading(grad_coarse, section_all).astype(LOW).reshape(count, -1, width),
            dot_leading(grad_mix_rows, enc_all).astype(LOW).reshape(count, -1, width),
        ],
        axis=1,
    )
    section_cols = scatter_tensor(section_cols)[0].astype(jnp.float32)

    ffn_out = scatter_dp(
        feed_forward_weights(
            where, normed_two_all, grad_ffn_all, hidden_low, grad_hidden_pre, 1
        )[0][0]
    ).astype(jnp.float32)

    head_parts, (grad_attn_all, grad_heads, grad_normed_part, bias_sums, rel_grad) = (
        attention_backward(
            where, spread_blocks(grad_attn), saved, rel_turned, basis_turned, local_heads
        )
    )
    grad_resid_in = first_norm_back(
        where,
        head_parts[0],
        collect_blocks(head_parts[1:]),
        saved[2],
        saved[3],
        gain_vals[:1],
        grad_resid_one,
    )
    weights, _, small, _ = attention_weights(
        where, saved, grad_attn_all, grad_heads, grad_normed_part, gain_vals[:1], sums_two,
        bias_sums, rel_grad, 1,
    )
    attn_out = scatter_dp(weights[0]).astype(jnp.float32)
    norm_cols = jnp.swapaxes(small[0, :6].reshape(6, windows, channels), 0, 1)
    head_cols = small[0, 8 : 10 + BASIS, :keys].reshape(2 + BASIS, local_heads, KEYD)
    head_cols = jnp.transpose(head_cols, (2, 0, 1))
    heads_cols = jnp.concatenate(
        [
            head_cols[:, 2:].reshape(windows, -1),
            head_cols[:, 0].reshape(windows, -1),
            head_cols[:, 1].reshape(windows, -1),
        ],
        axis=1,
    )
    small_out = scatter_dp(jnp.concatenate([norm_cols.reshape(windows, -1), heads_cols], axis=1))
    small_out = small_out[0]
    n_norm = 6 * channels
    group_cols = jnp.concatenate([small_out[:n_norm].reshape(6, channels), grad_section_small.T])
    group_cols = jnp.swapaxes(group_cols.reshape(10, count, -1), 0, 1).reshape(count, -1)
    group_cols = to_own(group_cols)
    norm_out = group_cols[0]
    for k in range(1, count):
        norm_out = norm_out + from_ahead(group_cols[k], count - k)
    norm_out = norm_out.reshape(10, -1)
    heads_out = small_out[n_norm:]
    return (
        section_out[None],
        grad_resid_in,
        encoder_grad[None],
        norm_out[0:2],
        norm_out[2:4],
        norm_out[4:6],
        attn_out[:, :keys],
        attn_out[:, keys : 2 * keys],
        attn_out[:, 2 * keys : 2 * keys + values],
        attn_out[:, 2 * keys + values :].T,
        ffn_out[:, :hidden_count],
        ffn_out[:, hidden_count:].T,
        heads_out[:n_position].reshape(position_weight.shape),
        heads_out[n_position : n_position + n_bias].reshape(content_bias.shape),
        heads_out[n_position + n_bias :].reshape(position_bias.shape),
        section_cols[1].T,
        section_cols[2].T,
        norm_out[6:9],
        norm_out[9],
        section_cols[0],
    )


def body_direct(
    activations,
    encoder,
    species,
    cotangent,
    norm_gain,
    norm_shift,
    species_table,
    query_weight,
    key_weight,
    value_weight,
    output_weight,
    expand_weight,
    contract_weight,
    position_weight,
    content_bias,
    position_bias,
    upsample_weight,
    lateral_weight,
    depthwise_weight,
    section_bias,
    pointwise_weight,
):
    count = lax.axis_size("tensor")
    own, width = activations.shape[1:]
    length = own * count
    local_heads = query_weight.shape[1] // KEYD
    keys = local_heads * KEYD
    values = local_heads * VALD
    hidden_count = expand_weight.shape[1]
    share = section_bias.shape[0]
    where = jnp.stack([lax.axis_index("dp"), lax.axis_index("tensor"), species[0]])

    packed = jnp.concatenate(
        [
            norm_gain.reshape(-1),
            norm_shift.reshape(-1),
            species_table.reshape(-1),
            depthwise_weight.reshape(-1),
            section_bias,
            jnp.transpose(position_weight, (1, 2, 0)).reshape(-1),
            content_bias.T.reshape(-1),
            position_bias.T.reshape(-1),
        ]
    )[None]
    attn_shard = jnp.concatenate([query_weight, key_weight, value_weight, output_weight.T], axis=1)
    attn_chips = chips_of(attn_shard)
    line = spread_blocks(packed)
    section_shard = jnp.concatenate([pointwise_weight, upsample_weight.T, lateral_weight.T], axis=0)
    w_section = lax.all_gather(section_shard, "tensor", axis=0, tiled=True)
    line, rows = join(line, activations[0])
    raw = spread_blocks(rows)
    small_chips = jnp.concatenate(chips_of(jnp.concatenate(line, axis=0)), axis=0)
    small_blocks = [small_chips, dp_flip(small_chips, 1)]
    attn_blocks = both_cores(*attn_chips)
    attn_blocks, small_blocks, raw, cot = join(attn_blocks, small_blocks, raw, cotangent[0])
    cot_chips = chips_of(cot)
    basis_turned = jnp.pad(basis_table(length, BASIS).astype(LOW)[::-1], ((0, 1), (0, 0)))
    rows, (depth_taps, bias_section, rel_turned, content_flat, position_flat) = unpack_small(
        where, small_blocks, basis_turned, width, local_heads, count
    )
    gain_one, gain_two, shift_one, shift_two, species_row = rows
    attn_parts, saved = attention_forward(
        where,
        raw,
        [species_row, gain_one, shift_one, content_flat, position_flat],
        rel_turned,
        attn_blocks,
        local_heads,
    )
    attn_parts, cot_chips = join(attn_parts, cot_chips)

    attn_received = collect_blocks(attn_parts[1:])
    cot_blocks = both_cores(*cot_chips)
    grad_deep, head, tail, w_point, w_up, w_lateral = section_grad_deep(
        cot_blocks, w_section, count
    )
    before, following = edges(head, tail)
    attn_received, before, following, expand, contract = join(
        attn_received, before, following, expand_weight, contract_weight
    )

    resid_one, unit_two, scale_two, normed_two = second_norm(
        attn_parts[0], attn_received, [raw[0], species_row], gain_two, shift_two
    )
    normed_two, before, following, expand, contract = join(
        normed_two, before, following, expand, contract
    )
    w_ffn = gather_dp(jnp.concatenate([expand, contract.T], axis=1))
    normed_blocks = spread_blocks(normed_two)
    grad_mix, grad_coarse, even, odd, bias_grad = section_grad_mix(
        grad_deep, before, following, depth_taps, w_up
    )
    grad_resid_two = direct_sums(core_pairs(even, odd), LOW)
    normed_blocks, grad_resid_two, enc = join(normed_blocks, grad_resid_two, encoder[0])

    grad_ffn = spread_blocks(grad_resid_two.astype(LOW))
    contract_part, normed_two_all, hidden_low, slope = feed_forward_up(where, normed_blocks, w_ffn)
    enc_chips = chips_of(enc)
    grad_ffn, contract_part, enc_chips = join(grad_ffn, contract_part, enc_chips)

    contract_sum = scatter_tensor(contract_part)
    enc_blocks = both_cores(*enc_chips)
    ffn_parts, (grad_ffn_all, grad_hidden_pre) = feed_forward_back(grad_ffn, slope, w_ffn)
    ffn_received = collect_blocks(ffn_parts[1:])
    ffn_grads = feed_forward_weights(
        where, normed_two_all, grad_ffn_all, hidden_low, grad_hidden_pre, 1
    )[0][0]
    enc_pairs = core_pairs(*section_grad_encoder(grad_mix, w_lateral))
    coarse_chips = chips_of((resid_one + contract_sum.astype(jnp.float32)).astype(LOW))
    ffn_received, ffn_grads, enc_pairs, enc_blocks, coarse_chips = join(
        ffn_received, ffn_grads, enc_pairs, enc_blocks, coarse_chips
    )

    grad_resid_one, grad_attn, sums_two = second_norm_back(
        ffn_parts[0], ffn_received, unit_two, scale_two, gain_two, grad_resid_two
    )
    grad_attn, ffn_grads, coarse_chips = join(grad_attn, ffn_grads, coarse_chips)
    grad_attn_blocks = spread_blocks(grad_attn)
    ffn_out = scatter_dp(ffn_grads).astype(jnp.float32)
    encoder_grad = chip_sums(enc_pairs, corner_sums(enc_pairs, LOW), LOW)
    coarse_blocks = both_cores(*coarse_chips)
    section_mix, head, tail = section_mixture(
        coarse_blocks, enc_blocks, w_up, w_lateral, bias_section
    )
    before, following = edges(head, tail)
    grad_attn_blocks, encoder_grad, before, following = join(
        grad_attn_blocks, encoder_grad, before, following
    )

    head_parts, (grad_attn_all, grad_heads, grad_normed_part, bias_sums, rel_grad) = (
        attention_backward(
            where, grad_attn_blocks, saved, rel_turned, basis_turned, local_heads
        )
    )
    head_parts, before, following = join(head_parts, before, following)
    head_received = collect_blocks(head_parts[1:])
    deep_rows, out_even, out_odd, taps_grad = section_deep(
        section_mix, before, following, depth_taps, w_point, grad_deep
    )
    cols_part = section_weights(
        deep_rows, grad_coarse, grad_mix, cot_blocks, coarse_blocks, enc_blocks, count
    )
    even, odd, small_even, small_odd = attention_weights(
        where,
        saved,
        grad_attn_all,
        grad_heads,
        grad_normed_part,
        gain_one,
        sums_two,
        bias_sums,
        rel_grad,
        len(attn_blocks),
    )
    head_received, ffn_out, out_even, out_odd, even, odd, small_even, small_odd, cols_part = join(
        head_received, ffn_out, out_even, out_odd, even, odd, small_even, small_odd, cols_part
    )

    section_cols = scatter_tensor(cols_part)[0].astype(jnp.float32)
    grad_resid_in = first_norm_back(
        where, head_parts[0], head_received, saved[2], saved[3], gain_one, grad_resid_one
    )
    section_out = scatter_halves(out_even, out_odd).astype(LOW)
    attn_out = scatter_halves(even, odd)
    small_out = scatter_halves(small_even, small_odd, small=True)

    n_norm = 4 + SPECIES
    group = share * count
    group_cols = jnp.concatenate([small_out[:n_norm, :group], taps_grad, bias_grad], axis=0)
    norm_out = group_cols
    for k in range(1, count):
        norm_out = norm_out + from_ahead(group_cols, k)
    norm_out = lax.dynamic_slice_in_dim(norm_out, lax.axis_index("tensor") * share, share, 1)
    part = KEYD // lax.axis_size("dp")
    heads_out = small_out[8 : 10 + BASIS, :keys].reshape(2 + BASIS, local_heads, KEYD)[:, :, :part]
    heads_out = jnp.transpose(heads_out, (2, 0, 1))
    return (
        section_out[None],
        grad_resid_in,
        encoder_grad[None],
        norm_out[0:2],
        norm_out[2:4],
        norm_out[4:n_norm],
        attn_out[:, :keys],
        attn_out[:, keys : 2 * keys],
        attn_out[:, 2 * keys : 2 * keys + values],
        attn_out[:, 2 * keys + values :].T,
        ffn_out[:, :hidden_count],
        ffn_out[:, hidden_count:].T,
        heads_out[:, 2:],
        heads_out[:, 0],
        heads_out[:, 1],
        section_cols[share : 2 * share].T,
        section_cols[2 * share :].T,
        norm_out[n_norm : n_norm + 3],
        norm_out[n_norm + 3],
        section_cols[:share],
    )


def solution(mesh):
    rows = P("dp", "tensor", None)
    narrow = P(None, ("dp", "tensor"))
    split = P("dp", "tensor")
    turned = P("tensor", "dp")
    vector = P(("dp", "tensor"))
    tall = P(("dp", "tensor"), None)
    position = P("dp", None, "tensor")
    weights = (split, split, split, turned, split, turned, position, split, split)
    return jax.shard_map(
        body_direct if mesh.shape["dp"] == 8 else body_plain,
        mesh=mesh,
        in_specs=(rows, rows, P("dp"), rows, narrow, narrow, narrow)
        + weights
        + (narrow, narrow, narrow, vector, tall),
        out_specs=(rows, rows, rows, narrow, narrow, narrow)
        + weights
        + (narrow, narrow, narrow, vector, tall),
        check_vma=False,
    )
```

```python
import math

import jax
import jax.numpy as jnp
from jax import lax
from jax.experimental import pallas as pl
from jax.experimental.pallas import tpu as pltpu
from jax.sharding import PartitionSpec as P

KEYD = 64
VALD = 192
BASIS = 32
SPECIES = 2
SCALE = 1.0 / math.sqrt(KEYD)
LOW = jnp.bfloat16


def dot_plain(left_side, right_side):
    return jnp.dot(left_side, right_side, preferred_element_type=jnp.float32)


def dot_transposed(left_side, right_side):
    return lax.dot_general(
        left_side, right_side, (((1,), (1,)), ((), ())), preferred_element_type=jnp.float32
    )


def dot_leading(left_side, right_side):
    return lax.dot_general(
        left_side, right_side, (((0,), (0,)), ((), ())), preferred_element_type=jnp.float32
    )


def exact_gelu(values):
    return jax.nn.gelu(values, approximate=False)


def normalize(values):
    centred = values - jnp.mean(values, axis=-1, keepdims=True)
    variance = jnp.mean(centred * centred, axis=-1, keepdims=True)
    scale = lax.rsqrt(variance + 1e-05)
    return centred * scale, scale


def normalize_back(unit, scale, grad_unit):
    return scale * (
        grad_unit
        - jnp.mean(grad_unit, axis=-1, keepdims=True)
        - unit * jnp.mean(grad_unit * unit, axis=-1, keepdims=True)
    )


def basis_table(length, features):
    distance = jnp.arange(2 * length - 1).astype(jnp.float32) - (length - 1)
    halves = features // 2
    fraction = jnp.arange(halves).astype(jnp.float32) / (halves - 1)
    lifetimes = 3.0 * jnp.power(length / 3.0, fraction)
    decays = jnp.exp(-0.6931471805599453 * jnp.abs(distance)[:, None] / lifetimes[None, :])
    return jnp.concatenate([decays, jnp.sign(distance)[:, None] * decays], axis=1)


def dot_rows(left_side, right_side):
    return jnp.dot(left_side, right_side, preferred_element_type=jnp.float32)


def run_kernel(kernel, ins, outs, scalars=None, scratch=(), far=(), far_outs=()):
    whole = pl.BlockSpec(memory_space=pltpu.VMEM)
    outside = pl.BlockSpec(memory_space=pl.ANY)
    specs = [outside] * len(far) + [whole] * len(ins)
    args = list(far) + list(ins)
    if scalars is not None:
        specs = [pl.BlockSpec(memory_space=pltpu.SMEM)] + specs
        args = [scalars] + args
    shapes = [jax.ShapeDtypeStruct(shape, dtype) for shape, dtype in list(outs) + list(far_outs)]
    return pl.pallas_call(
        kernel,
        in_specs=specs,
        out_specs=[whole] * len(outs) + [outside] * len(far_outs),
        out_shape=shapes,
        scratch_shapes=scratch,
        compiler_params=pltpu.CompilerParams(vmem_limit_bytes=53 * 1024 * 1024),
        name=kernel.__qualname__.split(".")[0],
    )(*args)


def start_copies(pairs, sems, first=0):
    copies = [
        pltpu.make_async_copy(source, target, sems.at[first + n])
        for n, (source, target) in enumerate(pairs)
    ]
    for copy in copies:
        copy.start()
    return copies


def wait_copies(copies):
    for copy in copies:
        copy.wait()


def halves(windows, shape, dtype):
    return [(shape, dtype)] * windows


def place(m, windows):
    return m // 2 + m % 2 * (windows // 2)


def lanes_of(head, width, shape):
    lane = lax.broadcasted_iota(jnp.int32, shape, len(shape) - 1)
    return (lane >= head * width) & (lane < (head + 1) * width)


def chunk_of(where_ref, step, count):
    return lax.rem(where_ref[1] + step, count)


def attention_forward(where, raw, row_params, rel_turned, blocks, local_heads, own):
    count, width = len(raw), raw[0].shape[1]
    length = count * own
    n_blocks, columns = len(blocks), blocks[0].shape[1]
    rows = width // n_blocks
    keys, values = local_heads * KEYD, local_heads * VALD

    def kernel(where_ref, *refs):
        raw_refs, refs = refs[:count], refs[count:]
        species_ref, gain_ref, shift_ref, content_ref, position_ref, rel_ref = refs[:6]
        block_refs, refs = refs[6 : 6 + n_blocks], refs[6 + n_blocks :]
        own_ref, refs = refs[0], refs[1:]
        part_refs, refs = refs[: count - 1], refs[count - 1 :]
        (weight_ref, normed_ref, unit_ref, scale_ref, probs_ref, content_out, position_out) = refs[:7]
        key_out, value_out, mixed_out, total_ref = refs[7:]
        for m in range(n_blocks):
            spot = (where_ref[0] ^ m) * rows if n_blocks > 1 else 0
            weight_ref[pl.ds(pl.multiple_of(spot, rows), rows), :] = block_refs[m][:rows, :]
        for k in range(count):
            resid = raw_refs[k][:own, :].astype(jnp.float32) + species_ref[...]
            unit, scale = normalize(resid)
            spot = pl.ds(pl.multiple_of(chunk_of(where_ref, k, count) * own, own), own)
            unit_ref[spot, :] = unit
            scale_ref[spot, :] = jnp.broadcast_to(scale, (own, 128))
            normed_ref[spot, :] = (unit * gain_ref[...] + shift_ref[...]).astype(LOW)
        normed = normed_ref[...]
        query = dot_rows(normed, weight_ref[:, :keys])
        content = (query + content_ref[...]).astype(LOW)
        position = (query + position_ref[...]).astype(LOW)
        key_low = dot_rows(normed, weight_ref[:, keys : 2 * keys]).astype(LOW)
        value_low = dot_rows(normed, weight_ref[:, 2 * keys : 2 * keys + values]).astype(LOW)
        content_out[...] = content
        position_out[...] = position
        key_out[...] = key_low
        value_out[...] = value_low
        mixed = jnp.zeros((length, values), jnp.float32)
        for h in range(local_heads):
            mine = lanes_of(h, KEYD, (length, keys))
            zero = jnp.zeros((), LOW)
            banded = dot_transposed(jnp.where(mine, position, zero), rel_ref[...])
            skewed = pltpu.roll(banded, length + 1, 1, stride=1, stride_axis=0)[:, :length]
            scores = (dot_transposed(jnp.where(mine, content, zero), key_low) + skewed) * SCALE
            exponent = jnp.exp(scores - jnp.max(scores, axis=-1, keepdims=True))
            probs = exponent / jnp.sum(exponent, axis=-1, keepdims=True)
            probs_ref[h] = probs
            mixed = jnp.where(
                lanes_of(h, VALD, (length, values)), dot_rows(probs.astype(LOW), value_low), mixed
            )
        mixed_out[...] = mixed.astype(LOW)
        total_ref[...] = dot_transposed(mixed.astype(LOW), weight_ref[:, 2 * keys + values :])
        for k in range(count):
            spot = pl.ds(pl.multiple_of(chunk_of(where_ref, k, count) * own, own), own)
            if k == 0:
                own_ref[...] = total_ref[spot, :]
            else:
                part_refs[k - 1][...] = total_ref[spot, :].astype(LOW)

    outs = (
        [((own, width), jnp.float32)]
        + [((own, width), LOW)] * (count - 1)
        + [
            ((width, columns), LOW),
            ((length, width), LOW),
            ((length, width), jnp.float32),
            ((length, 128), jnp.float32),
            ((local_heads, length, length), jnp.float32),
            ((length, keys), LOW),
            ((length, keys), LOW),
            ((length, keys), LOW),
            ((length, values), LOW),
            ((length, values), LOW),
        ]
    )
    found = run_kernel(
        kernel,
        list(raw) + list(row_params) + [rel_turned] + list(blocks),
        outs,
        scalars=where,
        scratch=[pltpu.VMEM((length, width), jnp.float32)],
    )
    return found[:count], found[count:]


def attention_backward(
    where, grads, saved, rel_turned, basis_turned, gain, sums_two, local_heads, own
):
    count, width = len(grads), grads[0].shape[1]
    length = count * own
    weight, _, unit_all, scale_all, probs_all, content_all, position_all, key_all, value_all, _ = saved
    keys, values = local_heads * KEYD, local_heads * VALD
    narrow = 2 * keys + values

    def kernel(where_ref, *refs):
        grad_refs, refs = refs[:count], refs[count:]
        weight_ref, probs_ref, content_ref, position_ref, key_ref, value_ref = refs[:6]
        rel_ref, basis_ref, unit_ref, scale_ref, gain_ref, two_ref = refs[6:12]
        own_ref, refs = refs[12], refs[13:]
        part_refs, refs = refs[: count - 1], refs[count - 1 :]
        attn_ref, heads_ref, bias_ref, weight_out, sums_ref, total_ref = refs
        for k in range(count):
            spot = pl.ds(pl.multiple_of(chunk_of(where_ref, k, count) * own, own), own)
            attn_ref[spot, :] = grad_refs[k][:own, :]
        grad_mixed = dot_rows(attn_ref[...], weight_ref[:, narrow:]).astype(LOW)
        content, position = content_ref[...], position_ref[...]
        key_low, value_low = key_ref[...], value_ref[...]
        grad_content = jnp.zeros((length, keys), jnp.float32)
        grad_position = jnp.zeros((length, keys), jnp.float32)
        grad_key = jnp.zeros((length, keys), jnp.float32)
        grad_rel = jnp.zeros((2 * length, keys), jnp.float32)
        grad_value = jnp.zeros((length, values), jnp.float32)
        row = lax.broadcasted_iota(jnp.int32, (length, length), 0)
        column = lax.broadcasted_iota(jnp.int32, (length, length), 1)
        reverse = (row + column == length - 1).astype(jnp.float32).astype(LOW)
        position_reversed = dot_rows(reverse, position).astype(LOW)
        for h in range(local_heads):
            mine = lanes_of(h, KEYD, (length, keys))
            ours = lanes_of(h, VALD, (length, values))
            probs = probs_ref[h]
            grad_probs = dot_transposed(
                jnp.where(ours, grad_mixed, jnp.zeros((), LOW)), value_low
            )
            centre = jnp.sum(probs * grad_probs, axis=-1, keepdims=True)
            grad_scores = (probs * (grad_probs - centre)).astype(LOW)
            grad_value = jnp.where(ours, dot_leading(probs.astype(LOW), grad_mixed), grad_value)
            grad_key = jnp.where(mine, dot_leading(grad_scores, content), grad_key)
            grad_content = jnp.where(mine, dot_rows(grad_scores, key_low), grad_content)
            band = dot_rows(reverse, grad_scores)
            band = jnp.concatenate([band, jnp.zeros((length, length), jnp.float32)], axis=1)
            band = pltpu.roll(band, 0, 1, stride=1, stride_axis=0).astype(LOW)
            turned = dot_rows(band, rel_ref[...])
            high = turned.astype(LOW)
            low = (turned - high.astype(jnp.float32)).astype(LOW)
            turned = dot_rows(reverse, high) + dot_rows(reverse, low)
            grad_position = jnp.where(mine, turned, grad_position)
            grad_rel = jnp.where(
                lanes_of(h, KEYD, (2 * length, keys)),
                dot_leading(band, position_reversed),
                grad_rel,
            )
        grad_content = grad_content * SCALE
        grad_position = grad_position * SCALE
        bias_ref[0:1, :] = jnp.sum(grad_content, axis=0, keepdims=True)
        bias_ref[1:2, :] = jnp.sum(grad_position, axis=0, keepdims=True)
        heads_ref[:, :keys] = (grad_content + grad_position).astype(LOW)
        heads_ref[:, keys : 2 * keys] = (grad_key * SCALE).astype(LOW)
        heads_ref[:, 2 * keys :] = grad_value.astype(LOW)
        weight_out[...] = dot_leading(basis_ref[...], (grad_rel * SCALE).astype(LOW))
        grad = dot_transposed(heads_ref[...], weight_ref[:, :narrow])
        total_ref[...] = grad
        unit = unit_ref[...]
        into = normalize_back(unit, scale_ref[:, :1], grad * gain_ref[...])
        table = jnp.sum(into, axis=0, keepdims=True) + two_ref[2:3, :]
        sums_ref[...] = jnp.zeros_like(sums_ref)
        sums_ref[0:1, :] = jnp.sum(grad * unit, axis=0, keepdims=True)
        sums_ref[1:2, :] = two_ref[0:1, :]
        sums_ref[2:3, :] = jnp.sum(grad, axis=0, keepdims=True)
        sums_ref[3:4, :] = two_ref[1:2, :]
        for kind in range(SPECIES):
            sums_ref[4 + kind : 5 + kind, :] = jnp.where(where_ref[2] == kind, table, 0.0)
        for k in range(count):
            spot = pl.ds(pl.multiple_of(chunk_of(where_ref, k, count) * own, own), own)
            if k == 0:
                own_ref[...] = total_ref[spot, :]
            else:
                part_refs[k - 1][:own, :] = total_ref[spot, :].astype(LOW)
                part_refs[k - 1][own:, :] = sums_ref[...].astype(LOW)

    outs = (
        [((own, width), jnp.float32)]
        + [((own + 16, width), LOW)] * (count - 1)
        + [
            ((length, width), LOW),
            ((length, narrow), LOW),
            ((2, keys), jnp.float32),
            ((BASIS, keys), jnp.float32),
            ((16, width), jnp.float32),
        ]
    )
    found = run_kernel(
        kernel,
        list(grads)
        + [weight, probs_all, content_all, position_all, key_all, value_all]
        + [rel_turned, basis_turned, unit_all, scale_all, gain, sums_two],
        outs,
        scalars=where,
        scratch=[pltpu.VMEM((length, width), jnp.float32)],
    )
    return found[:count], found[count:]


def attention_weights(
    where, saved, grad_attn, grad_heads, own_sums, received, bias_sums, rel_grad, n_blocks
):
    normed, mixed = saved[1], saved[9]
    width = normed.shape[1]
    rows = width // n_blocks
    narrow, values = grad_heads.shape[1], mixed.shape[1]
    columns = narrow + values
    keys = rel_grad.shape[1]
    count = len(received) + 1

    def kernel(where_ref, normed_ref, mixed_ref, attn_ref, heads_ref, own_ref, *refs):
        received_refs, refs = refs[: count - 1], refs[count - 1 :]
        bias_ref, rel_ref, half_refs, whole_ref = refs[0], refs[1], refs[2:-1], refs[-1]
        sums = own_ref[...]
        for ref in received_refs:
            sums = sums + ref[ref.shape[0] - 16 :, :].astype(jnp.float32)
        sums = sums[:8]
        whole_ref[:, :narrow] = dot_leading(normed_ref[...], heads_ref[...]).astype(LOW)
        whole_ref[:, narrow:] = dot_leading(attn_ref[...], mixed_ref[...]).astype(LOW)
        for m in range(n_blocks):
            spot = (where_ref[0] ^ m) if n_blocks > 1 else 0
            half = half_refs[place(m, n_blocks)]
            half[:rows, :] = whole_ref[pl.ds(pl.multiple_of(spot * rows, rows), rows), :]
            if n_blocks == 1:
                continue
            moved = pltpu.roll(sums, lax.rem(width - spot * rows, width), 1)[:, :256]
            turn = lax.rem(keys - spot * (KEYD // n_blocks), keys)
            rel = pltpu.roll(rel_ref[...], turn, 1)
            bias = pltpu.roll(bias_ref[...], turn, 1)
            bias = jnp.concatenate([bias, jnp.zeros((6, keys), jnp.float32)], axis=0)
            bias = jnp.concatenate([bias, jnp.zeros((8, 256 - keys), jnp.float32)], axis=1)
            half[rows:, :256] = jnp.concatenate([moved, bias], axis=0).astype(LOW)
            half[rows:, 256 : 256 + keys] = rel[:16].astype(LOW)
            half[rows:, 256 + keys : 256 + 2 * keys] = rel[16:].astype(LOW)
            half[rows:, 256 + 2 * keys :] = jnp.zeros((16, columns - 256 - 2 * keys), LOW)

    return run_kernel(
        kernel,
        [normed, mixed, grad_attn, grad_heads, own_sums] + list(received) + [bias_sums, rel_grad],
        halves(n_blocks, (rows + (16 if n_blocks > 1 else 0), columns), LOW),
        scalars=where,
        scratch=[pltpu.VMEM((width, columns), LOW)],
    )


def unpack_small(where, found, basis_turned, width, local_heads, count):
    total = found.shape[0]
    n_blocks = total // count
    share = width // total
    n_rows = 8 + SPECIES
    group = width // n_blocks
    keys = local_heads * KEYD
    piece = keys // n_blocks
    part = KEYD // n_blocks
    length = basis_turned.shape[0]

    def kernel(where_ref, *refs):
        found_ref, basis_ref, refs = refs[0], refs[1], refs[2:]
        row_refs, refs = refs[:5], refs[5:]
        taps_ref, bias_ref, rel_ref, content_ref, position_ref, weight_ref = refs

        def owner(shape):
            spot = lax.broadcasted_iota(jnp.int32, shape, 0)
            return spot // count, lax.rem(spot % count + where_ref[1], count)

        def widen(start, size, span):
            column = lax.broadcasted_iota(jnp.int32, (size, span), 1)
            inner = lax.broadcasted_iota(jnp.int32, (size, span), 0)
            if size == share:
                chosen = column % share == inner
            else:
                chosen = (column // KEYD == inner // part) & (column % part == inner % part)
            return dot_rows(
                found_ref[:, start : start + size],
                chosen.astype(jnp.float32).astype(LOW),
            )

        group_of, line_of = owner((total, width))
        column = lax.broadcasted_iota(jnp.int32, (total, width), 1) // share
        mask = group_of * count + line_of == column
        rows = [
            jnp.sum(jnp.where(mask, widen(r * share, share, width), 0.0), axis=0, keepdims=True)
            for r in range(4 + SPECIES)
        ]
        species = jnp.zeros((1, width), jnp.float32)
        for kind in range(SPECIES):
            species = jnp.where(where_ref[2] == kind, rows[4 + kind], species)
        for ref, row in zip(row_refs, rows[:4] + [species], strict=True):
            ref[...] = row
        group_of, line_of = owner((total, group))
        column = lax.broadcasted_iota(jnp.int32, (total, group), 1) // share
        mask = (group_of == where_ref[0]) & (line_of == column)
        rows = [
            jnp.sum(jnp.where(mask, widen(r * share, share, group), 0.0), axis=0, keepdims=True)
            for r in range(4 + SPECIES, n_rows)
        ]
        for r in range(3):
            taps_ref[r : r + 1, :] = rows[r]
        bias_ref[...] = rows[3]
        group_of, line_of = owner((total, keys))
        column = lax.broadcasted_iota(jnp.int32, (total, keys), 1) % KEYD // part
        mask = (line_of == where_ref[1]) & (group_of == column)
        start = n_rows * share
        for f in range(BASIS + 2):
            row = widen(start + f * piece, piece, keys)
            row = jnp.sum(jnp.where(mask, row, 0.0), axis=0, keepdims=True)
            if f < BASIS:
                weight_ref[f : f + 1, :] = row
            else:
                (content_ref if f == BASIS else position_ref)[...] = row
        rel_ref[...] = dot_rows(basis_ref[...], weight_ref[...].astype(LOW)).astype(LOW)

    found = run_kernel(
        kernel,
        [found, basis_turned],
        [((1, width), jnp.float32)] * 5
        + [((3, group), jnp.float32), ((1, group), jnp.float32)]
        + [((length, keys), LOW)]
        + [((1, keys), jnp.float32)] * 2,
        scalars=where,
        scratch=[pltpu.VMEM((BASIS, keys), jnp.float32)],
    )
    return found[:5], found[5:]


def second_norm(own_part, parts, resid_in, gain, shift):
    own, width = own_part.shape

    def kernel(own_ref, *refs):
        part_refs, refs = refs[: len(parts)], refs[len(parts) :]
        raw_ref, species_ref, gain_ref, shift_ref, resid_ref, unit_ref, scale_ref, low_ref = refs
        total = own_ref[...]
        for ref in part_refs:
            total = total + ref[...].astype(jnp.float32)
        resid = raw_ref[...].astype(jnp.float32) + species_ref[...] + total
        unit, scale = normalize(resid)
        resid_ref[...] = resid
        unit_ref[...] = unit
        scale_ref[...] = jnp.broadcast_to(scale, (own, 128))
        low_ref[...] = (unit * gain_ref[...] + shift_ref[...]).astype(LOW)

    return run_kernel(
        kernel,
        [own_part] + list(parts) + list(resid_in) + [gain, shift],
        [
            ((own, width), jnp.float32),
            ((own, width), jnp.float32),
            ((own, 128), jnp.float32),
            ((own, width), LOW),
        ],
    )


def second_norm_back(own_part, parts, unit, scale, gain, grad_resid):
    own, width = own_part.shape

    def kernel(own_ref, *refs):
        part_refs, refs = refs[: len(parts)], refs[len(parts) :]
        unit_ref, scale_ref, gain_ref, grad_ref, resid_ref, low_ref, sums_ref = refs
        total = own_ref[...]
        for ref in part_refs:
            total = total + ref[...].astype(jnp.float32)
        unit_rows = unit_ref[...]
        resid = grad_ref[...] + normalize_back(unit_rows, scale_ref[:, :1], total * gain_ref[...])
        resid_ref[...] = resid
        low_ref[...] = resid.astype(LOW)
        sums_ref[0:1, :] = jnp.sum(total * unit_rows, axis=0, keepdims=True)
        sums_ref[1:2, :] = jnp.sum(total, axis=0, keepdims=True)
        sums_ref[2:3, :] = jnp.sum(resid, axis=0, keepdims=True)

    return run_kernel(
        kernel,
        [own_part] + list(parts) + [unit, scale, gain, grad_resid],
        [((own, width), jnp.float32), ((own, width), LOW), ((3, width), jnp.float32)],
    )


def first_norm_back(where, own_part, parts, unit_all, scale_all, gain, grad_resid):
    own, width = own_part.shape

    def kernel(where_ref, own_ref, *refs):
        part_refs, refs = refs[: len(parts)], refs[len(parts) :]
        unit_ref, scale_ref, gain_ref, grad_ref, out_ref = refs
        total = own_ref[...]
        for ref in part_refs:
            total = total + ref[:own, :].astype(jnp.float32)
        spot = pl.ds(pl.multiple_of(where_ref[1] * own, own), own)
        out_ref[0] = grad_ref[...] + normalize_back(
            unit_ref[spot, :], scale_ref[spot, :1], total * gain_ref[...]
        )

    return run_kernel(
        kernel,
        [own_part] + list(parts) + [unit_all, scale_all, gain, grad_resid],
        [((1, own, width), jnp.float32)],
        scalars=where,
    )[0]


def feed_forward_up(where, normed, weight):
    count, (own, width) = len(normed), normed[0].shape
    length = count * own
    hidden_count = weight.shape[1] // 2

    def kernel(where_ref, *refs):
        normed_refs, (weight_ref, part_ref, normed_out, hidden_out, slope_out) = refs[:count], refs[count:]
        for k in range(count):
            normed_out[k * own : (k + 1) * own, :] = normed_refs[k][...]
        pre = dot_rows(normed_out[...], weight_ref[:, :hidden_count])
        below = 0.5 * (1.0 + lax.erf(pre * math.sqrt(0.5)))
        hidden_out[...] = (pre * below).astype(LOW)
        slope_out[...] = below + pre * jnp.exp(-0.5 * pre * pre) * (1.0 / math.sqrt(2.0 * math.pi))
        total = dot_transposed(hidden_out[...], weight_ref[:, hidden_count:])
        for k in range(count):
            spot = pl.ds(pl.multiple_of(chunk_of(where_ref, k, count) * own, own), own)
            part_ref[spot, :] = total[k * own : (k + 1) * own].astype(LOW)

    return run_kernel(
        kernel,
        list(normed) + [weight],
        [((length, width), LOW)] * 2
        + [((length, hidden_count), LOW), ((length, hidden_count), jnp.float32)],
        scalars=where,
    )


def feed_forward_back(grads, slope, weight):
    count, (own, width) = len(grads), grads[0].shape
    length = count * own
    hidden_count = weight.shape[1] // 2

    def kernel(*refs):
        grad_refs, (slope_ref, weight_ref, own_ref), refs = refs[:count], refs[count : count + 3], refs[count + 3 :]
        part_refs, (grad_out, pre_out) = refs[: count - 1], refs[count - 1 :]
        for k in range(count):
            grad_out[k * own : (k + 1) * own, :] = grad_refs[k][...]
        grad_hidden = dot_rows(grad_out[...], weight_ref[:, hidden_count:])
        pre_out[...] = (grad_hidden * slope_ref[...]).astype(LOW)
        total = dot_transposed(pre_out[...], weight_ref[:, :hidden_count])
        own_ref[...] = total[:own]
        for k in range(1, count):
            part_refs[k - 1][...] = total[k * own : (k + 1) * own].astype(LOW)

    found = run_kernel(
        kernel,
        list(grads) + [slope, weight],
        [((own, width), jnp.float32)]
        + [((own, width), LOW)] * (count - 1)
        + [((length, width), LOW), ((length, hidden_count), LOW)],
    )
    return found[:count], found[count:]


def feed_forward_weights(where, normed_all, grad_all, hidden, grad_pre, n_blocks):
    width = normed_all.shape[1]
    hidden_count = hidden.shape[1]
    rows = width // n_blocks

    def kernel(where_ref, normed_ref, grad_ref, hidden_ref, pre_ref, *refs):
        half_refs, whole_ref = refs[:-1], refs[-1]
        whole_ref[:, :hidden_count] = dot_leading(normed_ref[...], pre_ref[...]).astype(LOW)
        whole_ref[:, hidden_count:] = dot_leading(grad_ref[...], hidden_ref[...]).astype(LOW)
        for m in range(n_blocks):
            spot = (where_ref[0] ^ m) * rows if n_blocks > 1 else 0
            half_refs[place(m, n_blocks)][...] = whole_ref[
                pl.ds(pl.multiple_of(spot, rows), rows), :
            ]

    return run_kernel(
        kernel,
        [normed_all, grad_all, hidden, grad_pre],
        halves(n_blocks, (rows, 2 * hidden_count), LOW),
        scalars=where,
        scratch=[pltpu.VMEM((width, 2 * hidden_count), LOW)],
    )


def shifted(rows, first, last):
    count = rows.shape[0]
    place = lax.broadcasted_iota(jnp.int32, rows.shape, 0)
    before = jnp.where(place == 0, first, pltpu.roll(rows, 1, 0))
    after = jnp.where(place == count - 1, last, pltpu.roll(rows, count - 1, 0))
    return before, after


def section_gradient(where, blocks, weight, taps, count):
    width = blocks[0].shape[1]
    fine = blocks[0].shape[0] - 16
    own = fine // 2
    channels = weight.shape[0] // 3
    share = channels // count
    windows = len(blocks)
    rows = windows * fine

    def kernel(where_ref, *refs):
        block_refs, weight_ref, taps_ref, refs = (
            refs[:windows], refs[windows], refs[windows + 1], refs[windows + 2 :]
        )
        deep_ref, mix_ref, coarse_ref, bias_ref, refs = *refs[:4], refs[4:]
        half_refs, whole_refs, (rows_ref, sems) = refs[:windows], refs[windows:-2], refs[-2:]
        copies = start_copies(
            [
                (block_refs[m].at[:fine, :], rows_ref.at[m * fine : (m + 1) * fine, :])
                for m in range(windows)
            ]
            + [
                (block_refs[m].at[fine:, :], rows_ref.at[pl.ds(rows + 16 * m, 16), :])
                for m in range(windows)
            ],
            sems,
        )
        for which, ref in enumerate(whole_refs):
            for t in range(count):
                spot = (3 * t + which) * share
                ref[t * share : (t + 1) * share, :] = weight_ref[spot : spot + share, :]
        row = lax.broadcasted_iota(jnp.int32, (own, fine), 0)
        column = lax.broadcasted_iota(jnp.int32, (own, fine), 1)
        pool = (column // 2 == row).astype(jnp.float32).astype(LOW)
        bias = jnp.zeros((1, channels), jnp.float32)
        wait_copies(copies)
        deep = dot_transposed(rows_ref[...], whole_refs[0][...]).astype(LOW)
        deep_ref[...] = deep[:rows]
        for m in range(windows):
            edge = deep[rows + 16 * m : rows + 16 * (m + 1)].astype(jnp.float32)
            own_rows = deep[m * fine : (m + 1) * fine].astype(jnp.float32)
            previous, following = shifted(
                own_rows,
                jnp.where(where_ref[1] > 0, edge[0:1], 0.0),
                jnp.where(where_ref[1] < count - 1, edge[1:2], 0.0),
            )
            mix = (
                taps_ref[0:1, :] * following
                + taps_ref[1:2, :] * own_rows
                + taps_ref[2:3, :] * previous
            ).astype(LOW)
            mix_ref[m * fine : (m + 1) * fine, :] = mix
            bias = bias + jnp.sum(mix.astype(jnp.float32), axis=0, keepdims=True)
            coarse_ref[m * own : (m + 1) * own, :] = dot_rows(pool, mix).astype(LOW)
        bias_ref[...] = bias
        part = dot_rows(coarse_ref[...], whole_refs[1][...]).astype(LOW)
        for m in range(windows):
            half_refs[place(m, windows)][...] = part[m * own : (m + 1) * own]

    return run_kernel(
        kernel,
        [weight, taps],
        [((rows, channels), LOW)] * 2
        + [((windows * own, channels), LOW)]
        + [((1, channels), jnp.float32)]
        + halves(windows, (own, width), LOW)
        + [((channels, width), LOW)] * 3,
        scalars=where,
        scratch=[
            pltpu.VMEM((rows + 16 * windows, width), LOW),
            pltpu.SemaphoreType.DMA((2 * windows,)),
        ],
        far=blocks,
    )


def section_grad_encoder(where, mix, lateral, windows):
    rows = mix.shape[0]
    fine = rows // windows
    width = lateral.shape[1]

    def kernel(where_ref, mix_ref, lateral_ref, out_ref):
        part = dot_rows(mix_ref[...], lateral_ref[...]).astype(LOW)
        for m in range(windows):
            spot = pl.ds(pl.multiple_of((where_ref[0] ^ m) * fine, fine), fine)
            out_ref[spot, :] = part[m * fine : (m + 1) * fine]

    return run_kernel(kernel, [mix, lateral], [((rows, width), LOW)], scalars=where)[0]


def section_forward(
    where, coarse_blocks, fine_blocks, up, lateral, point, bias, taps, grad_deep, count
):
    windows = len(fine_blocks)
    fine, (channels, width) = grad_deep.shape[0] // windows, up.shape
    own = fine // 2
    long, short = fine_blocks[0].shape[0], coarse_blocks[0].shape[0]

    def kernel(where_ref, *refs):
        coarse_refs, fine_refs, refs = refs[:windows], refs[windows : 2 * windows], refs[2 * windows :]
        up_ref, lateral_ref, point_ref, bias_ref, taps_ref, grad_ref = refs[:6]
        deep_ref, sums_ref, half_refs = refs[6], refs[7], refs[8:-3]
        short_ref, long_ref, sems = refs[-3:]
        copies = start_copies(
            [
                (coarse_refs[m], short_ref.at[m * short : (m + 1) * short, :])
                for m in range(windows)
            ]
            + [
                (fine_refs[m], long_ref.at[m * long : (m + 1) * long, :]) for m in range(windows)
            ],
            sems,
        )
        row = lax.broadcasted_iota(jnp.int32, (long, short), 0)
        column = lax.broadcasted_iota(jnp.int32, (long, short), 1)
        source = jnp.where(row < fine, row // 2, row - fine + own)
        repeat = (source == column).astype(jnp.float32).astype(LOW)
        wait_copies(copies[:windows])
        coarse = dot_transposed(short_ref[...], up_ref[...])
        high = coarse.astype(LOW)
        low = (coarse - high.astype(jnp.float32)).astype(LOW)
        wait_copies(copies[windows:])
        lateral_part = dot_transposed(long_ref[...], lateral_ref[...])
        sums = [jnp.zeros((1, channels), jnp.float32)] * 3
        for m in range(windows):
            spot = slice(m * short, (m + 1) * short)
            mix = (
                dot_rows(repeat, high[spot])
                + dot_rows(repeat, low[spot])
                + lateral_part[m * long : (m + 1) * long]
                + bias_ref[...]
            ).astype(LOW).astype(jnp.float32)
            rows = mix[:fine]
            previous, following = shifted(
                rows,
                jnp.where(where_ref[1] > 0, mix[fine : fine + 1], 0.0),
                jnp.where(where_ref[1] < count - 1, mix[fine + 1 : fine + 2], 0.0),
            )
            spot = slice(m * fine, (m + 1) * fine)
            deep_ref[spot, :] = (
                taps_ref[0:1, :] * previous + taps_ref[1:2, :] * rows + taps_ref[2:3, :] * following
            ).astype(LOW)
            grad = grad_ref[spot, :].astype(jnp.float32)
            sums = [
                total + jnp.sum(part * grad, axis=0, keepdims=True)
                for total, part in zip(sums, (previous, rows, following), strict=True)
            ]
        for s, total in enumerate(sums):
            sums_ref[s : s + 1, :] = total
        part = dot_rows(deep_ref[...], point_ref[...]).astype(LOW)
        for m in range(windows):
            half_refs[place(m, windows)][...] = part[m * fine : (m + 1) * fine]

    return run_kernel(
        kernel,
        [up, lateral, point, bias, taps, grad_deep],
        [((windows * fine, channels), LOW), ((3, channels), jnp.float32)]
        + halves(windows, (fine, width), LOW),
        scalars=where,
        scratch=[
            pltpu.VMEM((windows * short, width), LOW),
            pltpu.VMEM((windows * long, width), LOW),
            pltpu.SemaphoreType.DMA((2 * windows,)),
        ],
        far=list(coarse_blocks) + list(fine_blocks),
    )


def section_weights(deep, grad_coarse, grad_mix, cot_blocks, coarse_blocks, fine_blocks, sums, count):
    windows = len(cot_blocks)
    channels, width = deep.shape[1], cot_blocks[0].shape[1]
    fine, own = deep.shape[0] // windows, grad_coarse.shape[0] // windows
    share = channels // count

    def kernel(*refs):
        cot_refs, refs = refs[:windows], refs[windows:]
        row_refs, refs = refs[:windows], refs[windows:]
        fine_refs, refs = refs[:windows], refs[windows:]
        deep_ref, coarse_ref, mix_ref, sums_ref, out_ref = refs[:5]
        cot_all, row_all, fine_all, sems = refs[5:]
        groups = ((cot_refs, cot_all, fine), (row_refs, row_all, own), (fine_refs, fine_all, fine))
        copies = [
            start_copies(
                [
                    (blocks[m].at[:size, :], whole.at[m * size : (m + 1) * size, :])
                    for m in range(windows)
                ],
                sems,
                n * windows,
            )
            for n, (blocks, whole, size) in enumerate(groups)
        ]
        row = lax.broadcasted_iota(jnp.int32, (channels, 128), 0)
        column = lax.broadcasted_iota(jnp.int32, (channels, 128), 1)
        for t in range(count):
            chosen = ((row == column + t * share) & (column < share)).astype(jnp.float32)
            out_ref[t, 3 * share :, :128] = dot_rows(
                sums_ref[...].astype(LOW), chosen.astype(LOW)
            ).astype(LOW)
            out_ref[t, 3 * share :, 128:] = jnp.zeros((16, width - 128), LOW)
        lefts = (deep_ref, coarse_ref, mix_ref)
        for which, (left_ref, (_, whole, _)) in enumerate(zip(lefts, groups, strict=True)):
            wait_copies(copies[which])
            low = dot_leading(left_ref[...], whole[...]).astype(LOW)
            for t in range(count):
                out_ref[t, which * share : (which + 1) * share, :] = low[t * share : (t + 1) * share]

    return run_kernel(
        kernel,
        [deep, grad_coarse, grad_mix, sums],
        [((count, 3 * share + 16, width), LOW)],
        scratch=[
            pltpu.VMEM((windows * fine, width), LOW),
            pltpu.VMEM((windows * own, width), LOW),
            pltpu.VMEM((windows * fine, width), LOW),
            pltpu.SemaphoreType.DMA((3 * windows,)),
        ],
        far=list(cot_blocks) + list(coarse_blocks) + list(fine_blocks),
    )[0]


def from_ahead(rows, step):
    count = lax.axis_size("tensor")
    return lax.ppermute(rows, "tensor", [((i + step) % count, i) for i in range(count)])


def spread_blocks(rows):
    return [rows] + [from_ahead(rows, k) for k in range(1, lax.axis_size("tensor"))]


def collect_blocks(parts):
    count = lax.axis_size("tensor")
    return [from_ahead(parts[k - 1], count - k) for k in range(1, count)]


def to_own(rows):
    return jnp.roll(rows, -lax.axis_index("tensor") * (rows.shape[0] // lax.axis_size("tensor")), 0)


def dp_flip(cells, mask):
    count = lax.axis_size("dp")
    return lax.ppermute(cells, "dp", [(i, i ^ mask) for i in range(count)])


def half_rows(cells, axis=0):
    return cells.shape[axis] // 32 * 16


def both_cores(*chips):
    return [block for chip in chips for block in (chip, dp_flip(chip, 1))]


def chips_of(shard):
    return [shard] + [dp_flip(shard, mask) for mask in (2, 4, 6)]


def send_sum(cells, mask, dtype):
    return dp_flip(cells.astype(dtype), mask)


def core_pairs(blocks):
    chips = len(blocks) // 2
    return [
        mine.astype(jnp.float32) + dp_flip(theirs, 1).astype(jnp.float32)
        for mine, theirs in zip(blocks[:chips], blocks[chips:], strict=True)
    ]


def corner_sums(pairs, dtype):
    half = half_rows(pairs[3])
    return send_sum(pairs[3][:half], 2, dtype), send_sum(pairs[3][half:], 4, dtype)


def chip_sums(pairs, corners, dtype):
    half = half_rows(pairs[3])
    corners = [corner.astype(jnp.float32) for corner in corners]
    near = jnp.concatenate([pairs[1][:half], pairs[1][half:] + corners[1]], axis=0)
    far = jnp.concatenate([pairs[2][:half] + corners[0], pairs[2][half:]], axis=0)
    near, far = send_sum(near, 2, dtype), send_sum(far, 4, dtype)
    return pairs[0] + near.astype(jnp.float32) + far.astype(jnp.float32)


def direct_sums(pairs, dtype):
    return pairs[0] + sum(
        send_sum(pairs[chip], 2 * chip, dtype).astype(jnp.float32) for chip in (1, 2, 3)
    )


def gather_dp(shard):
    return lax.all_gather(shard, "dp", axis=0, tiled=True)


def scatter_dp(whole):
    return lax.psum_scatter(whole, "dp", scatter_dimension=0, tiled=True)


def scatter_tensor(whole):
    return lax.psum_scatter(whole, "tensor", scatter_dimension=0, tiled=True)


def gather_small(cells):
    line = jnp.stack(spread_blocks(cells), axis=0)
    return lax.all_gather(jnp.roll(line, lax.axis_index("tensor"), 0), "dp", axis=0)


def join(*arrays):
    return lax.optimization_barrier(arrays)


def edges(head, tail):
    ends = lax.axis_size("tensor") - 1
    return (
        lax.ppermute(tail, "tensor", [(i, i + 1) for i in range(ends)]),
        lax.ppermute(head, "tensor", [(i + 1, i) for i in range(ends)]),
    )


def halo(cells):
    count = lax.axis_size("tensor")
    ends = count - 1
    before = lax.ppermute(cells[:, -1:], "tensor", [(i, i + 1) for i in range(ends)])
    after = lax.ppermute(cells[:, :1], "tensor", [(i + 1, i) for i in range(ends)])
    return jnp.concatenate([before, cells, after], axis=1)


def body_plain(
    activations,
    encoder,
    species,
    cotangent,
    norm_gain,
    norm_shift,
    species_table,
    query_weight,
    key_weight,
    value_weight,
    output_weight,
    expand_weight,
    contract_weight,
    position_weight,
    content_bias,
    position_bias,
    upsample_weight,
    lateral_weight,
    depthwise_weight,
    section_bias,
    pointwise_weight,
):
    windows = lax.axis_size("dp")
    count = lax.axis_size("tensor")
    own = activations.shape[1]
    length = own * count
    width = activations.shape[2]
    local_heads = query_weight.shape[1] // KEYD
    keys = local_heads * KEYD
    values = local_heads * VALD

    raw = spread_blocks(activations[0])
    attn_shard = jnp.concatenate([query_weight, key_weight, value_weight, output_weight.T], axis=1)
    attn_blocks = [gather_dp(attn_shard)]
    where = jnp.stack([lax.axis_index("dp"), lax.axis_index("tensor"), species[0]])

    small = jnp.concatenate(
        [norm_gain, norm_shift, species_table, depthwise_weight, section_bias[None]], axis=0
    )
    n_small = small.size
    n_position = position_weight.size
    n_bias = content_bias.size
    packed = gather_small(
        jnp.concatenate(
            [
                small.reshape(-1),
                position_weight.reshape(-1),
                content_bias.reshape(-1),
                position_bias.reshape(-1),
            ]
        )
    )
    small_all = packed[:, :, :n_small].reshape(windows, count, 10, -1)
    norm_all = jnp.transpose(small_all[:, :, :6], (2, 0, 1, 3)).reshape(6, width)
    norm_all = norm_all.astype(jnp.float32)
    gain_vals, shift_vals, table_rows = norm_all[:2], norm_all[2:4], norm_all[4:]
    small_group = lax.dynamic_index_in_dim(small_all, lax.axis_index("dp"), 0, False)
    small_group = jnp.swapaxes(small_group, 0, 1).reshape(10, -1).astype(jnp.float32)
    channels = small_group.shape[1]
    depth_taps = small_group[6:9]
    bias_section = small_group[9]
    heads_all = lax.dynamic_index_in_dim(packed, lax.axis_index("tensor"), 1, False)[:, n_small:]
    w_position = heads_all[:, :n_position].reshape(KEYD, BASIS, local_heads)
    bias_content = heads_all[:, n_position : n_position + n_bias].reshape(KEYD, local_heads)
    bias_position = heads_all[:, n_position + n_bias :].reshape(KEYD, local_heads)

    section_shard = jnp.concatenate([pointwise_weight, upsample_weight.T, lateral_weight.T], axis=0)
    w_section = lax.all_gather(section_shard, "tensor", axis=0).reshape(count, 3, -1, width)
    w_point = w_section[:, 0].reshape(channels, width)
    w_up = w_section[:, 1].reshape(channels, width)
    w_lat = w_section[:, 2].reshape(channels, width)
    cot_all = gather_dp(cotangent[0])
    ffn_shard = jnp.concatenate([expand_weight, contract_weight.T], axis=1)
    w_ffn = lax.all_gather(ffn_shard, "dp", axis=0, tiled=True)
    hidden_count = expand_weight.shape[1]
    enc_all = gather_dp(encoder[0])

    fine = 2 * own
    grad_deep = dot_transposed(cot_all, w_point).astype(LOW)
    grad_wide = halo(grad_deep.reshape(windows, fine, channels)).astype(jnp.float32)
    grad_mix = (
        depth_taps[0] * grad_wide[:, 2:]
        + depth_taps[1] * grad_wide[:, 1:-1]
        + depth_taps[2] * grad_wide[:, :-2]
    ).astype(LOW)
    grad_coarse = jnp.sum(
        grad_mix.astype(jnp.float32).reshape(windows * own, 2, channels), axis=1
    ).astype(LOW)
    grad_resid_two = scatter_dp(dot_plain(grad_coarse, w_up).astype(LOW)).astype(jnp.float32)
    grad_ffn = spread_blocks(grad_resid_two.astype(LOW))

    species_mask = (jnp.arange(SPECIES, dtype=jnp.int32) == species[0]).astype(jnp.float32)
    species_row = jnp.sum(species_mask[:, None] * table_rows, axis=0)
    content_flat = bias_content.astype(jnp.float32).T.reshape(1, -1)
    position_flat = bias_position.astype(jnp.float32).T.reshape(1, -1)
    basis_turned = jnp.pad(basis_table(length, BASIS).astype(LOW)[::-1], ((0, 1), (0, 0)))
    rel_weight = jnp.transpose(w_position, (1, 2, 0)).reshape(BASIS, -1)
    rel_turned = dot_plain(basis_turned, rel_weight).astype(LOW)
    attn_parts, saved = attention_forward(
        where,
        raw,
        [species_row[None], gain_vals[:1], shift_vals[:1], content_flat, position_flat],
        rel_turned,
        attn_blocks,
        local_heads,
        own,
    )
    resid_one, unit_two, scale_two, normed_two = second_norm(
        attn_parts[0],
        collect_blocks(attn_parts[1:]),
        [raw[0], species_row[None]],
        gain_vals[1:],
        shift_vals[1:],
    )

    contract_part, normed_two_all, hidden_low, slope = feed_forward_up(
        where, spread_blocks(normed_two), w_ffn
    )
    ffn_parts, (grad_ffn_all, grad_hidden_pre) = feed_forward_back(grad_ffn, slope, w_ffn)
    grad_resid_one, grad_attn, sums_two = second_norm_back(
        ffn_parts[0],
        collect_blocks(ffn_parts[1:]),
        unit_two,
        scale_two,
        gain_vals[1:],
        grad_resid_two,
    )

    resid_two = resid_one + scatter_tensor(contract_part).astype(jnp.float32)
    section_all = gather_dp(resid_two.astype(LOW))
    coarse = dot_transposed(section_all, w_up).reshape(windows, own, channels)
    section_mix = (
        jnp.repeat(coarse, 2, axis=1)
        + dot_transposed(enc_all, w_lat).reshape(windows, fine, channels)
        + bias_section
    ).astype(LOW)
    mix_wide = halo(section_mix).astype(jnp.float32)
    deep_rows = (
        depth_taps[0] * mix_wide[:, :-2]
        + depth_taps[1] * mix_wide[:, 1:-1]
        + depth_taps[2] * mix_wide[:, 2:]
    ).astype(LOW)
    deep_rows = deep_rows.reshape(windows * fine, channels)
    section_out = scatter_dp(dot_plain(deep_rows, w_point).astype(LOW)).astype(LOW)
    grad_mix_rows = grad_mix.reshape(windows * fine, channels)
    encoder_grad = scatter_dp(dot_plain(grad_mix_rows, w_lat).astype(LOW)).astype(jnp.float32)
    grad_centre = grad_wide[:, 1:-1]
    grad_section_small = jnp.stack(
        [jnp.sum(mix_wide[:, s : s + fine] * grad_centre, axis=(0, 1)) for s in range(3)]
        + [jnp.sum(grad_mix.astype(jnp.float32), axis=(0, 1))],
        axis=1,
    )
    section_cols = jnp.stack(
        [
            dot_leading(deep_rows, cot_all).astype(LOW).reshape(count, -1, width),
            dot_leading(grad_coarse, section_all).astype(LOW).reshape(count, -1, width),
            dot_leading(grad_mix_rows, enc_all).astype(LOW).reshape(count, -1, width),
        ],
        axis=1,
    )
    section_cols = scatter_tensor(section_cols)[0].astype(jnp.float32)

    ffn_out = scatter_dp(
        feed_forward_weights(
            where, normed_two_all, grad_ffn_all, hidden_low, grad_hidden_pre, 1
        )[0]
    ).astype(jnp.float32)

    head_parts, (grad_attn_all, grad_heads, bias_sums, rel_grad, own_sums) = attention_backward(
        where,
        spread_blocks(grad_attn),
        saved,
        rel_turned,
        basis_turned,
        gain_vals[:1],
        sums_two,
        local_heads,
        own,
    )
    head_received = collect_blocks(head_parts[1:])
    grad_resid_in = first_norm_back(
        where, head_parts[0], head_received, saved[2], saved[3], gain_vals[:1], grad_resid_one
    )
    weights = attention_weights(
        where, saved, grad_attn_all, grad_heads, own_sums, head_received, bias_sums, rel_grad, 1
    )[0]
    attn_out = scatter_dp(weights).astype(jnp.float32)
    norm_sums = own_sums[:6]
    for block in head_received:
        norm_sums = norm_sums + block[own : own + 6].astype(jnp.float32)
    norm_cols = jnp.swapaxes(norm_sums.reshape(6, windows, channels), 0, 1)
    head_cols = jnp.concatenate([bias_sums, rel_grad], axis=0)
    head_cols = jnp.transpose(head_cols.reshape(2 + BASIS, local_heads, KEYD), (2, 0, 1))
    heads_cols = jnp.concatenate(
        [
            head_cols[:, 2:].reshape(windows, -1),
            head_cols[:, 0].reshape(windows, -1),
            head_cols[:, 1].reshape(windows, -1),
        ],
        axis=1,
    )
    small_out = scatter_dp(jnp.concatenate([norm_cols.reshape(windows, -1), heads_cols], axis=1))
    small_out = small_out[0]
    n_norm = 6 * channels
    section_sums = grad_section_small.T
    for k in range(1, count):
        section_sums = section_sums + from_ahead(grad_section_small.T, k)
    norm_out = jnp.concatenate([small_out[:n_norm].reshape(6, channels), section_sums])
    share = channels // count
    norm_out = lax.dynamic_slice_in_dim(norm_out, lax.axis_index("tensor") * share, share, 1)
    heads_out = small_out[n_norm:]
    return (
        section_out[None],
        grad_resid_in,
        encoder_grad[None],
        norm_out[0:2],
        norm_out[2:4],
        norm_out[4:6],
        attn_out[:, :keys],
        attn_out[:, keys : 2 * keys],
        attn_out[:, 2 * keys : 2 * keys + values],
        attn_out[:, 2 * keys + values :].T,
        ffn_out[:, :hidden_count],
        ffn_out[:, hidden_count:].T,
        heads_out[:n_position].reshape(position_weight.shape),
        heads_out[n_position : n_position + n_bias].reshape(content_bias.shape),
        heads_out[n_position + n_bias :].reshape(position_bias.shape),
        section_cols[1].T,
        section_cols[2].T,
        norm_out[6:9],
        norm_out[9],
        section_cols[0],
    )


def body_direct(
    activations,
    encoder,
    species,
    cotangent,
    norm_gain,
    norm_shift,
    species_table,
    query_weight,
    key_weight,
    value_weight,
    output_weight,
    expand_weight,
    contract_weight,
    position_weight,
    content_bias,
    position_bias,
    upsample_weight,
    lateral_weight,
    depthwise_weight,
    section_bias,
    pointwise_weight,
):
    count = lax.axis_size("tensor")
    own, width = activations.shape[1:]
    length = own * count
    local_heads = query_weight.shape[1] // KEYD
    keys = local_heads * KEYD
    values = local_heads * VALD
    hidden_count = expand_weight.shape[1]
    share = section_bias.shape[0]
    where = jnp.stack([lax.axis_index("dp"), lax.axis_index("tensor"), species[0]])

    packed = jnp.concatenate(
        [
            norm_gain.reshape(-1),
            norm_shift.reshape(-1),
            species_table.reshape(-1),
            depthwise_weight.reshape(-1),
            section_bias,
            jnp.transpose(position_weight, (1, 2, 0)).reshape(-1),
            content_bias.T.reshape(-1),
            position_bias.T.reshape(-1),
        ]
    )
    entries = packed.shape[0]
    packed = jnp.pad(packed[None], ((0, 0), (0, width - entries)))
    ends = [cotangent[0, :1], cotangent[0, -1:], encoder[0, :1], encoder[0, -1:]]
    packed = jnp.concatenate([packed] + ends + [jnp.zeros((3, width), LOW)], axis=0)
    raw = spread_blocks(jnp.concatenate([activations[0], packed], axis=0))
    attn_shard = jnp.concatenate([query_weight, key_weight, value_weight, output_weight.T], axis=1)
    attn_rows = attn_shard.shape[0]
    attn_chips = chips_of(attn_shard)
    w_ffn = gather_dp(jnp.concatenate([expand_weight, contract_weight.T], axis=1))
    raw, attn_chips, cot, section_shard = join(
        raw, attn_chips, cotangent[0], [pointwise_weight, upsample_weight.T, lateral_weight.T]
    )
    section_shard = jnp.concatenate(section_shard, axis=0)
    w_section = lax.all_gather(section_shard, "tensor", axis=0, tiled=True)
    blank = jnp.zeros((14, width), LOW)
    cot = [cot, raw[-1][own + 2 : own + 3], raw[1][own + 1 : own + 2], blank]
    cot = jnp.concatenate(cot, axis=0)
    enc = [encoder[0], raw[-1][own + 4 : own + 5], raw[1][own + 3 : own + 4], blank]
    enc = jnp.concatenate(enc, axis=0)
    line = jnp.concatenate([block[own : own + 1, :entries] for block in raw], axis=0)
    small_rows = gather_dp(line)
    attn_blocks = both_cores(*attn_chips)
    small_rows, attn_blocks, cot = join(small_rows, attn_blocks, cot)
    cot_chips = chips_of(cot)
    basis_turned = jnp.pad(basis_table(length, BASIS).astype(LOW)[::-1], ((0, 1), (0, 0)))
    rows, (depth_taps, bias_section, rel_turned, content_flat, position_flat) = unpack_small(
        where, small_rows, basis_turned, width, local_heads, count
    )
    gain_one, gain_two, shift_one, shift_two, species_row = rows
    attn_parts, saved = attention_forward(
        where,
        raw,
        [species_row, gain_one, shift_one, content_flat, position_flat],
        rel_turned,
        attn_blocks,
        local_heads,
        own,
    )
    attn_parts, cot_chips = join(attn_parts, cot_chips)

    attn_received = collect_blocks(attn_parts[1:])
    cot_blocks = both_cores(*cot_chips)
    grad_deep, grad_mix, grad_coarse, bias_grad, *halves_two, w_point, w_up, w_lateral = (
        section_gradient(where, cot_blocks, w_section, depth_taps, count)
    )
    attn_received, halves_two = join(attn_received, halves_two)

    resid_one, unit_two, scale_two, normed_two = second_norm(
        attn_parts[0], attn_received, [activations[0], species_row], gain_two, shift_two
    )
    normed_two, halves_two = join(normed_two, halves_two)
    normed_blocks = spread_blocks(normed_two)
    grad_resid_two = direct_sums(core_pairs(halves_two), LOW)
    normed_blocks, grad_resid_two, enc = join(normed_blocks, grad_resid_two, enc)

    grad_ffn = spread_blocks(grad_resid_two.astype(LOW))
    contract_part, normed_two_all, hidden_low, slope = feed_forward_up(where, normed_blocks, w_ffn)
    enc_chips = chips_of(enc)
    grad_ffn, contract_part, enc_chips, late_mix = join(
        grad_ffn, contract_part, enc_chips, grad_mix
    )

    contract_sum = scatter_tensor(contract_part)
    encoder_part = section_grad_encoder(where, late_mix, w_lateral, lax.axis_size("dp"))
    enc_blocks = both_cores(*enc_chips)
    ffn_parts, (grad_ffn_all, grad_hidden_pre) = feed_forward_back(grad_ffn, slope, w_ffn)
    ffn_received = collect_blocks(ffn_parts[1:])
    ffn_halves = feed_forward_weights(
        where, normed_two_all, grad_ffn_all, hidden_low, grad_hidden_pre, len(attn_blocks)
    )
    ffn_received, ffn_halves, enc_blocks, encoder_part = join(
        ffn_received, ffn_halves, enc_blocks, encoder_part
    )
    encoder_grad = scatter_dp(encoder_part).astype(jnp.float32)

    grad_resid_one, grad_attn, sums_two = second_norm_back(
        ffn_parts[0], ffn_received, unit_two, scale_two, gain_two, grad_resid_two
    )
    coarse = (resid_one + contract_sum.astype(jnp.float32)).astype(LOW)
    grad_attn = [grad_attn, coarse[:1], coarse[-1:], jnp.zeros((6, width), LOW)]
    grad_attn, ffn_halves = join(jnp.concatenate(grad_attn, axis=0), ffn_halves)
    grad_attn_blocks = spread_blocks(grad_attn)
    ffn_pairs = core_pairs(ffn_halves)
    grad_attn_blocks, ffn_pairs = join(grad_attn_blocks, ffn_pairs)

    coarse = [coarse, grad_attn_blocks[-1][own + 1 : own + 2], grad_attn_blocks[1][own : own + 1]]
    coarse_chips = chips_of(jnp.concatenate(coarse + [blank], axis=0))
    ffn_corners = corner_sums(ffn_pairs, LOW)
    head_parts, (grad_attn_all, grad_heads, bias_sums, rel_grad, own_sums) = attention_backward(
        where,
        grad_attn_blocks,
        saved,
        rel_turned,
        basis_turned,
        gain_one,
        sums_two,
        local_heads,
        own,
    )
    head_parts, ffn_corners = join(head_parts, ffn_corners)
    head_received = collect_blocks(head_parts[1:])
    ffn_out = chip_sums(ffn_pairs, ffn_corners, LOW)
    coarse_blocks = both_cores(*coarse_chips)
    deep_rows, taps_grad, *out_halves = section_forward(
        where,
        coarse_blocks,
        enc_blocks,
        w_up,
        w_lateral,
        w_point,
        bias_section,
        depth_taps,
        grad_deep,
        count,
    )
    section_sums = jnp.pad(jnp.concatenate([taps_grad, bias_grad], axis=0), ((0, 12), (0, 0)))
    cols_part = section_weights(
        deep_rows,
        grad_coarse,
        grad_mix,
        cot_blocks,
        coarse_blocks,
        enc_blocks,
        section_sums,
        count,
    )
    section_cols = scatter_tensor(cols_part)[0].astype(jnp.float32)
    out_pairs = core_pairs(out_halves)
    head_received, out_pairs, ffn_out = join(head_received, out_pairs, ffn_out)

    grad_resid_in = first_norm_back(
        where, head_parts[0], head_received, saved[2], saved[3], gain_one, grad_resid_one
    )
    attn_halves = attention_weights(
        where,
        saved,
        grad_attn_all,
        grad_heads,
        own_sums,
        head_received,
        bias_sums,
        rel_grad,
        len(attn_blocks),
    )
    attn_pairs = core_pairs(attn_halves)
    out_corners = corner_sums(out_pairs, LOW)
    attn_pairs, out_corners, grad_resid_in, encoder_grad = join(
        attn_pairs, out_corners, grad_resid_in, encoder_grad
    )
    attn_out = direct_sums(attn_pairs, LOW)
    section_out = chip_sums(out_pairs, out_corners, LOW).astype(LOW)

    small_out, attn_out = attn_out[attn_rows:], attn_out[:attn_rows]
    norm_out = lax.dynamic_slice_in_dim(
        small_out[: 4 + SPECIES], lax.axis_index("tensor") * share, share, 1
    )
    part = KEYD // lax.axis_size("dp")

    def heads_of(rows):
        return rows.reshape(rows.shape[0], local_heads, KEYD)[:, :, :part]

    bias_out = jnp.transpose(heads_of(small_out[8:10, :keys]), (2, 0, 1))
    rel_out = [small_out[:, 256 : 256 + keys], small_out[:, 256 + keys : 256 + 2 * keys]]
    rel_out = jnp.transpose(heads_of(jnp.concatenate(rel_out, axis=0)), (2, 0, 1))
    return (
        section_out[None],
        grad_resid_in,
        encoder_grad[None],
        norm_out[0:2],
        norm_out[2:4],
        norm_out[4:],
        attn_out[:, :keys],
        attn_out[:, keys : 2 * keys],
        attn_out[:, 2 * keys : 2 * keys + values],
        attn_out[:, 2 * keys + values :].T,
        ffn_out[:, :hidden_count],
        ffn_out[:, hidden_count:].T,
        rel_out,
        bias_out[:, 0],
        bias_out[:, 1],
        section_cols[share : 2 * share].T,
        section_cols[2 * share : 3 * share].T,
        section_cols[3 * share : 3 * share + 3, :share],
        section_cols[3 * share + 3, :share],
        section_cols[:share],
    )


def solution(mesh):
    rows = P("dp", "tensor", None)
    narrow = P(None, ("dp", "tensor"))
    split = P("dp", "tensor")
    turned = P("tensor", "dp")
    vector = P(("dp", "tensor"))
    tall = P(("dp", "tensor"), None)
    position = P("dp", None, "tensor")
    weights = (split, split, split, turned, split, turned, position, split, split)
    return jax.shard_map(
        body_direct if mesh.shape["dp"] == 8 else body_plain,
        mesh=mesh,
        in_specs=(rows, rows, P("dp"), rows, narrow, narrow, narrow)
        + weights
        + (narrow, narrow, narrow, vector, tall),
        out_specs=(rows, rows, rows, narrow, narrow, narrow)
        + weights
        + (narrow, narrow, narrow, vector, tall),
        check_vma=False,
    )
```

```python
import math

import jax
import jax.numpy as jnp
from jax import lax
from jax.experimental import pallas as pl
from jax.experimental.pallas import tpu as pltpu
from jax.sharding import PartitionSpec as P

KEYD = 64
VALD = 192
BASIS = 32
SPECIES = 2
SCALE = 1.0 / math.sqrt(KEYD)
LOW = jnp.bfloat16


def dot_plain(left_side, right_side):
    return jnp.dot(left_side, right_side, preferred_element_type=jnp.float32)


def dot_transposed(left_side, right_side):
    return lax.dot_general(
        left_side, right_side, (((1,), (1,)), ((), ())), preferred_element_type=jnp.float32
    )


def dot_leading(left_side, right_side):
    return lax.dot_general(
        left_side, right_side, (((0,), (0,)), ((), ())), preferred_element_type=jnp.float32
    )


def exact_gelu(values):
    return jax.nn.gelu(values, approximate=False)


def normalize(values):
    centred = values - jnp.mean(values, axis=-1, keepdims=True)
    variance = jnp.mean(centred * centred, axis=-1, keepdims=True)
    scale = lax.rsqrt(variance + 1e-05)
    return centred * scale, scale


def normalize_back(unit, scale, grad_unit):
    return scale * (
        grad_unit
        - jnp.mean(grad_unit, axis=-1, keepdims=True)
        - unit * jnp.mean(grad_unit * unit, axis=-1, keepdims=True)
    )


def basis_table(length, features):
    distance = jnp.arange(2 * length - 1).astype(jnp.float32) - (length - 1)
    halves = features // 2
    fraction = jnp.arange(halves).astype(jnp.float32) / (halves - 1)
    lifetimes = 3.0 * jnp.power(length / 3.0, fraction)
    decays = jnp.exp(-0.6931471805599453 * jnp.abs(distance)[:, None] / lifetimes[None, :])
    return jnp.concatenate([decays, jnp.sign(distance)[:, None] * decays], axis=1)


def dot_rows(left_side, right_side):
    return jnp.dot(left_side, right_side, preferred_element_type=jnp.float32)


def run_kernel(kernel, ins, outs, scalars=None, scratch=(), far=(), far_outs=(), room=52):
    whole = pl.BlockSpec(memory_space=pltpu.VMEM)
    outside = pl.BlockSpec(memory_space=pl.ANY)
    specs = [outside] * len(far) + [whole] * len(ins)
    args = list(far) + list(ins)
    if scalars is not None:
        specs = [pl.BlockSpec(memory_space=pltpu.SMEM)] + specs
        args = [scalars] + args
    shapes = [jax.ShapeDtypeStruct(shape, dtype) for shape, dtype in list(outs) + list(far_outs)]
    return pl.pallas_call(
        kernel,
        in_specs=specs,
        out_specs=[whole] * len(outs) + [outside] * len(far_outs),
        out_shape=shapes,
        scratch_shapes=scratch,
        compiler_params=pltpu.CompilerParams(vmem_limit_bytes=room * 1024 * 1024),
        name=kernel.__qualname__.split(".")[0],
    )(*args)


def start_copies(pairs, sems, first=0):
    copies = [
        pltpu.make_async_copy(source, target, sems.at[first + n])
        for n, (source, target) in enumerate(pairs)
    ]
    for copy in copies:
        copy.start()
    return copies


def wait_copies(copies):
    for copy in copies:
        copy.wait()


def halves(windows, shape, dtype):
    return [(shape, dtype)] * windows


def place(m, windows):
    return m // 2 + m % 2 * (windows // 2)


def lanes_of(head, width, shape):
    lane = lax.broadcasted_iota(jnp.int32, shape, len(shape) - 1)
    return (lane >= head * width) & (lane < (head + 1) * width)


def chunk_of(where_ref, step, count):
    return lax.rem(where_ref[1] + step, count)


def attention_forward(where, raw, row_params, rel_turned, blocks, local_heads, own):
    count, width = len(raw), raw[0].shape[1]
    length = count * own
    n_blocks, columns = len(blocks), blocks[0].shape[1]
    rows = width // n_blocks
    keys, values = local_heads * KEYD, local_heads * VALD

    def kernel(where_ref, *refs):
        raw_refs, refs = refs[:count], refs[count:]
        species_ref, gain_ref, shift_ref, content_ref, position_ref, rel_ref = refs[:6]
        block_refs, refs = refs[6 : 6 + n_blocks], refs[6 + n_blocks :]
        own_ref, refs = refs[0], refs[1:]
        part_refs, refs = refs[: count - 1], refs[count - 1 :]
        (weight_ref, normed_ref, unit_ref, scale_ref, probs_ref, content_out, position_out) = refs[:7]
        key_out, value_out, mixed_out, total_ref = refs[7:]
        for m in range(n_blocks):
            spot = (where_ref[0] ^ m) * rows if n_blocks > 1 else 0
            weight_ref[pl.ds(pl.multiple_of(spot, rows), rows), :] = block_refs[m][:rows, :]
        for k in range(count):
            resid = raw_refs[k][:own, :].astype(jnp.float32) + species_ref[...]
            unit, scale = normalize(resid)
            spot = pl.ds(pl.multiple_of(chunk_of(where_ref, k, count) * own, own), own)
            unit_ref[spot, :] = unit
            scale_ref[spot, :] = jnp.broadcast_to(scale, (own, 128))
            normed_ref[spot, :] = (unit * gain_ref[...] + shift_ref[...]).astype(LOW)
        normed = normed_ref[...]
        query = dot_rows(normed, weight_ref[:, :keys])
        content = (query + content_ref[...]).astype(LOW)
        position = (query + position_ref[...]).astype(LOW)
        key_low = dot_rows(normed, weight_ref[:, keys : 2 * keys]).astype(LOW)
        value_low = dot_rows(normed, weight_ref[:, 2 * keys : 2 * keys + values]).astype(LOW)
        content_out[...] = content
        position_out[...] = position
        key_out[...] = key_low
        value_out[...] = value_low
        mixed = jnp.zeros((length, values), jnp.float32)
        for h in range(local_heads):
            mine = lanes_of(h, KEYD, (length, keys))
            zero = jnp.zeros((), LOW)
            banded = dot_transposed(jnp.where(mine, position, zero), rel_ref[...])
            skewed = pltpu.roll(banded, length + 1, 1, stride=1, stride_axis=0)[:, :length]
            scores = (dot_transposed(jnp.where(mine, content, zero), key_low) + skewed) * SCALE
            exponent = jnp.exp(scores - jnp.max(scores, axis=-1, keepdims=True))
            probs = exponent / jnp.sum(exponent, axis=-1, keepdims=True)
            probs_ref[h] = probs
            mixed = jnp.where(
                lanes_of(h, VALD, (length, values)), dot_rows(probs.astype(LOW), value_low), mixed
            )
        mixed_out[...] = mixed.astype(LOW)
        total_ref[...] = dot_transposed(mixed.astype(LOW), weight_ref[:, 2 * keys + values :])
        for k in range(count):
            spot = pl.ds(pl.multiple_of(chunk_of(where_ref, k, count) * own, own), own)
            if k == 0:
                own_ref[...] = total_ref[spot, :]
            else:
                part_refs[k - 1][...] = total_ref[spot, :].astype(LOW)

    outs = (
        [((own, width), jnp.float32)]
        + [((own, width), LOW)] * (count - 1)
        + [
            ((width, columns), LOW),
            ((length, width), LOW),
            ((length, width), jnp.float32),
            ((length, 128), jnp.float32),
            ((local_heads, length, length), jnp.float32),
            ((length, keys), LOW),
            ((length, keys), LOW),
            ((length, keys), LOW),
            ((length, values), LOW),
            ((length, values), LOW),
        ]
    )
    found = run_kernel(
        kernel,
        list(raw) + list(row_params) + [rel_turned] + list(blocks),
        outs,
        scalars=where,
        scratch=[pltpu.VMEM((length, width), jnp.float32)],
    )
    return found[:count], found[count:]


def attention_backward(
    where, grads, saved, rel_turned, basis_turned, gain, sums_two, local_heads, own
):
    count, width = len(grads), grads[0].shape[1]
    length = count * own
    weight, _, unit_all, scale_all, probs_all, content_all, position_all, key_all, value_all, _ = saved
    keys, values = local_heads * KEYD, local_heads * VALD
    narrow = 2 * keys + values

    def kernel(where_ref, *refs):
        grad_refs, refs = refs[:count], refs[count:]
        weight_ref, probs_ref, content_ref, position_ref, key_ref, value_ref = refs[:6]
        rel_ref, basis_ref, unit_ref, scale_ref, gain_ref, two_ref = refs[6:12]
        own_ref, refs = refs[12], refs[13:]
        part_refs, refs = refs[: count - 1], refs[count - 1 :]
        attn_ref, heads_ref, bias_ref, weight_out, sums_ref, total_ref = refs
        for k in range(count):
            spot = pl.ds(pl.multiple_of(chunk_of(where_ref, k, count) * own, own), own)
            attn_ref[spot, :] = grad_refs[k][:own, :]
        grad_mixed = dot_rows(attn_ref[...], weight_ref[:, narrow:]).astype(LOW)
        content, position = content_ref[...], position_ref[...]
        key_low, value_low = key_ref[...], value_ref[...]
        grad_content = jnp.zeros((length, keys), jnp.float32)
        grad_position = jnp.zeros((length, keys), jnp.float32)
        grad_key = jnp.zeros((length, keys), jnp.float32)
        grad_rel = jnp.zeros((2 * length, keys), jnp.float32)
        grad_value = jnp.zeros((length, values), jnp.float32)
        row = lax.broadcasted_iota(jnp.int32, (length, length), 0)
        column = lax.broadcasted_iota(jnp.int32, (length, length), 1)
        reverse = (row + column == length - 1).astype(jnp.float32).astype(LOW)
        position_reversed = dot_rows(reverse, position).astype(LOW)
        for h in range(local_heads):
            mine = lanes_of(h, KEYD, (length, keys))
            ours = lanes_of(h, VALD, (length, values))
            probs = probs_ref[h]
            grad_probs = dot_transposed(
                jnp.where(ours, grad_mixed, jnp.zeros((), LOW)), value_low
            )
            centre = jnp.sum(probs * grad_probs, axis=-1, keepdims=True)
            grad_scores = (probs * (grad_probs - centre)).astype(LOW)
            grad_value = jnp.where(ours, dot_leading(probs.astype(LOW), grad_mixed), grad_value)
            grad_key = jnp.where(mine, dot_leading(grad_scores, content), grad_key)
            grad_content = jnp.where(mine, dot_rows(grad_scores, key_low), grad_content)
            band = dot_rows(reverse, grad_scores)
            band = jnp.concatenate([band, jnp.zeros((length, length), jnp.float32)], axis=1)
            band = pltpu.roll(band, 0, 1, stride=1, stride_axis=0).astype(LOW)
            turned = dot_rows(band, rel_ref[...])
            high = turned.astype(LOW)
            low = (turned - high.astype(jnp.float32)).astype(LOW)
            turned = dot_rows(reverse, high) + dot_rows(reverse, low)
            grad_position = jnp.where(mine, turned, grad_position)
            grad_rel = jnp.where(
                lanes_of(h, KEYD, (2 * length, keys)),
                dot_leading(band, position_reversed),
                grad_rel,
            )
        grad_content = grad_content * SCALE
        grad_position = grad_position * SCALE
        bias_ref[0:1, :] = jnp.sum(grad_content, axis=0, keepdims=True)
        bias_ref[1:2, :] = jnp.sum(grad_position, axis=0, keepdims=True)
        heads_ref[:, :keys] = (grad_content + grad_position).astype(LOW)
        heads_ref[:, keys : 2 * keys] = (grad_key * SCALE).astype(LOW)
        heads_ref[:, 2 * keys :] = grad_value.astype(LOW)
        weight_out[...] = dot_leading(basis_ref[...], (grad_rel * SCALE).astype(LOW))
        grad = dot_transposed(heads_ref[...], weight_ref[:, :narrow])
        total_ref[...] = grad
        unit = unit_ref[...]
        into = normalize_back(unit, scale_ref[:, :1], grad * gain_ref[...])
        table = jnp.sum(into, axis=0, keepdims=True) + two_ref[2:3, :]
        sums_ref[...] = jnp.zeros_like(sums_ref)
        sums_ref[0:1, :] = jnp.sum(grad * unit, axis=0, keepdims=True)
        sums_ref[1:2, :] = two_ref[0:1, :]
        sums_ref[2:3, :] = jnp.sum(grad, axis=0, keepdims=True)
        sums_ref[3:4, :] = two_ref[1:2, :]
        for kind in range(SPECIES):
            sums_ref[4 + kind : 5 + kind, :] = jnp.where(where_ref[2] == kind, table, 0.0)
        for k in range(count):
            spot = pl.ds(pl.multiple_of(chunk_of(where_ref, k, count) * own, own), own)
            if k == 0:
                own_ref[...] = total_ref[spot, :]
            else:
                part_refs[k - 1][:own, :] = total_ref[spot, :].astype(LOW)
                part_refs[k - 1][own:, :] = sums_ref[...].astype(LOW)

    outs = (
        [((own, width), jnp.float32)]
        + [((own + 16, width), LOW)] * (count - 1)
        + [
            ((length, width), LOW),
            ((length, narrow), LOW),
            ((2, keys), jnp.float32),
            ((BASIS, keys), jnp.float32),
            ((16, width), jnp.float32),
        ]
    )
    found = run_kernel(
        kernel,
        list(grads)
        + [weight, probs_all, content_all, position_all, key_all, value_all]
        + [rel_turned, basis_turned, unit_all, scale_all, gain, sums_two],
        outs,
        scalars=where,
        scratch=[pltpu.VMEM((length, width), jnp.float32)],
    )
    return found[:count], found[count:]


def attention_weights(
    where, saved, grad_attn, grad_heads, own_sums, received, bias_sums, rel_grad, n_blocks
):
    normed, mixed = saved[1], saved[9]
    width = normed.shape[1]
    rows = width // n_blocks
    narrow, values = grad_heads.shape[1], mixed.shape[1]
    columns = narrow + values
    keys = rel_grad.shape[1]
    count = len(received) + 1

    def kernel(where_ref, normed_ref, mixed_ref, attn_ref, heads_ref, own_ref, *refs):
        received_refs, refs = refs[: count - 1], refs[count - 1 :]
        bias_ref, rel_ref, half_refs, whole_ref = refs[0], refs[1], refs[2:-1], refs[-1]
        sums = own_ref[...]
        for ref in received_refs:
            sums = sums + ref[ref.shape[0] - 16 :, :].astype(jnp.float32)
        sums = sums[:8]
        whole_ref[:, :narrow] = dot_leading(normed_ref[...], heads_ref[...]).astype(LOW)
        whole_ref[:, narrow:] = dot_leading(attn_ref[...], mixed_ref[...]).astype(LOW)
        for m in range(n_blocks):
            spot = (where_ref[0] ^ m) if n_blocks > 1 else 0
            half = half_refs[place(m, n_blocks)]
            half[:rows, :] = whole_ref[pl.ds(pl.multiple_of(spot * rows, rows), rows), :]
            if n_blocks == 1:
                continue
            moved = pltpu.roll(sums, lax.rem(width - spot * rows, width), 1)[:, :256]
            turn = lax.rem(keys - spot * (KEYD // n_blocks), keys)
            rel = pltpu.roll(rel_ref[...], turn, 1)
            bias = pltpu.roll(bias_ref[...], turn, 1)
            bias = jnp.concatenate([bias, jnp.zeros((6, keys), jnp.float32)], axis=0)
            bias = jnp.concatenate([bias, jnp.zeros((8, 256 - keys), jnp.float32)], axis=1)
            half[rows:, :256] = jnp.concatenate([moved, bias], axis=0).astype(LOW)
            half[rows:, 256 : 256 + keys] = rel[:16].astype(LOW)
            half[rows:, 256 + keys : 256 + 2 * keys] = rel[16:].astype(LOW)
            half[rows:, 256 + 2 * keys :] = jnp.zeros((16, columns - 256 - 2 * keys), LOW)

    return run_kernel(
        kernel,
        [normed, mixed, grad_attn, grad_heads, own_sums] + list(received) + [bias_sums, rel_grad],
        halves(n_blocks, (rows + (16 if n_blocks > 1 else 0), columns), LOW),
        scalars=where,
        scratch=[pltpu.VMEM((width, columns), LOW)],
    )


def pack_rows(rows, channel_rows, weights, biases, cotangent, encoder):
    own, width = rows.shape
    fine = cotangent.shape[0]
    part, heads, basis = weights.shape
    share = channel_rows[0].shape[1]
    n_rows = sum(block.shape[0] for block in channel_rows)
    first = n_rows * share

    def kernel(cot_ref, enc_ref, rows_ref, *refs):
        channel_refs, refs = refs[: len(channel_rows)], refs[len(channel_rows) :]
        weights_ref, content_ref, position_ref, out_ref, ends_ref, sems = refs
        copies = start_copies(
            [
                (cot_ref.at[:16, :], ends_ref.at[0:16, :]),
                (cot_ref.at[fine - 16 :, :], ends_ref.at[16:32, :]),
                (enc_ref.at[:16, :], ends_ref.at[32:48, :]),
                (enc_ref.at[fine - 16 :, :], ends_ref.at[48:64, :]),
            ],
            sems,
        )
        out_ref[:own, :] = rows_ref[...]

        def place_of(size, start):
            column = lax.broadcasted_iota(jnp.int32, (size, width), 1) - start
            return column, lax.broadcasted_iota(jnp.int32, (size, width), 0)

        def widen(values, chosen, mine):
            found = dot_rows(values.astype(LOW), chosen.astype(jnp.float32).astype(LOW))
            return jnp.sum(jnp.where(mine, found, 0.0), axis=0, keepdims=True)

        def in_order(values, start):
            height, size = values.shape
            column, index = place_of(size, start)
            chosen = (column >= 0) & (column % size == index)
            column, index = place_of(height, start)
            return widen(values, chosen, (column >= 0) & (column // size == index))

        channel = jnp.concatenate([ref[...].astype(jnp.float32) for ref in channel_refs], axis=0)
        row = in_order(channel, 0)
        values = jnp.concatenate(
            [weights_ref[k].astype(jnp.float32) for k in range(part)], axis=0
        )
        column, index = place_of(basis, first)
        chosen = (column >= 0) & (column // (heads * part) == index)
        column, index = place_of(part * heads, first)
        mine = (column % part == index // heads) & (column // part % heads == index % heads)
        mine = mine & (column >= 0) & (column < part * heads * basis)
        row = row + widen(values, chosen, mine)
        start = first + part * heads * basis
        for ref in (content_ref, position_ref):
            row = row + in_order(ref[...].astype(jnp.float32), start)
            start += part * heads
        wait_copies(copies)
        ends = ends_ref[...].astype(jnp.float32)
        tail = [row, ends[:1], ends[31:32], ends[32:33], ends[63:], jnp.zeros((3, width), jnp.float32)]
        out_ref[own:, :] = jnp.concatenate(tail, axis=0).astype(LOW)

    return run_kernel(
        kernel,
        [rows] + list(channel_rows) + [weights] + list(biases),
        [((own + 8, width), LOW)],
        scratch=[pltpu.VMEM((64, width), LOW), pltpu.SemaphoreType.DMA((4,))],
        far=[cotangent, encoder],
        room=62,
    )[0]


def pick_rows(blocks, own, entries):
    width = blocks[0].shape[1]

    def kernel(*refs):
        block_refs, (line_ref, cot_ref, enc_ref) = refs[: len(blocks)], refs[len(blocks) :]
        tails = [ref[own:, :].astype(jnp.float32) for ref in block_refs]
        blank = jnp.zeros((14, width), jnp.float32)
        line_ref[...] = jnp.concatenate([tail[:1, :entries] for tail in tails], axis=0).astype(LOW)
        cot_ref[...] = jnp.concatenate([tails[-1][2:3], tails[1][1:2], blank], axis=0).astype(LOW)
        enc_ref[...] = jnp.concatenate([tails[-1][4:5], tails[1][3:4], blank], axis=0).astype(LOW)

    return run_kernel(
        kernel,
        blocks,
        [((len(blocks), entries), LOW), ((16, width), LOW), ((16, width), LOW)],
        room=62,
    )


def unpack_small(where, found, basis_turned, width, local_heads, count):
    total = found.shape[0]
    n_blocks = total // count
    share = width // total
    n_rows = 8 + SPECIES
    group = width // n_blocks
    keys = local_heads * KEYD
    piece = keys // n_blocks
    part = KEYD // n_blocks
    length = basis_turned.shape[0]

    def kernel(where_ref, *refs):
        found_ref, basis_ref, refs = refs[0], refs[1], refs[2:]
        row_refs, refs = refs[:5], refs[5:]
        taps_ref, bias_ref, rel_ref, content_ref, position_ref, weight_ref = refs

        def owner(shape):
            spot = lax.broadcasted_iota(jnp.int32, shape, 0)
            return spot // count, lax.rem(spot % count + where_ref[1], count)

        def widen(start, size, span):
            column = lax.broadcasted_iota(jnp.int32, (size, span), 1)
            inner = lax.broadcasted_iota(jnp.int32, (size, span), 0)
            if size == share:
                chosen = column % share == inner
            else:
                chosen = (column // KEYD == inner // part) & (column % part == inner % part)
            return dot_rows(
                found_ref[:, start : start + size],
                chosen.astype(jnp.float32).astype(LOW),
            )

        group_of, line_of = owner((total, width))
        column = lax.broadcasted_iota(jnp.int32, (total, width), 1) // share
        mask = group_of * count + line_of == column
        rows = [
            jnp.sum(jnp.where(mask, widen(r * share, share, width), 0.0), axis=0, keepdims=True)
            for r in range(4 + SPECIES)
        ]
        species = jnp.zeros((1, width), jnp.float32)
        for kind in range(SPECIES):
            species = jnp.where(where_ref[2] == kind, rows[4 + kind], species)
        for ref, row in zip(row_refs, rows[:4] + [species], strict=True):
            ref[...] = row
        group_of, line_of = owner((total, group))
        column = lax.broadcasted_iota(jnp.int32, (total, group), 1) // share
        mask = (group_of == where_ref[0]) & (line_of == column)
        rows = [
            jnp.sum(jnp.where(mask, widen(r * share, share, group), 0.0), axis=0, keepdims=True)
            for r in range(4 + SPECIES, n_rows)
        ]
        for r in range(3):
            taps_ref[r : r + 1, :] = rows[r]
        bias_ref[...] = rows[3]
        group_of, line_of = owner((total, keys))
        column = lax.broadcasted_iota(jnp.int32, (total, keys), 1) % KEYD // part
        mask = (line_of == where_ref[1]) & (group_of == column)
        start = n_rows * share
        for f in range(BASIS + 2):
            row = widen(start + f * piece, piece, keys)
            row = jnp.sum(jnp.where(mask, row, 0.0), axis=0, keepdims=True)
            if f < BASIS:
                weight_ref[f : f + 1, :] = row
            else:
                (content_ref if f == BASIS else position_ref)[...] = row
        rel_ref[...] = dot_rows(basis_ref[...], weight_ref[...].astype(LOW)).astype(LOW)

    found = run_kernel(
        kernel,
        [found, basis_turned],
        [((1, width), jnp.float32)] * 5
        + [((3, group), jnp.float32), ((1, group), jnp.float32)]
        + [((length, keys), LOW)]
        + [((1, keys), jnp.float32)] * 2,
        scalars=where,
        scratch=[pltpu.VMEM((BASIS, keys), jnp.float32)],
    )
    return found[:5], found[5:]


def second_norm(own_part, parts, resid_in, gain, shift):
    own, width = own_part.shape

    def kernel(own_ref, *refs):
        part_refs, refs = refs[: len(parts)], refs[len(parts) :]
        raw_ref, species_ref, gain_ref, shift_ref, resid_ref, unit_ref, scale_ref, low_ref = refs
        total = own_ref[...]
        for ref in part_refs:
            total = total + ref[...].astype(jnp.float32)
        resid = raw_ref[...].astype(jnp.float32) + species_ref[...] + total
        unit, scale = normalize(resid)
        resid_ref[...] = resid
        unit_ref[...] = unit
        scale_ref[...] = jnp.broadcast_to(scale, (own, 128))
        low_ref[...] = (unit * gain_ref[...] + shift_ref[...]).astype(LOW)

    return run_kernel(
        kernel,
        [own_part] + list(parts) + list(resid_in) + [gain, shift],
        [
            ((own, width), jnp.float32),
            ((own, width), jnp.float32),
            ((own, 128), jnp.float32),
            ((own, width), LOW),
        ],
    )


def second_norm_back(own_part, parts, unit, scale, gain, grad_resid):
    own, width = own_part.shape

    def kernel(own_ref, *refs):
        part_refs, refs = refs[: len(parts)], refs[len(parts) :]
        unit_ref, scale_ref, gain_ref, grad_ref, resid_ref, low_ref, sums_ref = refs
        total = own_ref[...]
        for ref in part_refs:
            total = total + ref[...].astype(jnp.float32)
        unit_rows = unit_ref[...]
        resid = grad_ref[...] + normalize_back(unit_rows, scale_ref[:, :1], total * gain_ref[...])
        resid_ref[...] = resid
        low_ref[...] = resid.astype(LOW)
        sums_ref[0:1, :] = jnp.sum(total * unit_rows, axis=0, keepdims=True)
        sums_ref[1:2, :] = jnp.sum(total, axis=0, keepdims=True)
        sums_ref[2:3, :] = jnp.sum(resid, axis=0, keepdims=True)

    return run_kernel(
        kernel,
        [own_part] + list(parts) + [unit, scale, gain, grad_resid],
        [((own, width), jnp.float32), ((own, width), LOW), ((3, width), jnp.float32)],
    )


def first_norm_back(where, own_part, parts, unit_all, scale_all, gain, grad_resid):
    own, width = own_part.shape

    def kernel(where_ref, own_ref, *refs):
        part_refs, refs = refs[: len(parts)], refs[len(parts) :]
        unit_ref, scale_ref, gain_ref, grad_ref, out_ref = refs
        total = own_ref[...]
        for ref in part_refs:
            total = total + ref[:own, :].astype(jnp.float32)
        spot = pl.ds(pl.multiple_of(where_ref[1] * own, own), own)
        out_ref[0] = grad_ref[...] + normalize_back(
            unit_ref[spot, :], scale_ref[spot, :1], total * gain_ref[...]
        )

    return run_kernel(
        kernel,
        [own_part] + list(parts) + [unit_all, scale_all, gain, grad_resid],
        [((1, own, width), jnp.float32)],
        scalars=where,
    )[0]


def feed_forward_up(where, normed, weight):
    count, (own, width) = len(normed), normed[0].shape
    length = count * own
    hidden_count = weight.shape[1] // 2

    def kernel(where_ref, *refs):
        normed_refs, (weight_ref, part_ref, normed_out, hidden_out, slope_out) = refs[:count], refs[count:]
        for k in range(count):
            normed_out[k * own : (k + 1) * own, :] = normed_refs[k][...]
        pre = dot_rows(normed_out[...], weight_ref[:, :hidden_count])
        below = 0.5 * (1.0 + lax.erf(pre * math.sqrt(0.5)))
        hidden_out[...] = (pre * below).astype(LOW)
        slope_out[...] = below + pre * jnp.exp(-0.5 * pre * pre) * (1.0 / math.sqrt(2.0 * math.pi))
        total = dot_transposed(hidden_out[...], weight_ref[:, hidden_count:])
        for k in range(count):
            spot = pl.ds(pl.multiple_of(chunk_of(where_ref, k, count) * own, own), own)
            part_ref[spot, :] = total[k * own : (k + 1) * own].astype(LOW)

    return run_kernel(
        kernel,
        list(normed) + [weight],
        [((length, width), LOW)] * 2
        + [((length, hidden_count), LOW), ((length, hidden_count), jnp.float32)],
        scalars=where,
    )


def feed_forward_back(grads, slope, weight):
    count, (own, width) = len(grads), grads[0].shape
    length = count * own
    hidden_count = weight.shape[1] // 2

    def kernel(*refs):
        grad_refs, (slope_ref, weight_ref, own_ref), refs = refs[:count], refs[count : count + 3], refs[count + 3 :]
        part_refs, (grad_out, pre_out) = refs[: count - 1], refs[count - 1 :]
        for k in range(count):
            grad_out[k * own : (k + 1) * own, :] = grad_refs[k][...]
        grad_hidden = dot_rows(grad_out[...], weight_ref[:, hidden_count:])
        pre_out[...] = (grad_hidden * slope_ref[...]).astype(LOW)
        total = dot_transposed(pre_out[...], weight_ref[:, :hidden_count])
        own_ref[...] = total[:own]
        for k in range(1, count):
            part_refs[k - 1][...] = total[k * own : (k + 1) * own].astype(LOW)

    found = run_kernel(
        kernel,
        list(grads) + [slope, weight],
        [((own, width), jnp.float32)]
        + [((own, width), LOW)] * (count - 1)
        + [((length, width), LOW), ((length, hidden_count), LOW)],
    )
    return found[:count], found[count:]


def feed_forward_weights(where, normed_all, grad_all, hidden, grad_pre, n_blocks):
    width = normed_all.shape[1]
    hidden_count = hidden.shape[1]
    rows = width // n_blocks

    def kernel(where_ref, normed_ref, grad_ref, hidden_ref, pre_ref, *refs):
        half_refs, whole_ref = refs[:-1], refs[-1]
        whole_ref[:, :hidden_count] = dot_leading(normed_ref[...], pre_ref[...]).astype(LOW)
        whole_ref[:, hidden_count:] = dot_leading(grad_ref[...], hidden_ref[...]).astype(LOW)
        for m in range(n_blocks):
            spot = (where_ref[0] ^ m) * rows if n_blocks > 1 else 0
            half_refs[place(m, n_blocks)][...] = whole_ref[
                pl.ds(pl.multiple_of(spot, rows), rows), :
            ]

    return run_kernel(
        kernel,
        [normed_all, grad_all, hidden, grad_pre],
        halves(n_blocks, (rows, 2 * hidden_count), LOW),
        scalars=where,
        scratch=[pltpu.VMEM((width, 2 * hidden_count), LOW)],
    )


def shifted(rows, first, last):
    count = rows.shape[0]
    place = lax.broadcasted_iota(jnp.int32, rows.shape, 0)
    before = jnp.where(place == 0, first, pltpu.roll(rows, 1, 0))
    after = jnp.where(place == count - 1, last, pltpu.roll(rows, count - 1, 0))
    return before, after


def section_gradient(where, blocks, weight, taps, count):
    width = blocks[0].shape[1]
    fine = blocks[0].shape[0] - 16
    own = fine // 2
    channels = weight.shape[0] // 3
    share = channels // count
    windows = len(blocks)
    rows = windows * fine

    def kernel(where_ref, *refs):
        block_refs, weight_ref, taps_ref, refs = (
            refs[:windows], refs[windows], refs[windows + 1], refs[windows + 2 :]
        )
        deep_ref, mix_ref, coarse_ref, bias_ref, refs = *refs[:4], refs[4:]
        half_refs, whole_refs, (rows_ref, sems) = refs[:windows], refs[windows:-2], refs[-2:]
        copies = start_copies(
            [
                (block_refs[m].at[:fine, :], rows_ref.at[m * fine : (m + 1) * fine, :])
                for m in range(windows)
            ]
            + [
                (block_refs[m].at[fine:, :], rows_ref.at[pl.ds(rows + 16 * m, 16), :])
                for m in range(windows)
            ],
            sems,
        )
        for which, ref in enumerate(whole_refs):
            for t in range(count):
                spot = (3 * t + which) * share
                ref[t * share : (t + 1) * share, :] = weight_ref[spot : spot + share, :]
        row = lax.broadcasted_iota(jnp.int32, (own, fine), 0)
        column = lax.broadcasted_iota(jnp.int32, (own, fine), 1)
        pool = (column // 2 == row).astype(jnp.float32).astype(LOW)
        bias = jnp.zeros((1, channels), jnp.float32)
        wait_copies(copies)
        deep = dot_transposed(rows_ref[...], whole_refs[0][...]).astype(LOW)
        deep_ref[...] = deep[:rows]
        for m in range(windows):
            edge = deep[rows + 16 * m : rows + 16 * (m + 1)].astype(jnp.float32)
            own_rows = deep[m * fine : (m + 1) * fine].astype(jnp.float32)
            previous, following = shifted(
                own_rows,
                jnp.where(where_ref[1] > 0, edge[0:1], 0.0),
                jnp.where(where_ref[1] < count - 1, edge[1:2], 0.0),
            )
            mix = (
                taps_ref[0:1, :] * following
                + taps_ref[1:2, :] * own_rows
                + taps_ref[2:3, :] * previous
            ).astype(LOW)
            mix_ref[m * fine : (m + 1) * fine, :] = mix
            bias = bias + jnp.sum(mix.astype(jnp.float32), axis=0, keepdims=True)
            coarse_ref[m * own : (m + 1) * own, :] = dot_rows(pool, mix).astype(LOW)
        bias_ref[...] = bias
        part = dot_rows(coarse_ref[...], whole_refs[1][...]).astype(LOW)
        for m in range(windows):
            half_refs[place(m, windows)][...] = part[m * own : (m + 1) * own]

    return run_kernel(
        kernel,
        [weight, taps],
        [((rows, channels), LOW)] * 2
        + [((windows * own, channels), LOW)]
        + [((1, channels), jnp.float32)]
        + halves(windows, (own, width), LOW)
        + [((channels, width), LOW)] * 3,
        scalars=where,
        scratch=[
            pltpu.VMEM((rows + 16 * windows, width), LOW),
            pltpu.SemaphoreType.DMA((2 * windows,)),
        ],
        far=blocks,
    )


def section_grad_encoder(where, mix, lateral, windows):
    rows = mix.shape[0]
    fine = rows // windows
    width = lateral.shape[1]

    def kernel(where_ref, mix_ref, lateral_ref, out_ref):
        part = dot_rows(mix_ref[...], lateral_ref[...]).astype(LOW)
        for m in range(windows):
            spot = pl.ds(pl.multiple_of((where_ref[0] ^ m) * fine, fine), fine)
            out_ref[spot, :] = part[m * fine : (m + 1) * fine]

    return run_kernel(kernel, [mix, lateral], [((rows, width), LOW)], scalars=where)[0]


def section_forward(
    where, coarse_blocks, fine_blocks, up, lateral, point, bias, taps, grad_deep, count
):
    windows = len(fine_blocks)
    fine, (channels, width) = grad_deep.shape[0] // windows, up.shape
    own = fine // 2
    long, short = fine_blocks[0].shape[0], coarse_blocks[0].shape[0]

    def kernel(where_ref, *refs):
        coarse_refs, fine_refs, refs = refs[:windows], refs[windows : 2 * windows], refs[2 * windows :]
        up_ref, lateral_ref, point_ref, bias_ref, taps_ref, grad_ref = refs[:6]
        deep_ref, sums_ref, half_refs = refs[6], refs[7], refs[8:-3]
        short_ref, long_ref, sems = refs[-3:]
        copies = start_copies(
            [
                (coarse_refs[m], short_ref.at[m * short : (m + 1) * short, :])
                for m in range(windows)
            ]
            + [
                (fine_refs[m], long_ref.at[m * long : (m + 1) * long, :]) for m in range(windows)
            ],
            sems,
        )
        row = lax.broadcasted_iota(jnp.int32, (long, short), 0)
        column = lax.broadcasted_iota(jnp.int32, (long, short), 1)
        source = jnp.where(row < fine, row // 2, row - fine + own)
        repeat = (source == column).astype(jnp.float32).astype(LOW)
        wait_copies(copies[:windows])
        coarse = dot_transposed(short_ref[...], up_ref[...])
        high = coarse.astype(LOW)
        low = (coarse - high.astype(jnp.float32)).astype(LOW)
        wait_copies(copies[windows:])
        lateral_part = dot_transposed(long_ref[...], lateral_ref[...])
        sums = [jnp.zeros((1, channels), jnp.float32)] * 3
        for m in range(windows):
            spot = slice(m * short, (m + 1) * short)
            mix = (
                dot_rows(repeat, high[spot])
                + dot_rows(repeat, low[spot])
                + lateral_part[m * long : (m + 1) * long]
                + bias_ref[...]
            ).astype(LOW).astype(jnp.float32)
            rows = mix[:fine]
            previous, following = shifted(
                rows,
                jnp.where(where_ref[1] > 0, mix[fine : fine + 1], 0.0),
                jnp.where(where_ref[1] < count - 1, mix[fine + 1 : fine + 2], 0.0),
            )
            spot = slice(m * fine, (m + 1) * fine)
            deep_ref[spot, :] = (
                taps_ref[0:1, :] * previous + taps_ref[1:2, :] * rows + taps_ref[2:3, :] * following
            ).astype(LOW)
            grad = grad_ref[spot, :].astype(jnp.float32)
            sums = [
                total + jnp.sum(part * grad, axis=0, keepdims=True)
                for total, part in zip(sums, (previous, rows, following), strict=True)
            ]
        for s, total in enumerate(sums):
            sums_ref[s : s + 1, :] = total
        part = dot_rows(deep_ref[...], point_ref[...]).astype(LOW)
        for m in range(windows):
            half_refs[place(m, windows)][...] = part[m * fine : (m + 1) * fine]

    return run_kernel(
        kernel,
        [up, lateral, point, bias, taps, grad_deep],
        [((windows * fine, channels), LOW), ((3, channels), jnp.float32)]
        + halves(windows, (fine, width), LOW),
        scalars=where,
        scratch=[
            pltpu.VMEM((windows * short, width), LOW),
            pltpu.VMEM((windows * long, width), LOW),
            pltpu.SemaphoreType.DMA((2 * windows,)),
        ],
        far=list(coarse_blocks) + list(fine_blocks),
    )


def section_weights(deep, grad_coarse, grad_mix, cot_blocks, coarse_blocks, fine_blocks, sums, count):
    windows = len(cot_blocks)
    channels, width = deep.shape[1], cot_blocks[0].shape[1]
    fine, own = deep.shape[0] // windows, grad_coarse.shape[0] // windows
    share = channels // count

    def kernel(*refs):
        cot_refs, refs = refs[:windows], refs[windows:]
        row_refs, refs = refs[:windows], refs[windows:]
        fine_refs, refs = refs[:windows], refs[windows:]
        deep_ref, coarse_ref, mix_ref, sums_ref, out_ref = refs[:5]
        cot_all, row_all, fine_all, sems = refs[5:]
        groups = ((cot_refs, cot_all, fine), (row_refs, row_all, own), (fine_refs, fine_all, fine))
        copies = [
            start_copies(
                [
                    (blocks[m].at[:size, :], whole.at[m * size : (m + 1) * size, :])
                    for m in range(windows)
                ],
                sems,
                n * windows,
            )
            for n, (blocks, whole, size) in enumerate(groups)
        ]
        row = lax.broadcasted_iota(jnp.int32, (channels, 128), 0)
        column = lax.broadcasted_iota(jnp.int32, (channels, 128), 1)
        for t in range(count):
            chosen = ((row == column + t * share) & (column < share)).astype(jnp.float32)
            out_ref[t, 3 * share :, :128] = dot_rows(
                sums_ref[...].astype(LOW), chosen.astype(LOW)
            ).astype(LOW)
            out_ref[t, 3 * share :, 128:] = jnp.zeros((16, width - 128), LOW)
        lefts = (deep_ref, coarse_ref, mix_ref)
        for which, (left_ref, (_, whole, _)) in enumerate(zip(lefts, groups, strict=True)):
            wait_copies(copies[which])
            low = dot_leading(left_ref[...], whole[...]).astype(LOW)
            for t in range(count):
                out_ref[t, which * share : (which + 1) * share, :] = low[t * share : (t + 1) * share]

    return run_kernel(
        kernel,
        [deep, grad_coarse, grad_mix, sums],
        [((count, 3 * share + 16, width), LOW)],
        scratch=[
            pltpu.VMEM((windows * fine, width), LOW),
            pltpu.VMEM((windows * own, width), LOW),
            pltpu.VMEM((windows * fine, width), LOW),
            pltpu.SemaphoreType.DMA((3 * windows,)),
        ],
        far=list(cot_blocks) + list(coarse_blocks) + list(fine_blocks),
    )[0]


def from_ahead(rows, step):
    count = lax.axis_size("tensor")
    return lax.ppermute(rows, "tensor", [((i + step) % count, i) for i in range(count)])


def spread_blocks(rows):
    return [rows] + [from_ahead(rows, k) for k in range(1, lax.axis_size("tensor"))]


def collect_blocks(parts):
    count = lax.axis_size("tensor")
    return [from_ahead(parts[k - 1], count - k) for k in range(1, count)]


def to_own(rows):
    return jnp.roll(rows, -lax.axis_index("tensor") * (rows.shape[0] // lax.axis_size("tensor")), 0)


def dp_flip(cells, mask):
    count = lax.axis_size("dp")
    return lax.ppermute(cells, "dp", [(i, i ^ mask) for i in range(count)])


def half_rows(cells, axis=0):
    return cells.shape[axis] // 32 * 16


def both_cores(*chips):
    return [block for chip in chips for block in (chip, dp_flip(chip, 1))]


def chips_of(shard):
    return [shard] + [dp_flip(shard, mask) for mask in (2, 4, 6)]


def send_sum(cells, mask, dtype):
    return dp_flip(cells.astype(dtype), mask)


def core_pairs(blocks):
    chips = len(blocks) // 2
    return [
        mine.astype(jnp.float32) + dp_flip(theirs, 1).astype(jnp.float32)
        for mine, theirs in zip(blocks[:chips], blocks[chips:], strict=True)
    ]


def corner_sums(pairs, dtype):
    half = half_rows(pairs[3])
    return send_sum(pairs[3][:half], 2, dtype), send_sum(pairs[3][half:], 4, dtype)


def chip_sums(pairs, corners, dtype):
    half = half_rows(pairs[3])
    corners = [corner.astype(jnp.float32) for corner in corners]
    near = jnp.concatenate([pairs[1][:half], pairs[1][half:] + corners[1]], axis=0)
    far = jnp.concatenate([pairs[2][:half] + corners[0], pairs[2][half:]], axis=0)
    near, far = send_sum(near, 2, dtype), send_sum(far, 4, dtype)
    return pairs[0] + near.astype(jnp.float32) + far.astype(jnp.float32)


def direct_sums(pairs, dtype):
    return pairs[0] + sum(
        send_sum(pairs[chip], 2 * chip, dtype).astype(jnp.float32) for chip in (1, 2, 3)
    )


def gather_dp(shard):
    return lax.all_gather(shard, "dp", axis=0, tiled=True)


def scatter_dp(whole):
    return lax.psum_scatter(whole, "dp", scatter_dimension=0, tiled=True)


def scatter_tensor(whole):
    return lax.psum_scatter(whole, "tensor", scatter_dimension=0, tiled=True)


def gather_small(cells):
    line = jnp.stack(spread_blocks(cells), axis=0)
    return lax.all_gather(jnp.roll(line, lax.axis_index("tensor"), 0), "dp", axis=0)


def join(*arrays):
    return lax.optimization_barrier(arrays)


def edges(head, tail):
    ends = lax.axis_size("tensor") - 1
    return (
        lax.ppermute(tail, "tensor", [(i, i + 1) for i in range(ends)]),
        lax.ppermute(head, "tensor", [(i + 1, i) for i in range(ends)]),
    )


def halo(cells):
    count = lax.axis_size("tensor")
    ends = count - 1
    before = lax.ppermute(cells[:, -1:], "tensor", [(i, i + 1) for i in range(ends)])
    after = lax.ppermute(cells[:, :1], "tensor", [(i + 1, i) for i in range(ends)])
    return jnp.concatenate([before, cells, after], axis=1)


def body_plain(
    activations,
    encoder,
    species,
    cotangent,
    norm_gain,
    norm_shift,
    species_table,
    query_weight,
    key_weight,
    value_weight,
    output_weight,
    expand_weight,
    contract_weight,
    position_weight,
    content_bias,
    position_bias,
    upsample_weight,
    lateral_weight,
    depthwise_weight,
    section_bias,
    pointwise_weight,
):
    windows = lax.axis_size("dp")
    count = lax.axis_size("tensor")
    own = activations.shape[1]
    length = own * count
    width = activations.shape[2]
    local_heads = query_weight.shape[1] // KEYD
    keys = local_heads * KEYD
    values = local_heads * VALD

    raw = spread_blocks(activations[0])
    attn_shard = jnp.concatenate([query_weight, key_weight, value_weight, output_weight.T], axis=1)
    attn_blocks = [gather_dp(attn_shard)]
    where = jnp.stack([lax.axis_index("dp"), lax.axis_index("tensor"), species[0]])

    small = jnp.concatenate(
        [norm_gain, norm_shift, species_table, depthwise_weight, section_bias[None]], axis=0
    )
    n_small = small.size
    n_position = position_weight.size
    n_bias = content_bias.size
    packed = gather_small(
        jnp.concatenate(
            [
                small.reshape(-1),
                position_weight.reshape(-1),
                content_bias.reshape(-1),
                position_bias.reshape(-1),
            ]
        )
    )
    small_all = packed[:, :, :n_small].reshape(windows, count, 10, -1)
    norm_all = jnp.transpose(small_all[:, :, :6], (2, 0, 1, 3)).reshape(6, width)
    norm_all = norm_all.astype(jnp.float32)
    gain_vals, shift_vals, table_rows = norm_all[:2], norm_all[2:4], norm_all[4:]
    small_group = lax.dynamic_index_in_dim(small_all, lax.axis_index("dp"), 0, False)
    small_group = jnp.swapaxes(small_group, 0, 1).reshape(10, -1).astype(jnp.float32)
    channels = small_group.shape[1]
    depth_taps = small_group[6:9]
    bias_section = small_group[9]
    heads_all = lax.dynamic_index_in_dim(packed, lax.axis_index("tensor"), 1, False)[:, n_small:]
    w_position = heads_all[:, :n_position].reshape(KEYD, BASIS, local_heads)
    bias_content = heads_all[:, n_position : n_position + n_bias].reshape(KEYD, local_heads)
    bias_position = heads_all[:, n_position + n_bias :].reshape(KEYD, local_heads)

    section_shard = jnp.concatenate([pointwise_weight, upsample_weight.T, lateral_weight.T], axis=0)
    w_section = lax.all_gather(section_shard, "tensor", axis=0).reshape(count, 3, -1, width)
    w_point = w_section[:, 0].reshape(channels, width)
    w_up = w_section[:, 1].reshape(channels, width)
    w_lat = w_section[:, 2].reshape(channels, width)
    cot_all = gather_dp(cotangent[0])
    ffn_shard = jnp.concatenate([expand_weight, contract_weight.T], axis=1)
    w_ffn = lax.all_gather(ffn_shard, "dp", axis=0, tiled=True)
    hidden_count = expand_weight.shape[1]
    enc_all = gather_dp(encoder[0])

    fine = 2 * own
    grad_deep = dot_transposed(cot_all, w_point).astype(LOW)
    grad_wide = halo(grad_deep.reshape(windows, fine, channels)).astype(jnp.float32)
    grad_mix = (
        depth_taps[0] * grad_wide[:, 2:]
        + depth_taps[1] * grad_wide[:, 1:-1]
        + depth_taps[2] * grad_wide[:, :-2]
    ).astype(LOW)
    grad_coarse = jnp.sum(
        grad_mix.astype(jnp.float32).reshape(windows * own, 2, channels), axis=1
    ).astype(LOW)
    grad_resid_two = scatter_dp(dot_plain(grad_coarse, w_up).astype(LOW)).astype(jnp.float32)
    grad_ffn = spread_blocks(grad_resid_two.astype(LOW))

    species_mask = (jnp.arange(SPECIES, dtype=jnp.int32) == species[0]).astype(jnp.float32)
    species_row = jnp.sum(species_mask[:, None] * table_rows, axis=0)
    content_flat = bias_content.astype(jnp.float32).T.reshape(1, -1)
    position_flat = bias_position.astype(jnp.float32).T.reshape(1, -1)
    basis_turned = jnp.pad(basis_table(length, BASIS).astype(LOW)[::-1], ((0, 1), (0, 0)))
    rel_weight = jnp.transpose(w_position, (1, 2, 0)).reshape(BASIS, -1)
    rel_turned = dot_plain(basis_turned, rel_weight).astype(LOW)
    attn_parts, saved = attention_forward(
        where,
        raw,
        [species_row[None], gain_vals[:1], shift_vals[:1], content_flat, position_flat],
        rel_turned,
        attn_blocks,
        local_heads,
        own,
    )
    resid_one, unit_two, scale_two, normed_two = second_norm(
        attn_parts[0],
        collect_blocks(attn_parts[1:]),
        [raw[0], species_row[None]],
        gain_vals[1:],
        shift_vals[1:],
    )

    contract_part, normed_two_all, hidden_low, slope = feed_forward_up(
        where, spread_blocks(normed_two), w_ffn
    )
    ffn_parts, (grad_ffn_all, grad_hidden_pre) = feed_forward_back(grad_ffn, slope, w_ffn)
    grad_resid_one, grad_attn, sums_two = second_norm_back(
        ffn_parts[0],
        collect_blocks(ffn_parts[1:]),
        unit_two,
        scale_two,
        gain_vals[1:],
        grad_resid_two,
    )

    resid_two = resid_one + scatter_tensor(contract_part).astype(jnp.float32)
    section_all = gather_dp(resid_two.astype(LOW))
    coarse = dot_transposed(section_all, w_up).reshape(windows, own, channels)
    section_mix = (
        jnp.repeat(coarse, 2, axis=1)
        + dot_transposed(enc_all, w_lat).reshape(windows, fine, channels)
        + bias_section
    ).astype(LOW)
    mix_wide = halo(section_mix).astype(jnp.float32)
    deep_rows = (
        depth_taps[0] * mix_wide[:, :-2]
        + depth_taps[1] * mix_wide[:, 1:-1]
        + depth_taps[2] * mix_wide[:, 2:]
    ).astype(LOW)
    deep_rows = deep_rows.reshape(windows * fine, channels)
    section_out = scatter_dp(dot_plain(deep_rows, w_point).astype(LOW)).astype(LOW)
    grad_mix_rows = grad_mix.reshape(windows * fine, channels)
    encoder_grad = scatter_dp(dot_plain(grad_mix_rows, w_lat).astype(LOW)).astype(jnp.float32)
    grad_centre = grad_wide[:, 1:-1]
    grad_section_small = jnp.stack(
        [jnp.sum(mix_wide[:, s : s + fine] * grad_centre, axis=(0, 1)) for s in range(3)]
        + [jnp.sum(grad_mix.astype(jnp.float32), axis=(0, 1))],
        axis=1,
    )
    section_cols = jnp.stack(
        [
            dot_leading(deep_rows, cot_all).astype(LOW).reshape(count, -1, width),
            dot_leading(grad_coarse, section_all).astype(LOW).reshape(count, -1, width),
            dot_leading(grad_mix_rows, enc_all).astype(LOW).reshape(count, -1, width),
        ],
        axis=1,
    )
    section_cols = scatter_tensor(section_cols)[0].astype(jnp.float32)

    ffn_out = scatter_dp(
        feed_forward_weights(
            where, normed_two_all, grad_ffn_all, hidden_low, grad_hidden_pre, 1
        )[0]
    ).astype(jnp.float32)

    head_parts, (grad_attn_all, grad_heads, bias_sums, rel_grad, own_sums) = attention_backward(
        where,
        spread_blocks(grad_attn),
        saved,
        rel_turned,
        basis_turned,
        gain_vals[:1],
        sums_two,
        local_heads,
        own,
    )
    head_received = collect_blocks(head_parts[1:])
    grad_resid_in = first_norm_back(
        where, head_parts[0], head_received, saved[2], saved[3], gain_vals[:1], grad_resid_one
    )
    weights = attention_weights(
        where, saved, grad_attn_all, grad_heads, own_sums, head_received, bias_sums, rel_grad, 1
    )[0]
    attn_out = scatter_dp(weights).astype(jnp.float32)
    norm_sums = own_sums[:6]
    for block in head_received:
        norm_sums = norm_sums + block[own : own + 6].astype(jnp.float32)
    norm_cols = jnp.swapaxes(norm_sums.reshape(6, windows, channels), 0, 1)
    head_cols = jnp.concatenate([bias_sums, rel_grad], axis=0)
    head_cols = jnp.transpose(head_cols.reshape(2 + BASIS, local_heads, KEYD), (2, 0, 1))
    heads_cols = jnp.concatenate(
        [
            head_cols[:, 2:].reshape(windows, -1),
            head_cols[:, 0].reshape(windows, -1),
            head_cols[:, 1].reshape(windows, -1),
        ],
        axis=1,
    )
    small_out = scatter_dp(jnp.concatenate([norm_cols.reshape(windows, -1), heads_cols], axis=1))
    small_out = small_out[0]
    n_norm = 6 * channels
    section_sums = grad_section_small.T
    for k in range(1, count):
        section_sums = section_sums + from_ahead(grad_section_small.T, k)
    norm_out = jnp.concatenate([small_out[:n_norm].reshape(6, channels), section_sums])
    share = channels // count
    norm_out = lax.dynamic_slice_in_dim(norm_out, lax.axis_index("tensor") * share, share, 1)
    heads_out = small_out[n_norm:]
    return (
        section_out[None],
        grad_resid_in,
        encoder_grad[None],
        norm_out[0:2],
        norm_out[2:4],
        norm_out[4:6],
        attn_out[:, :keys],
        attn_out[:, keys : 2 * keys],
        attn_out[:, 2 * keys : 2 * keys + values],
        attn_out[:, 2 * keys + values :].T,
        ffn_out[:, :hidden_count],
        ffn_out[:, hidden_count:].T,
        heads_out[:n_position].reshape(position_weight.shape),
        heads_out[n_position : n_position + n_bias].reshape(content_bias.shape),
        heads_out[n_position + n_bias :].reshape(position_bias.shape),
        section_cols[1].T,
        section_cols[2].T,
        norm_out[6:9],
        norm_out[9],
        section_cols[0],
    )


def body_direct(
    activations,
    encoder,
    species,
    cotangent,
    norm_gain,
    norm_shift,
    species_table,
    query_weight,
    key_weight,
    value_weight,
    output_weight,
    expand_weight,
    contract_weight,
    position_weight,
    content_bias,
    position_bias,
    upsample_weight,
    lateral_weight,
    depthwise_weight,
    section_bias,
    pointwise_weight,
):
    count = lax.axis_size("tensor")
    own, width = activations.shape[1:]
    length = own * count
    local_heads = query_weight.shape[1] // KEYD
    keys = local_heads * KEYD
    values = local_heads * VALD
    hidden_count = expand_weight.shape[1]
    share = section_bias.shape[0]
    where = jnp.stack([lax.axis_index("dp"), lax.axis_index("tensor"), species[0]])

    small = [norm_gain, norm_shift, species_table, depthwise_weight, section_bias[None]]
    entries = sum(block.size for block in small + [position_weight, content_bias, position_bias])
    raw = spread_blocks(
        pack_rows(
            activations[0],
            small,
            jnp.swapaxes(position_weight, 1, 2),
            [content_bias.T, position_bias.T],
            cotangent[0],
            encoder[0],
        )
    )
    attn_shard = jnp.concatenate([query_weight, key_weight, value_weight, output_weight.T], axis=1)
    attn_rows = attn_shard.shape[0]
    attn_chips = chips_of(attn_shard)
    raw, attn_chips, cot, section_shard = join(
        raw, attn_chips, cotangent[0], [pointwise_weight, upsample_weight.T, lateral_weight.T]
    )
    section_shard = jnp.concatenate(section_shard, axis=0)
    w_section = lax.all_gather(section_shard, "tensor", axis=0, tiled=True)
    line, cot_ends, enc_ends = pick_rows(raw, own, entries)
    cot = jnp.concatenate([cot, cot_ends], axis=0)
    blank = jnp.zeros((14, width), LOW)
    small_rows = gather_dp(line)
    attn_blocks = both_cores(*attn_chips)
    small_rows, attn_blocks, cot = join(small_rows, attn_blocks, cot)
    cot_chips = chips_of(cot)
    basis_turned = jnp.pad(basis_table(length, BASIS).astype(LOW)[::-1], ((0, 1), (0, 0)))
    rows, (depth_taps, bias_section, rel_turned, content_flat, position_flat) = unpack_small(
        where, small_rows, basis_turned, width, local_heads, count
    )
    gain_one, gain_two, shift_one, shift_two, species_row = rows
    attn_parts, saved = attention_forward(
        where,
        raw,
        [species_row, gain_one, shift_one, content_flat, position_flat],
        rel_turned,
        attn_blocks,
        local_heads,
        own,
    )
    attn_parts, cot_chips, ffn_shard, enc = join(
        attn_parts, cot_chips, [expand_weight, contract_weight.T], encoder[0]
    )
    w_ffn = gather_dp(jnp.concatenate(ffn_shard, axis=1))
    enc = jnp.concatenate([enc, enc_ends], axis=0)

    attn_received = collect_blocks(attn_parts[1:])
    cot_blocks = both_cores(*cot_chips)
    grad_deep, grad_mix, grad_coarse, bias_grad, *halves_two, w_point, w_up, w_lateral = (
        section_gradient(where, cot_blocks, w_section, depth_taps, count)
    )
    attn_received, halves_two = join(attn_received, halves_two)

    resid_one, unit_two, scale_two, normed_two = second_norm(
        attn_parts[0], attn_received, [activations[0], species_row], gain_two, shift_two
    )
    normed_two, halves_two = join(normed_two, halves_two)
    normed_blocks = spread_blocks(normed_two)
    grad_resid_two = direct_sums(core_pairs(halves_two), LOW)
    normed_blocks, grad_resid_two, enc = join(normed_blocks, grad_resid_two, enc)

    grad_ffn = spread_blocks(grad_resid_two.astype(LOW))
    contract_part, normed_two_all, hidden_low, slope = feed_forward_up(where, normed_blocks, w_ffn)
    enc_chips = chips_of(enc)
    grad_ffn, contract_part, enc_chips, late_mix = join(
        grad_ffn, contract_part, enc_chips, grad_mix
    )

    contract_sum = scatter_tensor(contract_part)
    enc_blocks = both_cores(*enc_chips)
    ffn_parts, (grad_ffn_all, grad_hidden_pre) = feed_forward_back(grad_ffn, slope, w_ffn)
    ffn_received = collect_blocks(ffn_parts[1:])
    ffn_received, grad_hidden_pre, enc_blocks = join(ffn_received, grad_hidden_pre, enc_blocks)

    grad_resid_one, grad_attn, sums_two = second_norm_back(
        ffn_parts[0], ffn_received, unit_two, scale_two, gain_two, grad_resid_two
    )
    coarse = (resid_one + contract_sum.astype(jnp.float32)).astype(LOW)
    grad_attn = [grad_attn, coarse[:1], coarse[-1:], jnp.zeros((6, width), LOW)]
    grad_attn, grad_hidden_pre, late_mix = join(
        jnp.concatenate(grad_attn, axis=0), grad_hidden_pre, late_mix
    )
    grad_attn_blocks = spread_blocks(grad_attn)
    encoder_part = section_grad_encoder(where, late_mix, w_lateral, lax.axis_size("dp"))
    ffn_halves = feed_forward_weights(
        where, normed_two_all, grad_ffn_all, hidden_low, grad_hidden_pre, lax.axis_size("dp")
    )
    grad_attn_blocks, ffn_halves, encoder_part = join(grad_attn_blocks, ffn_halves, encoder_part)
    encoder_grad = scatter_dp(encoder_part).astype(jnp.float32)

    coarse = [coarse, grad_attn_blocks[-1][own + 1 : own + 2], grad_attn_blocks[1][own : own + 1]]
    coarse_chips = chips_of(jnp.concatenate(coarse + [blank], axis=0))
    ffn_pairs = core_pairs(ffn_halves)
    head_parts, (grad_attn_all, grad_heads, bias_sums, rel_grad, own_sums) = attention_backward(
        where,
        grad_attn_blocks,
        saved,
        rel_turned,
        basis_turned,
        gain_one,
        sums_two,
        local_heads,
        own,
    )
    head_parts, coarse_chips, ffn_pairs = join(head_parts, coarse_chips, ffn_pairs)
    ffn_corners = corner_sums(ffn_pairs, LOW)
    head_received = collect_blocks(head_parts[1:])
    ffn_out = chip_sums(ffn_pairs, ffn_corners, LOW)
    coarse_blocks = both_cores(*coarse_chips)
    deep_rows, taps_grad, *out_halves = section_forward(
        where,
        coarse_blocks,
        enc_blocks,
        w_up,
        w_lateral,
        w_point,
        bias_section,
        depth_taps,
        grad_deep,
        count,
    )
    section_sums = jnp.pad(jnp.concatenate([taps_grad, bias_grad], axis=0), ((0, 12), (0, 0)))
    cols_part = section_weights(
        deep_rows,
        grad_coarse,
        grad_mix,
        cot_blocks,
        coarse_blocks,
        enc_blocks,
        section_sums,
        count,
    )
    section_cols = scatter_tensor(cols_part)[0].astype(jnp.float32)
    out_pairs = core_pairs(out_halves)
    head_received, out_pairs, ffn_out = join(head_received, out_pairs, ffn_out)

    grad_resid_in = first_norm_back(
        where, head_parts[0], head_received, saved[2], saved[3], gain_one, grad_resid_one
    )
    attn_halves = attention_weights(
        where,
        saved,
        grad_attn_all,
        grad_heads,
        own_sums,
        head_received,
        bias_sums,
        rel_grad,
        len(attn_blocks),
    )
    attn_pairs = core_pairs(attn_halves)
    section_out = direct_sums(out_pairs, LOW).astype(LOW)
    attn_pairs, section_out, grad_resid_in, encoder_grad = join(
        attn_pairs, section_out, grad_resid_in, encoder_grad
    )
    attn_out = direct_sums(attn_pairs, LOW)

    small_out, attn_out = attn_out[attn_rows:], attn_out[:attn_rows]
    norm_out = lax.dynamic_slice_in_dim(
        small_out[: 4 + SPECIES], lax.axis_index("tensor") * share, share, 1
    )
    part = KEYD // lax.axis_size("dp")

    def heads_of(rows):
        return rows.reshape(rows.shape[0], local_heads, KEYD)[:, :, :part]

    bias_out = jnp.transpose(heads_of(small_out[8:10, :keys]), (2, 0, 1))
    rel_out = [small_out[:, 256 : 256 + keys], small_out[:, 256 + keys : 256 + 2 * keys]]
    rel_out = jnp.transpose(heads_of(jnp.concatenate(rel_out, axis=0)), (2, 0, 1))
    return (
        section_out[None],
        grad_resid_in,
        encoder_grad[None],
        norm_out[0:2],
        norm_out[2:4],
        norm_out[4:],
        attn_out[:, :keys],
        attn_out[:, keys : 2 * keys],
        attn_out[:, 2 * keys : 2 * keys + values],
        attn_out[:, 2 * keys + values :].T,
        ffn_out[:, :hidden_count],
        ffn_out[:, hidden_count:].T,
        rel_out,
        bias_out[:, 0],
        bias_out[:, 1],
        section_cols[share : 2 * share].T,
        section_cols[2 * share : 3 * share].T,
        section_cols[3 * share : 3 * share + 3, :share],
        section_cols[3 * share + 3, :share],
        section_cols[:share],
    )


def solution(mesh):
    rows = P("dp", "tensor", None)
    narrow = P(None, ("dp", "tensor"))
    split = P("dp", "tensor")
    turned = P("tensor", "dp")
    vector = P(("dp", "tensor"))
    tall = P(("dp", "tensor"), None)
    position = P("dp", None, "tensor")
    weights = (split, split, split, turned, split, turned, position, split, split)
    return jax.shard_map(
        body_direct if mesh.shape["dp"] == 8 else body_plain,
        mesh=mesh,
        in_specs=(rows, rows, P("dp"), rows, narrow, narrow, narrow)
        + weights
        + (narrow, narrow, narrow, vector, tall),
        out_specs=(rows, rows, rows, narrow, narrow, narrow)
        + weights
        + (narrow, narrow, narrow, vector, tall),
        check_vma=False,
    )
```

```python
import math

import jax
import jax.numpy as jnp
from jax import lax
from jax.experimental import pallas as pl
from jax.experimental.pallas import tpu as pltpu
from jax.sharding import PartitionSpec as P

KEYD = 64
VALD = 192
BASIS = 32
SPECIES = 2
SCALE = 1.0 / math.sqrt(KEYD)
LOW = jnp.bfloat16


def dot_plain(left_side, right_side):
    return jnp.dot(left_side, right_side, preferred_element_type=jnp.float32)


def dot_transposed(left_side, right_side):
    return lax.dot_general(
        left_side, right_side, (((1,), (1,)), ((), ())), preferred_element_type=jnp.float32
    )


def dot_leading(left_side, right_side):
    return lax.dot_general(
        left_side, right_side, (((0,), (0,)), ((), ())), preferred_element_type=jnp.float32
    )


def exact_gelu(values):
    return jax.nn.gelu(values, approximate=False)


def normalize(values):
    centred = values - jnp.mean(values, axis=-1, keepdims=True)
    variance = jnp.mean(centred * centred, axis=-1, keepdims=True)
    scale = lax.rsqrt(variance + 1e-05)
    return centred * scale, scale


def normalize_back(unit, scale, grad_unit):
    return scale * (
        grad_unit
        - jnp.mean(grad_unit, axis=-1, keepdims=True)
        - unit * jnp.mean(grad_unit * unit, axis=-1, keepdims=True)
    )


def basis_table(length, features):
    distance = jnp.arange(2 * length - 1).astype(jnp.float32) - (length - 1)
    halves = features // 2
    fraction = jnp.arange(halves).astype(jnp.float32) / (halves - 1)
    lifetimes = 3.0 * jnp.power(length / 3.0, fraction)
    decays = jnp.exp(-0.6931471805599453 * jnp.abs(distance)[:, None] / lifetimes[None, :])
    return jnp.concatenate([decays, jnp.sign(distance)[:, None] * decays], axis=1)


def dot_rows(left_side, right_side):
    return jnp.dot(left_side, right_side, preferred_element_type=jnp.float32)


def run_kernel(kernel, ins, outs, scalars=None, scratch=(), far=(), far_outs=(), room=52):
    whole = pl.BlockSpec(memory_space=pltpu.VMEM)
    outside = pl.BlockSpec(memory_space=pl.ANY)
    specs = [outside] * len(far) + [whole] * len(ins)
    args = list(far) + list(ins)
    if scalars is not None:
        specs = [pl.BlockSpec(memory_space=pltpu.SMEM)] + specs
        args = [scalars] + args
    shapes = [jax.ShapeDtypeStruct(shape, dtype) for shape, dtype in list(outs) + list(far_outs)]
    return pl.pallas_call(
        kernel,
        in_specs=specs,
        out_specs=[whole] * len(outs) + [outside] * len(far_outs),
        out_shape=shapes,
        scratch_shapes=scratch,
        compiler_params=pltpu.CompilerParams(vmem_limit_bytes=room * 1024 * 1024),
        name=kernel.__qualname__.split(".")[0],
    )(*args)


def start_copies(pairs, sems, first=0):
    copies = [
        pltpu.make_async_copy(source, target, sems.at[first + n])
        for n, (source, target) in enumerate(pairs)
    ]
    for copy in copies:
        copy.start()
    return copies


def wait_copies(copies):
    for copy in copies:
        copy.wait()


def halves(windows, shape, dtype):
    return [(shape, dtype)] * windows


def place(m, windows):
    return m // 2 + m % 2 * (windows // 2)


def lanes_of(head, width, shape):
    lane = lax.broadcasted_iota(jnp.int32, shape, len(shape) - 1)
    return (lane >= head * width) & (lane < (head + 1) * width)


def chunk_of(where_ref, step, count):
    return lax.rem(where_ref[1] + step, count)


def attention_forward(where, raw, row_params, rel_turned, blocks, local_heads, own):
    count, width = len(raw), raw[0].shape[1]
    length = count * own
    n_blocks, columns = len(blocks), blocks[0].shape[1]
    rows = width // n_blocks
    keys, values = local_heads * KEYD, local_heads * VALD

    def kernel(where_ref, *refs):
        raw_refs, refs = refs[:count], refs[count:]
        species_ref, gain_ref, shift_ref, content_ref, position_ref, rel_ref = refs[:6]
        block_refs, refs = refs[6 : 6 + n_blocks], refs[6 + n_blocks :]
        own_ref, refs = refs[0], refs[1:]
        part_refs, refs = refs[: count - 1], refs[count - 1 :]
        (weight_ref, normed_ref, unit_ref, scale_ref, probs_ref, content_out, position_out) = refs[:7]
        key_out, value_out, mixed_out, total_ref = refs[7:]
        for m in range(n_blocks):
            spot = (where_ref[0] ^ m) * rows if n_blocks > 1 else 0
            weight_ref[pl.ds(pl.multiple_of(spot, rows), rows), :] = block_refs[m][:rows, :]
        for k in range(count):
            resid = raw_refs[k][:own, :].astype(jnp.float32) + species_ref[...]
            unit, scale = normalize(resid)
            spot = pl.ds(pl.multiple_of(chunk_of(where_ref, k, count) * own, own), own)
            unit_ref[spot, :] = unit
            scale_ref[spot, :] = jnp.broadcast_to(scale, (own, 128))
            normed_ref[spot, :] = (unit * gain_ref[...] + shift_ref[...]).astype(LOW)
        normed = normed_ref[...]
        query = dot_rows(normed, weight_ref[:, :keys])
        content = (query + content_ref[...]).astype(LOW)
        position = (query + position_ref[...]).astype(LOW)
        key_low = dot_rows(normed, weight_ref[:, keys : 2 * keys]).astype(LOW)
        value_low = dot_rows(normed, weight_ref[:, 2 * keys : 2 * keys + values]).astype(LOW)
        content_out[...] = content
        position_out[...] = position
        key_out[...] = key_low
        value_out[...] = value_low
        mixed = jnp.zeros((length, values), jnp.float32)
        for h in range(local_heads):
            mine = lanes_of(h, KEYD, (length, keys))
            zero = jnp.zeros((), LOW)
            banded = dot_transposed(jnp.where(mine, position, zero), rel_ref[...])
            skewed = pltpu.roll(banded, length + 1, 1, stride=1, stride_axis=0)[:, :length]
            scores = (dot_transposed(jnp.where(mine, content, zero), key_low) + skewed) * SCALE
            exponent = jnp.exp(scores - jnp.max(scores, axis=-1, keepdims=True))
            probs = exponent / jnp.sum(exponent, axis=-1, keepdims=True)
            probs_ref[h] = probs
            mixed = jnp.where(
                lanes_of(h, VALD, (length, values)), dot_rows(probs.astype(LOW), value_low), mixed
            )
        mixed_out[...] = mixed.astype(LOW)
        total_ref[...] = dot_transposed(mixed.astype(LOW), weight_ref[:, 2 * keys + values :])
        for k in range(count):
            spot = pl.ds(pl.multiple_of(chunk_of(where_ref, k, count) * own, own), own)
            if k == 0:
                own_ref[...] = total_ref[spot, :]
            else:
                part_refs[k - 1][...] = total_ref[spot, :].astype(LOW)

    outs = (
        [((own, width), jnp.float32)]
        + [((own, width), LOW)] * (count - 1)
        + [
            ((width, columns), LOW),
            ((length, width), LOW),
            ((length, width), jnp.float32),
            ((length, 128), jnp.float32),
            ((local_heads, length, length), jnp.float32),
            ((length, keys), LOW),
            ((length, keys), LOW),
            ((length, keys), LOW),
            ((length, values), LOW),
            ((length, values), LOW),
        ]
    )
    found = run_kernel(
        kernel,
        list(raw) + list(row_params) + [rel_turned] + list(blocks),
        outs,
        scalars=where,
        scratch=[pltpu.VMEM((length, width), jnp.float32)],
    )
    return found[:count], found[count:]


def attention_backward(
    where, grads, saved, rel_turned, basis_turned, gain, sums_two, local_heads, own
):
    count, width = len(grads), grads[0].shape[1]
    length = count * own
    weight, _, unit_all, scale_all, probs_all, content_all, position_all, key_all, value_all, _ = saved
    keys, values = local_heads * KEYD, local_heads * VALD
    narrow = 2 * keys + values

    def kernel(where_ref, *refs):
        grad_refs, refs = refs[:count], refs[count:]
        weight_ref, probs_ref, content_ref, position_ref, key_ref, value_ref = refs[:6]
        rel_ref, basis_ref, unit_ref, scale_ref, gain_ref, two_ref = refs[6:12]
        own_ref, refs = refs[12], refs[13:]
        part_refs, refs = refs[: count - 1], refs[count - 1 :]
        attn_ref, heads_ref, bias_ref, weight_out, sums_ref, total_ref = refs
        for k in range(count):
            spot = pl.ds(pl.multiple_of(chunk_of(where_ref, k, count) * own, own), own)
            attn_ref[spot, :] = grad_refs[k][:own, :]
        grad_mixed = dot_rows(attn_ref[...], weight_ref[:, narrow:]).astype(LOW)
        content, position = content_ref[...], position_ref[...]
        key_low, value_low = key_ref[...], value_ref[...]
        grad_content = jnp.zeros((length, keys), jnp.float32)
        grad_position = jnp.zeros((length, keys), jnp.float32)
        grad_key = jnp.zeros((length, keys), jnp.float32)
        grad_rel = jnp.zeros((2 * length, keys), jnp.float32)
        grad_value = jnp.zeros((length, values), jnp.float32)
        row = lax.broadcasted_iota(jnp.int32, (length, length), 0)
        column = lax.broadcasted_iota(jnp.int32, (length, length), 1)
        reverse = (row + column == length - 1).astype(jnp.float32).astype(LOW)
        position_reversed = dot_rows(reverse, position).astype(LOW)
        for h in range(local_heads):
            mine = lanes_of(h, KEYD, (length, keys))
            ours = lanes_of(h, VALD, (length, values))
            probs = probs_ref[h]
            grad_probs = dot_transposed(
                jnp.where(ours, grad_mixed, jnp.zeros((), LOW)), value_low
            )
            centre = jnp.sum(probs * grad_probs, axis=-1, keepdims=True)
            grad_scores = (probs * (grad_probs - centre)).astype(LOW)
            grad_value = jnp.where(ours, dot_leading(probs.astype(LOW), grad_mixed), grad_value)
            grad_key = jnp.where(mine, dot_leading(grad_scores, content), grad_key)
            grad_content = jnp.where(mine, dot_rows(grad_scores, key_low), grad_content)
            band = dot_rows(reverse, grad_scores)
            band = jnp.concatenate([band, jnp.zeros((length, length), jnp.float32)], axis=1)
            band = pltpu.roll(band, 0, 1, stride=1, stride_axis=0).astype(LOW)
            turned = dot_rows(band, rel_ref[...])
            high = turned.astype(LOW)
            low = (turned - high.astype(jnp.float32)).astype(LOW)
            turned = dot_rows(reverse, high) + dot_rows(reverse, low)
            grad_position = jnp.where(mine, turned, grad_position)
            grad_rel = jnp.where(
                lanes_of(h, KEYD, (2 * length, keys)),
                dot_leading(band, position_reversed),
                grad_rel,
            )
        grad_content = grad_content * SCALE
        grad_position = grad_position * SCALE
        bias_ref[0:1, :] = jnp.sum(grad_content, axis=0, keepdims=True)
        bias_ref[1:2, :] = jnp.sum(grad_position, axis=0, keepdims=True)
        heads_ref[:, :keys] = (grad_content + grad_position).astype(LOW)
        heads_ref[:, keys : 2 * keys] = (grad_key * SCALE).astype(LOW)
        heads_ref[:, 2 * keys :] = grad_value.astype(LOW)
        weight_out[...] = dot_leading(basis_ref[...], (grad_rel * SCALE).astype(LOW))
        grad = dot_transposed(heads_ref[...], weight_ref[:, :narrow])
        total_ref[...] = grad
        unit = unit_ref[...]
        into = normalize_back(unit, scale_ref[:, :1], grad * gain_ref[...])
        table = jnp.sum(into, axis=0, keepdims=True) + two_ref[2:3, :]
        sums_ref[...] = jnp.zeros_like(sums_ref)
        sums_ref[0:1, :] = jnp.sum(grad * unit, axis=0, keepdims=True)
        sums_ref[1:2, :] = two_ref[0:1, :]
        sums_ref[2:3, :] = jnp.sum(grad, axis=0, keepdims=True)
        sums_ref[3:4, :] = two_ref[1:2, :]
        for kind in range(SPECIES):
            sums_ref[4 + kind : 5 + kind, :] = jnp.where(where_ref[2] == kind, table, 0.0)
        for k in range(count):
            spot = pl.ds(pl.multiple_of(chunk_of(where_ref, k, count) * own, own), own)
            if k == 0:
                own_ref[...] = total_ref[spot, :]
            else:
                part_refs[k - 1][:own, :] = total_ref[spot, :].astype(LOW)
                part_refs[k - 1][own:, :] = sums_ref[...].astype(LOW)

    outs = (
        [((own, width), jnp.float32)]
        + [((own + 16, width), LOW)] * (count - 1)
        + [
            ((length, width), LOW),
            ((length, narrow), LOW),
            ((2, keys), jnp.float32),
            ((BASIS, keys), jnp.float32),
            ((16, width), jnp.float32),
        ]
    )
    found = run_kernel(
        kernel,
        list(grads)
        + [weight, probs_all, content_all, position_all, key_all, value_all]
        + [rel_turned, basis_turned, unit_all, scale_all, gain, sums_two],
        outs,
        scalars=where,
        scratch=[pltpu.VMEM((length, width), jnp.float32)],
    )
    return found[:count], found[count:]


def attention_weights(
    where, saved, grad_attn, grad_heads, own_sums, received, bias_sums, rel_grad, n_blocks
):
    normed, mixed = saved[1], saved[9]
    width = normed.shape[1]
    rows = width // n_blocks
    narrow, values = grad_heads.shape[1], mixed.shape[1]
    columns = narrow + values
    keys = rel_grad.shape[1]
    count = len(received) + 1

    def kernel(where_ref, normed_ref, mixed_ref, attn_ref, heads_ref, own_ref, *refs):
        received_refs, refs = refs[: count - 1], refs[count - 1 :]
        bias_ref, rel_ref, half_refs, whole_ref = refs[0], refs[1], refs[2:-1], refs[-1]
        sums = own_ref[...]
        for ref in received_refs:
            sums = sums + ref[ref.shape[0] - 16 :, :].astype(jnp.float32)
        sums = sums[:8]
        whole_ref[:, :narrow] = dot_leading(normed_ref[...], heads_ref[...]).astype(LOW)
        whole_ref[:, narrow:] = dot_leading(attn_ref[...], mixed_ref[...]).astype(LOW)
        for m in range(n_blocks):
            spot = (where_ref[0] ^ m) if n_blocks > 1 else 0
            half = half_refs[place(m, n_blocks)]
            half[:rows, :] = whole_ref[pl.ds(pl.multiple_of(spot * rows, rows), rows), :]
            if n_blocks == 1:
                continue
            moved = pltpu.roll(sums, lax.rem(width - spot * rows, width), 1)[:, :256]
            turn = lax.rem(keys - spot * (KEYD // n_blocks), keys)
            rel = pltpu.roll(rel_ref[...], turn, 1)
            bias = pltpu.roll(bias_ref[...], turn, 1)
            bias = jnp.concatenate([bias, jnp.zeros((6, keys), jnp.float32)], axis=0)
            bias = jnp.concatenate([bias, jnp.zeros((8, 256 - keys), jnp.float32)], axis=1)
            half[rows:, :256] = jnp.concatenate([moved, bias], axis=0).astype(LOW)
            half[rows:, 256 : 256 + keys] = rel[:16].astype(LOW)
            half[rows:, 256 + keys : 256 + 2 * keys] = rel[16:].astype(LOW)
            half[rows:, 256 + 2 * keys :] = jnp.zeros((16, columns - 256 - 2 * keys), LOW)

    return run_kernel(
        kernel,
        [normed, mixed, grad_attn, grad_heads, own_sums] + list(received) + [bias_sums, rel_grad],
        halves(n_blocks, (rows + (16 if n_blocks > 1 else 0), columns), LOW),
        scalars=where,
        scratch=[pltpu.VMEM((width, columns), LOW)],
    )


def pack_rows(rows, channel_rows, weights, biases, cotangent, encoder):
    own, width = rows.shape
    fine = cotangent.shape[0]
    part, heads, basis = weights.shape
    share = channel_rows[0].shape[1]
    n_rows = sum(block.shape[0] for block in channel_rows)
    first = n_rows * share

    def kernel(cot_ref, enc_ref, rows_ref, *refs):
        channel_refs, refs = refs[: len(channel_rows)], refs[len(channel_rows) :]
        weights_ref, content_ref, position_ref, out_ref, ends_ref, sems = refs
        copies = start_copies(
            [
                (cot_ref.at[:16, :], ends_ref.at[0:16, :]),
                (cot_ref.at[fine - 16 :, :], ends_ref.at[16:32, :]),
                (enc_ref.at[:16, :], ends_ref.at[32:48, :]),
                (enc_ref.at[fine - 16 :, :], ends_ref.at[48:64, :]),
            ],
            sems,
        )
        out_ref[:own, :] = rows_ref[...]

        def place_of(size, start):
            column = lax.broadcasted_iota(jnp.int32, (size, width), 1) - start
            return column, lax.broadcasted_iota(jnp.int32, (size, width), 0)

        def widen(values, chosen, mine):
            found = dot_rows(values.astype(LOW), chosen.astype(jnp.float32).astype(LOW))
            return jnp.sum(jnp.where(mine, found, 0.0), axis=0, keepdims=True)

        def in_order(values, start):
            height, size = values.shape
            column, index = place_of(size, start)
            chosen = (column >= 0) & (column % size == index)
            column, index = place_of(height, start)
            return widen(values, chosen, (column >= 0) & (column // size == index))

        channel = jnp.concatenate([ref[...].astype(jnp.float32) for ref in channel_refs], axis=0)
        row = in_order(channel, 0)
        values = jnp.concatenate(
            [weights_ref[k].astype(jnp.float32) for k in range(part)], axis=0
        )
        column, index = place_of(basis, first)
        chosen = (column >= 0) & (column // (heads * part) == index)
        column, index = place_of(part * heads, first)
        mine = (column % part == index // heads) & (column // part % heads == index % heads)
        mine = mine & (column >= 0) & (column < part * heads * basis)
        row = row + widen(values, chosen, mine)
        start = first + part * heads * basis
        for ref in (content_ref, position_ref):
            row = row + in_order(ref[...].astype(jnp.float32), start)
            start += part * heads
        wait_copies(copies)
        ends = ends_ref[...].astype(jnp.float32)
        tail = [row, ends[:1], ends[31:32], ends[32:33], ends[63:], jnp.zeros((3, width), jnp.float32)]
        out_ref[own:, :] = jnp.concatenate(tail, axis=0).astype(LOW)

    return run_kernel(
        kernel,
        [rows] + list(channel_rows) + [weights] + list(biases),
        [((own + 8, width), LOW)],
        scratch=[pltpu.VMEM((64, width), LOW), pltpu.SemaphoreType.DMA((4,))],
        far=[cotangent, encoder],
        room=62,
    )[0]


def pick_rows(blocks, own, entries):
    width = blocks[0].shape[1]

    def kernel(*refs):
        block_refs, (line_ref, cot_ref, enc_ref) = refs[: len(blocks)], refs[len(blocks) :]
        tails = [ref[own:, :].astype(jnp.float32) for ref in block_refs]
        blank = jnp.zeros((14, width), jnp.float32)
        line_ref[...] = jnp.concatenate([tail[:1, :entries] for tail in tails], axis=0).astype(LOW)
        cot_ref[...] = jnp.concatenate([tails[-1][2:3], tails[1][1:2], blank], axis=0).astype(LOW)
        enc_ref[...] = jnp.concatenate([tails[-1][4:5], tails[1][3:4], blank], axis=0).astype(LOW)

    return run_kernel(
        kernel,
        blocks,
        [((len(blocks), entries), LOW), ((16, width), LOW), ((16, width), LOW)],
        room=62,
    )


def unpack_small(where, found, basis_turned, width, local_heads, count):
    total = found.shape[0]
    n_blocks = total // count
    share = width // total
    n_rows = 8 + SPECIES
    group = width // n_blocks
    keys = local_heads * KEYD
    piece = keys // n_blocks
    part = KEYD // n_blocks
    length = basis_turned.shape[0]

    def kernel(where_ref, *refs):
        found_ref, basis_ref, refs = refs[0], refs[1], refs[2:]
        row_refs, refs = refs[:5], refs[5:]
        taps_ref, bias_ref, rel_ref, content_ref, position_ref, weight_ref = refs

        def owner(shape):
            spot = lax.broadcasted_iota(jnp.int32, shape, 0)
            return spot // count, lax.rem(spot % count + where_ref[1], count)

        def widen(start, size, span):
            column = lax.broadcasted_iota(jnp.int32, (size, span), 1)
            inner = lax.broadcasted_iota(jnp.int32, (size, span), 0)
            if size == share:
                chosen = column % share == inner
            else:
                chosen = (column // KEYD == inner // part) & (column % part == inner % part)
            return dot_rows(
                found_ref[:, start : start + size],
                chosen.astype(jnp.float32).astype(LOW),
            )

        group_of, line_of = owner((total, width))
        column = lax.broadcasted_iota(jnp.int32, (total, width), 1) // share
        mask = group_of * count + line_of == column
        rows = [
            jnp.sum(jnp.where(mask, widen(r * share, share, width), 0.0), axis=0, keepdims=True)
            for r in range(4 + SPECIES)
        ]
        species = jnp.zeros((1, width), jnp.float32)
        for kind in range(SPECIES):
            species = jnp.where(where_ref[2] == kind, rows[4 + kind], species)
        for ref, row in zip(row_refs, rows[:4] + [species], strict=True):
            ref[...] = row
        group_of, line_of = owner((total, group))
        column = lax.broadcasted_iota(jnp.int32, (total, group), 1) // share
        mask = (group_of == where_ref[0]) & (line_of == column)
        rows = [
            jnp.sum(jnp.where(mask, widen(r * share, share, group), 0.0), axis=0, keepdims=True)
            for r in range(4 + SPECIES, n_rows)
        ]
        for r in range(3):
            taps_ref[r : r + 1, :] = rows[r]
        bias_ref[...] = rows[3]
        group_of, line_of = owner((total, keys))
        column = lax.broadcasted_iota(jnp.int32, (total, keys), 1) % KEYD // part
        mask = (line_of == where_ref[1]) & (group_of == column)
        start = n_rows * share
        for f in range(BASIS + 2):
            row = widen(start + f * piece, piece, keys)
            row = jnp.sum(jnp.where(mask, row, 0.0), axis=0, keepdims=True)
            if f < BASIS:
                weight_ref[f : f + 1, :] = row
            else:
                (content_ref if f == BASIS else position_ref)[...] = row
        rel_ref[...] = dot_rows(basis_ref[...], weight_ref[...].astype(LOW)).astype(LOW)

    found = run_kernel(
        kernel,
        [found, basis_turned],
        [((1, width), jnp.float32)] * 5
        + [((3, group), jnp.float32), ((1, group), jnp.float32)]
        + [((length, keys), LOW)]
        + [((1, keys), jnp.float32)] * 2,
        scalars=where,
        scratch=[pltpu.VMEM((BASIS, keys), jnp.float32)],
    )
    return found[:5], found[5:]


def second_norm(own_part, parts, resid_in, gain, shift):
    own, width = own_part.shape

    def kernel(own_ref, *refs):
        part_refs, refs = refs[: len(parts)], refs[len(parts) :]
        raw_ref, species_ref, gain_ref, shift_ref, resid_ref, unit_ref, scale_ref, low_ref = refs
        total = own_ref[...]
        for ref in part_refs:
            total = total + ref[...].astype(jnp.float32)
        resid = raw_ref[...].astype(jnp.float32) + species_ref[...] + total
        unit, scale = normalize(resid)
        resid_ref[...] = resid
        unit_ref[...] = unit
        scale_ref[...] = jnp.broadcast_to(scale, (own, 128))
        low_ref[...] = (unit * gain_ref[...] + shift_ref[...]).astype(LOW)

    return run_kernel(
        kernel,
        [own_part] + list(parts) + list(resid_in) + [gain, shift],
        [
            ((own, width), jnp.float32),
            ((own, width), jnp.float32),
            ((own, 128), jnp.float32),
            ((own, width), LOW),
        ],
    )


def second_norm_back(own_part, parts, unit, scale, gain, grad_resid):
    own, width = own_part.shape

    def kernel(own_ref, *refs):
        part_refs, refs = refs[: len(parts)], refs[len(parts) :]
        unit_ref, scale_ref, gain_ref, grad_ref, resid_ref, low_ref, sums_ref = refs
        total = own_ref[...]
        for ref in part_refs:
            total = total + ref[...].astype(jnp.float32)
        unit_rows = unit_ref[...]
        resid = grad_ref[...] + normalize_back(unit_rows, scale_ref[:, :1], total * gain_ref[...])
        resid_ref[...] = resid
        low_ref[...] = resid.astype(LOW)
        sums_ref[0:1, :] = jnp.sum(total * unit_rows, axis=0, keepdims=True)
        sums_ref[1:2, :] = jnp.sum(total, axis=0, keepdims=True)
        sums_ref[2:3, :] = jnp.sum(resid, axis=0, keepdims=True)

    return run_kernel(
        kernel,
        [own_part] + list(parts) + [unit, scale, gain, grad_resid],
        [((own, width), jnp.float32), ((own, width), LOW), ((3, width), jnp.float32)],
    )


def first_norm_back(where, own_part, parts, unit_all, scale_all, gain, grad_resid):
    own, width = own_part.shape

    def kernel(where_ref, own_ref, *refs):
        part_refs, refs = refs[: len(parts)], refs[len(parts) :]
        unit_ref, scale_ref, gain_ref, grad_ref, out_ref = refs
        total = own_ref[...]
        for ref in part_refs:
            total = total + ref[:own, :].astype(jnp.float32)
        spot = pl.ds(pl.multiple_of(where_ref[1] * own, own), own)
        out_ref[0] = grad_ref[...] + normalize_back(
            unit_ref[spot, :], scale_ref[spot, :1], total * gain_ref[...]
        )

    return run_kernel(
        kernel,
        [own_part] + list(parts) + [unit_all, scale_all, gain, grad_resid],
        [((1, own, width), jnp.float32)],
        scalars=where,
    )[0]


def feed_forward_up(where, normed, weight):
    count, (own, width) = len(normed), normed[0].shape
    length = count * own
    hidden_count = weight.shape[1] // 2

    def kernel(where_ref, *refs):
        normed_refs, (weight_ref, part_ref, normed_out, hidden_out, slope_out) = refs[:count], refs[count:]
        for k in range(count):
            normed_out[k * own : (k + 1) * own, :] = normed_refs[k][...]
        pre = dot_rows(normed_out[...], weight_ref[:, :hidden_count])
        below = 0.5 * (1.0 + lax.erf(pre * math.sqrt(0.5)))
        hidden_out[...] = (pre * below).astype(LOW)
        slope_out[...] = below + pre * jnp.exp(-0.5 * pre * pre) * (1.0 / math.sqrt(2.0 * math.pi))
        total = dot_transposed(hidden_out[...], weight_ref[:, hidden_count:])
        for k in range(count):
            spot = pl.ds(pl.multiple_of(chunk_of(where_ref, k, count) * own, own), own)
            part_ref[spot, :] = total[k * own : (k + 1) * own].astype(LOW)

    return run_kernel(
        kernel,
        list(normed) + [weight],
        [((length, width), LOW)] * 2
        + [((length, hidden_count), LOW), ((length, hidden_count), jnp.float32)],
        scalars=where,
    )


def feed_forward_back(grads, slope, weight):
    count, (own, width) = len(grads), grads[0].shape
    length = count * own
    hidden_count = weight.shape[1] // 2

    def kernel(*refs):
        grad_refs, (slope_ref, weight_ref, own_ref), refs = refs[:count], refs[count : count + 3], refs[count + 3 :]
        part_refs, (grad_out, pre_out) = refs[: count - 1], refs[count - 1 :]
        for k in range(count):
            grad_out[k * own : (k + 1) * own, :] = grad_refs[k][...]
        grad_hidden = dot_rows(grad_out[...], weight_ref[:, hidden_count:])
        pre_out[...] = (grad_hidden * slope_ref[...]).astype(LOW)
        total = dot_transposed(pre_out[...], weight_ref[:, :hidden_count])
        own_ref[...] = total[:own]
        for k in range(1, count):
            part_refs[k - 1][...] = total[k * own : (k + 1) * own].astype(LOW)

    found = run_kernel(
        kernel,
        list(grads) + [slope, weight],
        [((own, width), jnp.float32)]
        + [((own, width), LOW)] * (count - 1)
        + [((length, width), LOW), ((length, hidden_count), LOW)],
    )
    return found[:count], found[count:]


def feed_forward_weights(where, normed_all, grad_all, hidden, grad_pre, n_blocks):
    width = normed_all.shape[1]
    hidden_count = hidden.shape[1]
    rows = width // n_blocks

    def kernel(where_ref, normed_ref, grad_ref, hidden_ref, pre_ref, *refs):
        half_refs, whole_ref = refs[:-1], refs[-1]
        whole_ref[:, :hidden_count] = dot_leading(normed_ref[...], pre_ref[...]).astype(LOW)
        whole_ref[:, hidden_count:] = dot_leading(grad_ref[...], hidden_ref[...]).astype(LOW)
        for m in range(n_blocks):
            spot = (where_ref[0] ^ m) * rows if n_blocks > 1 else 0
            half_refs[place(m, n_blocks)][...] = whole_ref[
                pl.ds(pl.multiple_of(spot, rows), rows), :
            ]

    return run_kernel(
        kernel,
        [normed_all, grad_all, hidden, grad_pre],
        halves(n_blocks, (rows, 2 * hidden_count), LOW),
        scalars=where,
        scratch=[pltpu.VMEM((width, 2 * hidden_count), LOW)],
    )


def shifted(rows, first, last):
    count = rows.shape[0]
    place = lax.broadcasted_iota(jnp.int32, rows.shape, 0)
    before = jnp.where(place == 0, first, pltpu.roll(rows, 1, 0))
    after = jnp.where(place == count - 1, last, pltpu.roll(rows, count - 1, 0))
    return before, after


def section_gradient(where, blocks, weight, taps, count):
    width = blocks[0].shape[1]
    fine = blocks[0].shape[0] - 16
    own = fine // 2
    channels = weight.shape[0] // 3
    share = channels // count
    windows = len(blocks)
    rows = windows * fine

    def kernel(where_ref, *refs):
        block_refs, weight_ref, taps_ref, refs = (
            refs[:windows], refs[windows], refs[windows + 1], refs[windows + 2 :]
        )
        deep_ref, mix_ref, coarse_ref, bias_ref, refs = *refs[:4], refs[4:]
        half_refs, whole_refs, (rows_ref, sems) = refs[:windows], refs[windows:-2], refs[-2:]
        copies = start_copies(
            [
                (block_refs[m].at[:fine, :], rows_ref.at[m * fine : (m + 1) * fine, :])
                for m in range(windows)
            ]
            + [
                (block_refs[m].at[fine:, :], rows_ref.at[pl.ds(rows + 16 * m, 16), :])
                for m in range(windows)
            ],
            sems,
        )
        for which, ref in enumerate(whole_refs):
            for t in range(count):
                spot = (3 * t + which) * share
                ref[t * share : (t + 1) * share, :] = weight_ref[spot : spot + share, :]
        row = lax.broadcasted_iota(jnp.int32, (own, fine), 0)
        column = lax.broadcasted_iota(jnp.int32, (own, fine), 1)
        pool = (column // 2 == row).astype(jnp.float32).astype(LOW)
        bias = jnp.zeros((1, channels), jnp.float32)
        wait_copies(copies)
        deep = dot_transposed(rows_ref[...], whole_refs[0][...]).astype(LOW)
        deep_ref[...] = deep[:rows]
        for m in range(windows):
            edge = deep[rows + 16 * m : rows + 16 * (m + 1)].astype(jnp.float32)
            own_rows = deep[m * fine : (m + 1) * fine].astype(jnp.float32)
            previous, following = shifted(
                own_rows,
                jnp.where(where_ref[1] > 0, edge[0:1], 0.0),
                jnp.where(where_ref[1] < count - 1, edge[1:2], 0.0),
            )
            mix = (
                taps_ref[0:1, :] * following
                + taps_ref[1:2, :] * own_rows
                + taps_ref[2:3, :] * previous
            ).astype(LOW)
            mix_ref[m * fine : (m + 1) * fine, :] = mix
            bias = bias + jnp.sum(mix.astype(jnp.float32), axis=0, keepdims=True)
            coarse_ref[m * own : (m + 1) * own, :] = dot_rows(pool, mix).astype(LOW)
        bias_ref[...] = bias
        part = dot_rows(coarse_ref[...], whole_refs[1][...]).astype(LOW)
        for m in range(windows):
            half_refs[place(m, windows)][...] = part[m * own : (m + 1) * own]

    return run_kernel(
        kernel,
        [weight, taps],
        [((rows, channels), LOW)] * 2
        + [((windows * own, channels), LOW)]
        + [((1, channels), jnp.float32)]
        + halves(windows, (own, width), LOW)
        + [((channels, width), LOW)] * 3,
        scalars=where,
        scratch=[
            pltpu.VMEM((rows + 16 * windows, width), LOW),
            pltpu.SemaphoreType.DMA((2 * windows,)),
        ],
        far=blocks,
    )


def section_grad_encoder(where, mix, lateral, windows):
    rows = mix.shape[0]
    fine = rows // windows
    width = lateral.shape[1]

    def kernel(where_ref, mix_ref, lateral_ref, out_ref):
        part = dot_rows(mix_ref[...], lateral_ref[...]).astype(LOW)
        for m in range(windows):
            spot = pl.ds(pl.multiple_of((where_ref[0] ^ m) * fine, fine), fine)
            out_ref[spot, :] = part[m * fine : (m + 1) * fine]

    return run_kernel(kernel, [mix, lateral], [((rows, width), LOW)], scalars=where)[0]


def section_forward(
    where, coarse_blocks, fine_blocks, up, lateral, point, bias, taps, grad_deep, count
):
    windows = len(fine_blocks)
    fine, (channels, width) = grad_deep.shape[0] // windows, up.shape
    own = fine // 2
    long, short = fine_blocks[0].shape[0], coarse_blocks[0].shape[0]

    def kernel(where_ref, *refs):
        coarse_refs, fine_refs, refs = refs[:windows], refs[windows : 2 * windows], refs[2 * windows :]
        up_ref, lateral_ref, point_ref, bias_ref, taps_ref, grad_ref = refs[:6]
        deep_ref, sums_ref, half_refs = refs[6], refs[7], refs[8:-3]
        short_ref, long_ref, sems = refs[-3:]
        copies = start_copies(
            [
                (coarse_refs[m], short_ref.at[m * short : (m + 1) * short, :])
                for m in range(windows)
            ]
            + [
                (fine_refs[m], long_ref.at[m * long : (m + 1) * long, :]) for m in range(windows)
            ],
            sems,
        )
        row = lax.broadcasted_iota(jnp.int32, (long, short), 0)
        column = lax.broadcasted_iota(jnp.int32, (long, short), 1)
        source = jnp.where(row < fine, row // 2, row - fine + own)
        repeat = (source == column).astype(jnp.float32).astype(LOW)
        wait_copies(copies[:windows])
        coarse = dot_transposed(short_ref[...], up_ref[...])
        high = coarse.astype(LOW)
        low = (coarse - high.astype(jnp.float32)).astype(LOW)
        wait_copies(copies[windows:])
        lateral_part = dot_transposed(long_ref[...], lateral_ref[...])
        sums = [jnp.zeros((1, channels), jnp.float32)] * 3
        for m in range(windows):
            spot = slice(m * short, (m + 1) * short)
            mix = (
                dot_rows(repeat, high[spot])
                + dot_rows(repeat, low[spot])
                + lateral_part[m * long : (m + 1) * long]
                + bias_ref[...]
            ).astype(LOW).astype(jnp.float32)
            rows = mix[:fine]
            previous, following = shifted(
                rows,
                jnp.where(where_ref[1] > 0, mix[fine : fine + 1], 0.0),
                jnp.where(where_ref[1] < count - 1, mix[fine + 1 : fine + 2], 0.0),
            )
            spot = slice(m * fine, (m + 1) * fine)
            deep_ref[spot, :] = (
                taps_ref[0:1, :] * previous + taps_ref[1:2, :] * rows + taps_ref[2:3, :] * following
            ).astype(LOW)
            grad = grad_ref[spot, :].astype(jnp.float32)
            sums = [
                total + jnp.sum(part * grad, axis=0, keepdims=True)
                for total, part in zip(sums, (previous, rows, following), strict=True)
            ]
        for s, total in enumerate(sums):
            sums_ref[s : s + 1, :] = total
        part = dot_rows(deep_ref[...], point_ref[...]).astype(LOW)
        for m in range(windows):
            half_refs[place(m, windows)][...] = part[m * fine : (m + 1) * fine]

    return run_kernel(
        kernel,
        [up, lateral, point, bias, taps, grad_deep],
        [((windows * fine, channels), LOW), ((3, channels), jnp.float32)]
        + halves(windows, (fine, width), LOW),
        scalars=where,
        scratch=[
            pltpu.VMEM((windows * short, width), LOW),
            pltpu.VMEM((windows * long, width), LOW),
            pltpu.SemaphoreType.DMA((2 * windows,)),
        ],
        far=list(coarse_blocks) + list(fine_blocks),
    )


def section_weights(deep, grad_coarse, grad_mix, cot_blocks, coarse_blocks, fine_blocks, sums, count):
    windows = len(cot_blocks)
    channels, width = deep.shape[1], cot_blocks[0].shape[1]
    fine, own = deep.shape[0] // windows, grad_coarse.shape[0] // windows
    share = channels // count

    def kernel(*refs):
        cot_refs, refs = refs[:windows], refs[windows:]
        row_refs, refs = refs[:windows], refs[windows:]
        fine_refs, refs = refs[:windows], refs[windows:]
        deep_ref, coarse_ref, mix_ref, sums_ref, out_ref = refs[:5]
        cot_all, row_all, fine_all, sems = refs[5:]
        groups = ((cot_refs, cot_all, fine), (row_refs, row_all, own), (fine_refs, fine_all, fine))
        copies = [
            start_copies(
                [
                    (blocks[m].at[:size, :], whole.at[m * size : (m + 1) * size, :])
                    for m in range(windows)
                ],
                sems,
                n * windows,
            )
            for n, (blocks, whole, size) in enumerate(groups)
        ]
        row = lax.broadcasted_iota(jnp.int32, (channels, 128), 0)
        column = lax.broadcasted_iota(jnp.int32, (channels, 128), 1)
        for t in range(count):
            chosen = ((row == column + t * share) & (column < share)).astype(jnp.float32)
            out_ref[t, 3 * share :, :128] = dot_rows(
                sums_ref[...].astype(LOW), chosen.astype(LOW)
            ).astype(LOW)
            out_ref[t, 3 * share :, 128:] = jnp.zeros((16, width - 128), LOW)
        lefts = (deep_ref, coarse_ref, mix_ref)
        for which, (left_ref, (_, whole, _)) in enumerate(zip(lefts, groups, strict=True)):
            wait_copies(copies[which])
            low = dot_leading(left_ref[...], whole[...]).astype(LOW)
            for t in range(count):
                out_ref[t, which * share : (which + 1) * share, :] = low[t * share : (t + 1) * share]

    return run_kernel(
        kernel,
        [deep, grad_coarse, grad_mix, sums],
        [((count, 3 * share + 16, width), LOW)],
        scratch=[
            pltpu.VMEM((windows * fine, width), LOW),
            pltpu.VMEM((windows * own, width), LOW),
            pltpu.VMEM((windows * fine, width), LOW),
            pltpu.SemaphoreType.DMA((3 * windows,)),
        ],
        far=list(cot_blocks) + list(coarse_blocks) + list(fine_blocks),
    )[0]


def from_ahead(rows, step):
    count = lax.axis_size("tensor")
    return lax.ppermute(rows, "tensor", [((i + step) % count, i) for i in range(count)])


def spread_blocks(rows):
    return [rows] + [from_ahead(rows, k) for k in range(1, lax.axis_size("tensor"))]


def collect_blocks(parts):
    count = lax.axis_size("tensor")
    return [from_ahead(parts[k - 1], count - k) for k in range(1, count)]


def to_own(rows):
    return jnp.roll(rows, -lax.axis_index("tensor") * (rows.shape[0] // lax.axis_size("tensor")), 0)


def dp_flip(cells, mask):
    count = lax.axis_size("dp")
    return lax.ppermute(cells, "dp", [(i, i ^ mask) for i in range(count)])


def half_rows(cells, axis=0):
    return cells.shape[axis] // 32 * 16


def both_cores(*chips):
    return [block for chip in chips for block in (chip, dp_flip(chip, 1))]


def chips_of(shard):
    return [shard] + [dp_flip(shard, mask) for mask in (2, 4, 6)]


def send_sum(cells, mask, dtype):
    return dp_flip(cells.astype(dtype), mask)


def core_pairs(blocks):
    chips = len(blocks) // 2
    return [
        mine.astype(jnp.float32) + dp_flip(theirs, 1).astype(jnp.float32)
        for mine, theirs in zip(blocks[:chips], blocks[chips:], strict=True)
    ]


def corner_sums(pairs, dtype):
    half = half_rows(pairs[3])
    return send_sum(pairs[3][:half], 2, dtype), send_sum(pairs[3][half:], 4, dtype)


def chip_sums(pairs, corners, dtype):
    half = half_rows(pairs[3])
    corners = [corner.astype(jnp.float32) for corner in corners]
    near = jnp.concatenate([pairs[1][:half], pairs[1][half:] + corners[1]], axis=0)
    far = jnp.concatenate([pairs[2][:half] + corners[0], pairs[2][half:]], axis=0)
    near, far = send_sum(near, 2, dtype), send_sum(far, 4, dtype)
    return pairs[0] + near.astype(jnp.float32) + far.astype(jnp.float32)


def direct_sums(pairs, dtype):
    return pairs[0] + sum(
        send_sum(pairs[chip], 2 * chip, dtype).astype(jnp.float32) for chip in (1, 2, 3)
    )


def gather_dp(shard):
    return lax.all_gather(shard, "dp", axis=0, tiled=True)


def scatter_dp(whole):
    return lax.psum_scatter(whole, "dp", scatter_dimension=0, tiled=True)


def scatter_tensor(whole):
    return lax.psum_scatter(whole, "tensor", scatter_dimension=0, tiled=True)


def gather_small(cells):
    line = jnp.stack(spread_blocks(cells), axis=0)
    return lax.all_gather(jnp.roll(line, lax.axis_index("tensor"), 0), "dp", axis=0)


def join(*arrays):
    return lax.optimization_barrier(arrays)


def edges(head, tail):
    ends = lax.axis_size("tensor") - 1
    return (
        lax.ppermute(tail, "tensor", [(i, i + 1) for i in range(ends)]),
        lax.ppermute(head, "tensor", [(i + 1, i) for i in range(ends)]),
    )


def halo(cells):
    count = lax.axis_size("tensor")
    ends = count - 1
    before = lax.ppermute(cells[:, -1:], "tensor", [(i, i + 1) for i in range(ends)])
    after = lax.ppermute(cells[:, :1], "tensor", [(i + 1, i) for i in range(ends)])
    return jnp.concatenate([before, cells, after], axis=1)


def body_plain(
    activations,
    encoder,
    species,
    cotangent,
    norm_gain,
    norm_shift,
    species_table,
    query_weight,
    key_weight,
    value_weight,
    output_weight,
    expand_weight,
    contract_weight,
    position_weight,
    content_bias,
    position_bias,
    upsample_weight,
    lateral_weight,
    depthwise_weight,
    section_bias,
    pointwise_weight,
):
    windows = lax.axis_size("dp")
    count = lax.axis_size("tensor")
    own = activations.shape[1]
    length = own * count
    width = activations.shape[2]
    local_heads = query_weight.shape[1] // KEYD
    keys = local_heads * KEYD
    values = local_heads * VALD

    raw = spread_blocks(activations[0])
    attn_shard = jnp.concatenate([query_weight, key_weight, value_weight, output_weight.T], axis=1)
    attn_blocks = [gather_dp(attn_shard)]
    where = jnp.stack([lax.axis_index("dp"), lax.axis_index("tensor"), species[0]])

    small = jnp.concatenate(
        [norm_gain, norm_shift, species_table, depthwise_weight, section_bias[None]], axis=0
    )
    n_small = small.size
    n_position = position_weight.size
    n_bias = content_bias.size
    packed = gather_small(
        jnp.concatenate(
            [
                small.reshape(-1),
                position_weight.reshape(-1),
                content_bias.reshape(-1),
                position_bias.reshape(-1),
            ]
        )
    )
    small_all = packed[:, :, :n_small].reshape(windows, count, 10, -1)
    norm_all = jnp.transpose(small_all[:, :, :6], (2, 0, 1, 3)).reshape(6, width)
    norm_all = norm_all.astype(jnp.float32)
    gain_vals, shift_vals, table_rows = norm_all[:2], norm_all[2:4], norm_all[4:]
    small_group = lax.dynamic_index_in_dim(small_all, lax.axis_index("dp"), 0, False)
    small_group = jnp.swapaxes(small_group, 0, 1).reshape(10, -1).astype(jnp.float32)
    channels = small_group.shape[1]
    depth_taps = small_group[6:9]
    bias_section = small_group[9]
    heads_all = lax.dynamic_index_in_dim(packed, lax.axis_index("tensor"), 1, False)[:, n_small:]
    w_position = heads_all[:, :n_position].reshape(KEYD, BASIS, local_heads)
    bias_content = heads_all[:, n_position : n_position + n_bias].reshape(KEYD, local_heads)
    bias_position = heads_all[:, n_position + n_bias :].reshape(KEYD, local_heads)

    section_shard = jnp.concatenate([pointwise_weight, upsample_weight.T, lateral_weight.T], axis=0)
    w_section = lax.all_gather(section_shard, "tensor", axis=0).reshape(count, 3, -1, width)
    w_point = w_section[:, 0].reshape(channels, width)
    w_up = w_section[:, 1].reshape(channels, width)
    w_lat = w_section[:, 2].reshape(channels, width)
    cot_all = gather_dp(cotangent[0])
    ffn_shard = jnp.concatenate([expand_weight, contract_weight.T], axis=1)
    w_ffn = lax.all_gather(ffn_shard, "dp", axis=0, tiled=True)
    hidden_count = expand_weight.shape[1]
    enc_all = gather_dp(encoder[0])

    fine = 2 * own
    grad_deep = dot_transposed(cot_all, w_point).astype(LOW)
    grad_wide = halo(grad_deep.reshape(windows, fine, channels)).astype(jnp.float32)
    grad_mix = (
        depth_taps[0] * grad_wide[:, 2:]
        + depth_taps[1] * grad_wide[:, 1:-1]
        + depth_taps[2] * grad_wide[:, :-2]
    ).astype(LOW)
    grad_coarse = jnp.sum(
        grad_mix.astype(jnp.float32).reshape(windows * own, 2, channels), axis=1
    ).astype(LOW)
    grad_resid_two = scatter_dp(dot_plain(grad_coarse, w_up).astype(LOW)).astype(jnp.float32)
    grad_ffn = spread_blocks(grad_resid_two.astype(LOW))

    species_mask = (jnp.arange(SPECIES, dtype=jnp.int32) == species[0]).astype(jnp.float32)
    species_row = jnp.sum(species_mask[:, None] * table_rows, axis=0)
    content_flat = bias_content.astype(jnp.float32).T.reshape(1, -1)
    position_flat = bias_position.astype(jnp.float32).T.reshape(1, -1)
    basis_turned = jnp.pad(basis_table(length, BASIS).astype(LOW)[::-1], ((0, 1), (0, 0)))
    rel_weight = jnp.transpose(w_position, (1, 2, 0)).reshape(BASIS, -1)
    rel_turned = dot_plain(basis_turned, rel_weight).astype(LOW)
    attn_parts, saved = attention_forward(
        where,
        raw,
        [species_row[None], gain_vals[:1], shift_vals[:1], content_flat, position_flat],
        rel_turned,
        attn_blocks,
        local_heads,
        own,
    )
    resid_one, unit_two, scale_two, normed_two = second_norm(
        attn_parts[0],
        collect_blocks(attn_parts[1:]),
        [raw[0], species_row[None]],
        gain_vals[1:],
        shift_vals[1:],
    )

    contract_part, normed_two_all, hidden_low, slope = feed_forward_up(
        where, spread_blocks(normed_two), w_ffn
    )
    ffn_parts, (grad_ffn_all, grad_hidden_pre) = feed_forward_back(grad_ffn, slope, w_ffn)
    grad_resid_one, grad_attn, sums_two = second_norm_back(
        ffn_parts[0],
        collect_blocks(ffn_parts[1:]),
        unit_two,
        scale_two,
        gain_vals[1:],
        grad_resid_two,
    )

    resid_two = resid_one + scatter_tensor(contract_part).astype(jnp.float32)
    section_all = gather_dp(resid_two.astype(LOW))
    coarse = dot_transposed(section_all, w_up).reshape(windows, own, channels)
    section_mix = (
        jnp.repeat(coarse, 2, axis=1)
        + dot_transposed(enc_all, w_lat).reshape(windows, fine, channels)
        + bias_section
    ).astype(LOW)
    mix_wide = halo(section_mix).astype(jnp.float32)
    deep_rows = (
        depth_taps[0] * mix_wide[:, :-2]
        + depth_taps[1] * mix_wide[:, 1:-1]
        + depth_taps[2] * mix_wide[:, 2:]
    ).astype(LOW)
    deep_rows = deep_rows.reshape(windows * fine, channels)
    section_out = scatter_dp(dot_plain(deep_rows, w_point).astype(LOW)).astype(LOW)
    grad_mix_rows = grad_mix.reshape(windows * fine, channels)
    encoder_grad = scatter_dp(dot_plain(grad_mix_rows, w_lat).astype(LOW)).astype(jnp.float32)
    grad_centre = grad_wide[:, 1:-1]
    grad_section_small = jnp.stack(
        [jnp.sum(mix_wide[:, s : s + fine] * grad_centre, axis=(0, 1)) for s in range(3)]
        + [jnp.sum(grad_mix.astype(jnp.float32), axis=(0, 1))],
        axis=1,
    )
    section_cols = jnp.stack(
        [
            dot_leading(deep_rows, cot_all).astype(LOW).reshape(count, -1, width),
            dot_leading(grad_coarse, section_all).astype(LOW).reshape(count, -1, width),
            dot_leading(grad_mix_rows, enc_all).astype(LOW).reshape(count, -1, width),
        ],
        axis=1,
    )
    section_cols = scatter_tensor(section_cols)[0].astype(jnp.float32)

    ffn_out = scatter_dp(
        feed_forward_weights(
            where, normed_two_all, grad_ffn_all, hidden_low, grad_hidden_pre, 1
        )[0]
    ).astype(jnp.float32)

    head_parts, (grad_attn_all, grad_heads, bias_sums, rel_grad, own_sums) = attention_backward(
        where,
        spread_blocks(grad_attn),
        saved,
        rel_turned,
        basis_turned,
        gain_vals[:1],
        sums_two,
        local_heads,
        own,
    )
    head_received = collect_blocks(head_parts[1:])
    grad_resid_in = first_norm_back(
        where, head_parts[0], head_received, saved[2], saved[3], gain_vals[:1], grad_resid_one
    )
    weights = attention_weights(
        where, saved, grad_attn_all, grad_heads, own_sums, head_received, bias_sums, rel_grad, 1
    )[0]
    attn_out = scatter_dp(weights).astype(jnp.float32)
    norm_sums = own_sums[:6]
    for block in head_received:
        norm_sums = norm_sums + block[own : own + 6].astype(jnp.float32)
    norm_cols = jnp.swapaxes(norm_sums.reshape(6, windows, channels), 0, 1)
    head_cols = jnp.concatenate([bias_sums, rel_grad], axis=0)
    head_cols = jnp.transpose(head_cols.reshape(2 + BASIS, local_heads, KEYD), (2, 0, 1))
    heads_cols = jnp.concatenate(
        [
            head_cols[:, 2:].reshape(windows, -1),
            head_cols[:, 0].reshape(windows, -1),
            head_cols[:, 1].reshape(windows, -1),
        ],
        axis=1,
    )
    small_out = scatter_dp(jnp.concatenate([norm_cols.reshape(windows, -1), heads_cols], axis=1))
    small_out = small_out[0]
    n_norm = 6 * channels
    section_sums = grad_section_small.T
    for k in range(1, count):
        section_sums = section_sums + from_ahead(grad_section_small.T, k)
    norm_out = jnp.concatenate([small_out[:n_norm].reshape(6, channels), section_sums])
    share = channels // count
    norm_out = lax.dynamic_slice_in_dim(norm_out, lax.axis_index("tensor") * share, share, 1)
    heads_out = small_out[n_norm:]
    return (
        section_out[None],
        grad_resid_in,
        encoder_grad[None],
        norm_out[0:2],
        norm_out[2:4],
        norm_out[4:6],
        attn_out[:, :keys],
        attn_out[:, keys : 2 * keys],
        attn_out[:, 2 * keys : 2 * keys + values],
        attn_out[:, 2 * keys + values :].T,
        ffn_out[:, :hidden_count],
        ffn_out[:, hidden_count:].T,
        heads_out[:n_position].reshape(position_weight.shape),
        heads_out[n_position : n_position + n_bias].reshape(content_bias.shape),
        heads_out[n_position + n_bias :].reshape(position_bias.shape),
        section_cols[1].T,
        section_cols[2].T,
        norm_out[6:9],
        norm_out[9],
        section_cols[0],
    )


def body_direct(
    activations,
    encoder,
    species,
    cotangent,
    norm_gain,
    norm_shift,
    species_table,
    query_weight,
    key_weight,
    value_weight,
    output_weight,
    expand_weight,
    contract_weight,
    position_weight,
    content_bias,
    position_bias,
    upsample_weight,
    lateral_weight,
    depthwise_weight,
    section_bias,
    pointwise_weight,
):
    count = lax.axis_size("tensor")
    own, width = activations.shape[1:]
    length = own * count
    local_heads = query_weight.shape[1] // KEYD
    keys = local_heads * KEYD
    values = local_heads * VALD
    hidden_count = expand_weight.shape[1]
    share = section_bias.shape[0]
    where = jnp.stack([lax.axis_index("dp"), lax.axis_index("tensor"), species[0]])

    small = [norm_gain, norm_shift, species_table, depthwise_weight, section_bias[None]]
    entries = sum(block.size for block in small + [position_weight, content_bias, position_bias])
    raw = spread_blocks(
        pack_rows(
            activations[0],
            small,
            jnp.swapaxes(position_weight, 1, 2),
            [content_bias.T, position_bias.T],
            cotangent[0],
            encoder[0],
        )
    )
    attn_shard = jnp.concatenate([query_weight, key_weight, value_weight, output_weight.T], axis=1)
    attn_rows = attn_shard.shape[0]
    attn_chips = chips_of(attn_shard)
    raw, attn_chips, cot, section_shard = join(
        raw, attn_chips, cotangent[0], [pointwise_weight, upsample_weight.T, lateral_weight.T]
    )
    section_shard = jnp.concatenate(section_shard, axis=0)
    w_section = lax.all_gather(section_shard, "tensor", axis=0, tiled=True)
    line, cot_ends, enc_ends = pick_rows(raw, own, entries)
    cot = jnp.concatenate([cot, cot_ends], axis=0)
    blank = jnp.zeros((14, width), LOW)
    small_rows = gather_dp(line)
    attn_blocks = both_cores(*attn_chips)
    small_rows, attn_blocks, cot = join(small_rows, attn_blocks, cot)
    cot_chips = chips_of(cot)
    basis_turned = jnp.pad(basis_table(length, BASIS).astype(LOW)[::-1], ((0, 1), (0, 0)))
    rows, (depth_taps, bias_section, rel_turned, content_flat, position_flat) = unpack_small(
        where, small_rows, basis_turned, width, local_heads, count
    )
    gain_one, gain_two, shift_one, shift_two, species_row = rows
    attn_parts, saved = attention_forward(
        where,
        raw,
        [species_row, gain_one, shift_one, content_flat, position_flat],
        rel_turned,
        attn_blocks,
        local_heads,
        own,
    )
    attn_parts, cot_chips, ffn_shard, enc = join(
        attn_parts, cot_chips, [expand_weight, contract_weight.T], encoder[0]
    )
    w_ffn = gather_dp(jnp.concatenate(ffn_shard, axis=1))
    enc = jnp.concatenate([enc, enc_ends], axis=0)

    attn_received = collect_blocks(attn_parts[1:])
    cot_blocks = both_cores(*cot_chips)
    grad_deep, grad_mix, grad_coarse, bias_grad, *halves_two, w_point, w_up, w_lateral = (
        section_gradient(where, cot_blocks, w_section, depth_taps, count)
    )
    attn_received, halves_two = join(attn_received, halves_two)

    resid_one, unit_two, scale_two, normed_two = second_norm(
        attn_parts[0], attn_received, [activations[0], species_row], gain_two, shift_two
    )
    normed_two, halves_two = join(normed_two, halves_two)
    normed_blocks = spread_blocks(normed_two)
    grad_resid_two = direct_sums(core_pairs(halves_two), LOW)
    normed_blocks, grad_resid_two, enc = join(normed_blocks, grad_resid_two, enc)

    grad_ffn = spread_blocks(grad_resid_two.astype(LOW))
    contract_part, normed_two_all, hidden_low, slope = feed_forward_up(where, normed_blocks, w_ffn)
    enc_chips = chips_of(enc)
    grad_ffn, contract_part, enc_chips, late_mix = join(
        grad_ffn, contract_part, enc_chips, grad_mix
    )

    contract_sum = scatter_tensor(contract_part)
    enc_blocks = both_cores(*enc_chips)
    ffn_parts, (grad_ffn_all, grad_hidden_pre) = feed_forward_back(grad_ffn, slope, w_ffn)
    ffn_received = collect_blocks(ffn_parts[1:])
    ffn_received, grad_hidden_pre, enc_blocks = join(ffn_received, grad_hidden_pre, enc_blocks)

    grad_resid_one, grad_attn, sums_two = second_norm_back(
        ffn_parts[0], ffn_received, unit_two, scale_two, gain_two, grad_resid_two
    )
    coarse = (resid_one + contract_sum.astype(jnp.float32)).astype(LOW)
    grad_attn = [grad_attn, coarse[:1], coarse[-1:], jnp.zeros((6, width), LOW)]
    grad_attn, grad_hidden_pre, late_mix = join(
        jnp.concatenate(grad_attn, axis=0), grad_hidden_pre, late_mix
    )
    grad_attn_blocks = spread_blocks(grad_attn)
    encoder_part = section_grad_encoder(where, late_mix, w_lateral, lax.axis_size("dp"))
    ffn_halves = feed_forward_weights(
        where, normed_two_all, grad_ffn_all, hidden_low, grad_hidden_pre, lax.axis_size("dp")
    )
    grad_attn_blocks, ffn_halves, encoder_part = join(grad_attn_blocks, ffn_halves, encoder_part)
    encoder_grad = scatter_dp(encoder_part).astype(jnp.float32)

    coarse = [coarse, grad_attn_blocks[-1][own + 1 : own + 2], grad_attn_blocks[1][own : own + 1]]
    coarse_chips = chips_of(jnp.concatenate(coarse + [blank], axis=0))
    ffn_pairs = core_pairs(ffn_halves)
    head_parts, (grad_attn_all, grad_heads, bias_sums, rel_grad, own_sums) = attention_backward(
        where,
        grad_attn_blocks,
        saved,
        rel_turned,
        basis_turned,
        gain_one,
        sums_two,
        local_heads,
        own,
    )
    head_parts, coarse_chips, ffn_pairs = join(head_parts, coarse_chips, ffn_pairs)
    head_received = collect_blocks(head_parts[1:])
    ffn_out = direct_sums(ffn_pairs, LOW)
    coarse_blocks = both_cores(*coarse_chips)
    deep_rows, taps_grad, *out_halves = section_forward(
        where,
        coarse_blocks,
        enc_blocks,
        w_up,
        w_lateral,
        w_point,
        bias_section,
        depth_taps,
        grad_deep,
        count,
    )
    section_sums = jnp.pad(jnp.concatenate([taps_grad, bias_grad], axis=0), ((0, 12), (0, 0)))
    cols_part = section_weights(
        deep_rows,
        grad_coarse,
        grad_mix,
        cot_blocks,
        coarse_blocks,
        enc_blocks,
        section_sums,
        count,
    )
    section_cols = scatter_tensor(cols_part)[0].astype(jnp.float32)
    out_pairs = core_pairs(out_halves)
    head_received, out_pairs, ffn_out = join(head_received, out_pairs, ffn_out)

    grad_resid_in = first_norm_back(
        where, head_parts[0], head_received, saved[2], saved[3], gain_one, grad_resid_one
    )
    attn_halves = attention_weights(
        where,
        saved,
        grad_attn_all,
        grad_heads,
        own_sums,
        head_received,
        bias_sums,
        rel_grad,
        len(attn_blocks),
    )
    attn_pairs = core_pairs(attn_halves)
    section_out = direct_sums(out_pairs, LOW).astype(LOW)
    attn_pairs, section_out, grad_resid_in, encoder_grad = join(
        attn_pairs, section_out, grad_resid_in, encoder_grad
    )
    attn_out = direct_sums(attn_pairs, LOW)

    small_out, attn_out = attn_out[attn_rows:], attn_out[:attn_rows]
    norm_out = lax.dynamic_slice_in_dim(
        small_out[: 4 + SPECIES], lax.axis_index("tensor") * share, share, 1
    )
    part = KEYD // lax.axis_size("dp")

    def heads_of(rows):
        return rows.reshape(rows.shape[0], local_heads, KEYD)[:, :, :part]

    bias_out = jnp.transpose(heads_of(small_out[8:10, :keys]), (2, 0, 1))
    rel_out = [small_out[:, 256 : 256 + keys], small_out[:, 256 + keys : 256 + 2 * keys]]
    rel_out = jnp.transpose(heads_of(jnp.concatenate(rel_out, axis=0)), (2, 0, 1))
    return (
        section_out[None],
        grad_resid_in,
        encoder_grad[None],
        norm_out[0:2],
        norm_out[2:4],
        norm_out[4:],
        attn_out[:, :keys],
        attn_out[:, keys : 2 * keys],
        attn_out[:, 2 * keys : 2 * keys + values],
        attn_out[:, 2 * keys + values :].T,
        ffn_out[:, :hidden_count],
        ffn_out[:, hidden_count:].T,
        rel_out,
        bias_out[:, 0],
        bias_out[:, 1],
        section_cols[share : 2 * share].T,
        section_cols[2 * share : 3 * share].T,
        section_cols[3 * share : 3 * share + 3, :share],
        section_cols[3 * share + 3, :share],
        section_cols[:share],
    )


def solution(mesh):
    rows = P("dp", "tensor", None)
    narrow = P(None, ("dp", "tensor"))
    split = P("dp", "tensor")
    turned = P("tensor", "dp")
    vector = P(("dp", "tensor"))
    tall = P(("dp", "tensor"), None)
    position = P("dp", None, "tensor")
    weights = (split, split, split, turned, split, turned, position, split, split)
    return jax.shard_map(
        body_direct if mesh.shape["dp"] == 8 else body_plain,
        mesh=mesh,
        in_specs=(rows, rows, P("dp"), rows, narrow, narrow, narrow)
        + weights
        + (narrow, narrow, narrow, vector, tall),
        out_specs=(rows, rows, rows, narrow, narrow, narrow)
        + weights
        + (narrow, narrow, narrow, vector, tall),
        check_vma=False,
    )
```
